32 devices in a mesh: dp: 8 (over z, x), chan: 4 (over y, core).
Axes of the slice: x: 2, y: 2, z: 4, core: 2. Of those that a mesh axis runs over, the one named last changes fastest.
Arguments:
- images: bfloat16 [640, 9, 9, 512], P('dp'), may hold values from -6 to 6
- groups: int32 [640], P('dp'), may hold values from 0 to 2
- cotangent: bfloat16 [640, 9, 9, 512], P('dp', None, None, 'chan'), may hold values from -6 to 6
- weight_one: float32 [9, 512, 512], P(None, None, 'chan'), may hold values from -0.09375 to 0.09375
- gain_one: float32 [512], P('chan'), may hold values from 0.5 to 1.5
- shift_one: float32 [512], P('chan'), may hold values from -3 to 3
- weight_two: float32 [9, 512, 512], P(None, None, 'chan'), may hold values from -0.09375 to 0.09375
- gain_two: float32 [512], P('chan'), may hold values from 0.5 to 1.5
- shift_two: float32 [512], P('chan'), may hold values from -3 to 3
- moment_one: float32 [9, 512, 512], P(None, None, 'chan'), may hold values from -0.0006 to 0.0006
- moment_two: float32 [9, 512, 512], P(None, None, 'chan'), may hold values from -0.0006 to 0.0006
Outputs:
- block_output: bfloat16 [640, 9, 9, 512], P('dp', None, None, 'chan')
- input_grad: float32 [640, 9, 9, 512], P('dp', None, None, 'chan')
- weight_one_grad: float32 [9, 512, 512], P(None, None, 'chan')
- gain_one_grad: float32 [512], P('chan')
- shift_one_grad: float32 [512], P('chan')
- weight_two_grad: float32 [9, 512, 512], P(None, None, 'chan')
- gain_two_grad: float32 [512], P('chan')
- shift_two_grad: float32 [512], P('chan')
- moment_one_new: float32 [9, 512, 512], P(None, None, 'chan')
- moment_two_new: float32 [9, 512, 512], P(None, None, 'chan')
- weight_norms: float32 [2], replicated
- grad_norms: float32 [2], replicated
The draws below stay inside these ranges and needn't reach their ends.
All inputs are finite; a program needn't handle non-finite values.
Results may differ from the reference program's by a relative error of at most 0.015.
Values may be sent and summed in bfloat16 or wider, within the bound.
No kernel may reach another device: no remote copies, remote signals or barrier semaphores. Data moves between devices by JAX's collectives and lax.ppermute only.
A program may use at most 256 MiB of HBM per device.

```python
import jax
import jax.numpy as jnp
from jax import lax

C = 512
SIDE = 9
IMAGES = 640


def place_ends(values, own_key, least, top_value):
    dims = values.shape
    spot = [jax.random.randint(jax.random.fold_in(own_key, axis), (), 0, dims[axis]) for axis in range(len(dims))]
    values = values.at[tuple(spot)].set(least)
    longest = dims.index(max(dims))
    spot[longest] = (spot[longest] + 1) % dims[longest]
    return values.at[tuple(spot)].set(top_value)


def level_of(rng, dims, pieces, least, largest):
    loudness, own = 1.0, jax.random.fold_in(rng, 6)
    for axis_at, shards_of in pieces:
        heights = jnp.exp(jax.random.uniform(jax.random.fold_in(own, axis_at), (shards_of,), jnp.float32, least / len(pieces), largest / len(pieces)))
        loudness = loudness * jnp.repeat(heights, dims[axis_at] // shards_of).reshape([-1 if axis == axis_at else 1 for axis in range(len(dims))])
    return loudness


def centred(own_key, shape, scale, reach, cuts=(), kind=jnp.bfloat16):
    values = scale * jax.random.normal(own_key, shape, jnp.float32)
    if cuts:
        values = values * level_of(own_key, shape, cuts, -0.22, 0.18)
    return jnp.clip(values, -reach, reach).astype(kind)


def setup_inputs(seed: int = 0) -> dict:
    keys = jax.random.split(jax.random.key(seed), 12)
    return {
        "images": centred(keys[0], (IMAGES, SIDE, SIDE, C), 1.0, 6.0, ((0, 8),)),
        "groups": place_ends(jax.random.randint(keys[1], (IMAGES,), 0, 3), jax.random.fold_in(keys[1], 1), 0, 2).astype(jnp.int32),
        "cotangent": centred(keys[2], (IMAGES, SIDE, SIDE, C), 1.0, 6.0, ((0, 8), (3, 4))),
        "weight_one": centred(keys[3], (9, C, C), (9 * C) ** -0.5, 0.09375, ((2, 4),), jnp.float32),
        "gain_one": jnp.clip(1.0 + 0.1 * jax.random.normal(keys[4], (C,), jnp.float32), 0.5, 1.5),
        "shift_one": centred(keys[5], (C,), 0.5, 3.0, ((0, 4),), jnp.float32),
        "weight_two": centred(keys[6], (9, C, C), (9 * C) ** -0.5, 0.09375, ((2, 4),), jnp.float32),
        "gain_two": jnp.clip(1.0 + 0.1 * jax.random.normal(keys[7], (C,), jnp.float32), 0.5, 1.5),
        "shift_two": centred(keys[8], (C,), 0.5, 3.0, ((0, 4),), jnp.float32),
        "moment_one": centred(keys[9], (9, C, C), (1e-4), 0.0006, ((2, 4),), jnp.float32),
        "moment_two": centred(keys[10], (9, C, C), (1e-4), 0.0006, ((2, 4),), jnp.float32),
    }


@jax.custom_vjp
def low(v):
    return lax.optimization_barrier(v.astype(jnp.bfloat16)).astype(jnp.float32)

@jax.custom_vjp
def low_back(v):
    return v

def low_keep(v):
    return (low(v), None)

def low_pass(kept, grad):
    return (grad,)

def back_keep(v):
    return (v, None)

def back_low(kept, grad):
    return (low(grad),)
low.defvjp(low_keep, low_pass)
low_back.defvjp(back_keep, back_low)
EPSILON = 1e-05
MOMENTUM = 0.9
LEARN_RATE = 8.0
TRUST_COEF = 0.001
DECAY = 5e-05

def valid_pixels(groups, side):
    extent = 5 + 2 * groups
    places = jnp.arange(side, dtype=jnp.int32)
    inside = (places[None, :, None] < extent[:, None, None]) & (places[None, None, :] < extent[:, None, None])
    return inside.astype(jnp.float32)[..., None]

def convolve(source, kernel):
    side = source.shape[1]
    padded = jnp.pad(source, ((0, 0), (1, 1), (1, 1), (0, 0)))
    total = jnp.zeros(source.shape[:3] + (kernel.shape[2],), jnp.float32)
    for i in range(3):
        for j in range(3):
            total = total + jnp.einsum('bhwc,cd->bhwd', padded[:, i:i + side, j:j + side, :], kernel[3 * i + j], precision=lax.Precision.HIGHEST)
    return total

def batch_norm(hidden, gain, shift, valid_mask):
    pixel_count = jnp.sum(valid_mask)
    center = lax.optimization_barrier(jnp.sum(hidden * valid_mask, axis=(0, 1, 2))) / pixel_count
    centered = hidden - center
    spread = lax.optimization_barrier(jnp.sum(valid_mask * centered * centered, axis=(0, 1, 2))) / pixel_count
    return centered * lax.rsqrt(spread + EPSILON) * gain + shift

def lars_step(weight, grad, moment):
    weight_norm = jnp.sqrt(jnp.sum(weight * weight))
    grad_norm = jnp.sqrt(jnp.sum(grad * grad))
    trust = TRUST_COEF * weight_norm / (grad_norm + DECAY * weight_norm)
    moment_new = MOMENTUM * moment + LEARN_RATE * trust * (grad + DECAY * weight)
    return (moment_new, weight_norm, grad_norm)

def reference(images, groups, cotangent, weight_one, gain_one, shift_one, weight_two, gain_two, shift_two, moment_one, moment_two):
    valid_mask = valid_pixels(groups, images.shape[1])

    def forward(source, kernel_one, gain_a, shift_a, kernel_two, gain_b, shift_b):
        masked_in = source * valid_mask
        hidden_one = low_back(convolve(masked_in, low(kernel_one)))
        active = low(jax.nn.gelu(batch_norm(hidden_one, gain_a, shift_a, valid_mask)) * valid_mask)
        hidden_two = low_back(convolve(active, low(kernel_two)))
        return jax.nn.gelu(batch_norm(hidden_two, gain_b, shift_b, valid_mask) + masked_in) * valid_mask
    result, pullback = jax.vjp(forward, images.astype(jnp.float32), weight_one, gain_one, shift_one, weight_two, gain_two, shift_two)
    grads = pullback(cotangent.astype(jnp.float32))
    moment_one_new, wnorm_one, gnorm_one = lars_step(weight_one, grads[1], moment_one)
    moment_two_new, wnorm_two, gnorm_two = lars_step(weight_two, grads[4], moment_two)
    return (result.astype(jnp.bfloat16), grads[0], grads[1], grads[2], grads[3], grads[4], grads[5], grads[6], moment_one_new, moment_two_new, jnp.stack([wnorm_one, wnorm_two]), jnp.stack([gnorm_one, gnorm_two]))
```

```python
import functools

import jax
import jax.numpy as jnp
from jax import lax
from jax.experimental import pallas as pl
from jax.experimental.pallas import tpu as pltpu
from jax.sharding import PartitionSpec as P

EPSILON = 1e-05
MOMENTUM = 0.9
LEARN_RATE = 8.0
TRUST_COEF = 0.001
DECAY = 5e-05
GELU_A = 0.7978845608028654
GELU_B = 0.7978845608028654 * 0.044715
F32 = jnp.float32
BF16 = jnp.bfloat16
LANES = 128
PAIRS = ((0, 2), (2, 4), (4, 6), (6, 8), (8, 9))
VMEM_BYTES = 56 * 1024 * 1024


def chunk_starts(side, sizes):
    starts, at = [], 0
    for size in sizes:
        starts.append(at)
        at += size
    assert at == side
    return starts


def segments(*splits):
    ends = sorted({sum(s[: k + 1]) for s in splits for k in range(len(s))})
    result, start = [], 0
    for end in ends:
        where = []
        for s in splits:
            at = 0
            for index, size in enumerate(s):
                if at <= start < at + size:
                    where.append((index, at))
                at += size
        result.append((start, end, where))
        start = end
    return result


def pixel_mask(ext, r, c):
    return jnp.where(ext > jnp.maximum(r, c), 1.0, 0.0).astype(F32)


def gelu(v):
    t = jnp.tanh(v * (GELU_A + GELU_B * (v * v)))
    half = 0.5 * v
    return half + half * t


def gelu_both(v):
    sq = v * v
    t = jnp.tanh(v * (GELU_A + GELU_B * sq))
    half = 0.5 * v
    value = half + half * t
    slope = 0.5 + 0.5 * t + (half - half * (t * t)) * (GELU_A + (3.0 * GELU_B) * sq)
    return value, slope


def call(body, outs, ins, scratch=(), flops=0, bytes_=0, aliases=None, any_in=(), any_out=(), smem_in=()):
    vm = pl.BlockSpec(memory_space=pltpu.VMEM)
    anys = pl.BlockSpec(memory_space=pl.ANY)
    sm = pl.BlockSpec(memory_space=pltpu.SMEM)
    in_specs = [anys if k in any_in else sm if k in smem_in else vm for k in range(len(ins))]
    out_specs = [anys if k in any_out else vm for k in range(len(outs))]
    return pl.pallas_call(
        body,
        out_shape=[jax.ShapeDtypeStruct(s, d) for s, d in outs],
        in_specs=in_specs,
        out_specs=out_specs,
        scratch_shapes=list(scratch),
        input_output_aliases=aliases or {},
        compiler_params=pltpu.CompilerParams(vmem_limit_bytes=VMEM_BYTES),
        cost_estimate=pl.CostEstimate(flops=int(flops), bytes_accessed=int(bytes_), transcendentals=0),
    )(*ins)


def prep_body(xor_rows, chan_ref, w_ref, wb_ref, wt_ref, sq_ref):
    chan = chan_ref[0]
    blocks = wt_ref.shape[0]
    total = jnp.zeros((8, LANES), F32)
    for k in range(blocks):
        other = jnp.bitwise_xor(chan, k)
        rows = pl.ds(pl.multiple_of(other * LANES, LANES), LANES)
        for t in range(9):
            piece = w_ref[t, rows, :]
            total = total + jnp.sum((piece * piece).reshape(LANES // 8, 8, LANES), axis=0)
            low = piece.astype(BF16)
            if xor_rows:
                wb_ref[k * LANES : (k + 1) * LANES, t * LANES : (t + 1) * LANES] = low
            else:
                wb_ref[rows, t * LANES : (t + 1) * LANES] = low
            wt_ref[k, :, (8 - t) * LANES : (9 - t) * LANES] = piece.T.astype(BF16)
    sq_ref[...] = total


def prep(weight, chan, xor_rows):
    width = weight.shape[1]
    blocks = width // LANES
    return call(
        functools.partial(prep_body, xor_rows),
        [((width, 9 * LANES), BF16), ((blocks, LANES, 9 * LANES), BF16), ((8, LANES), F32)],
        [chan, weight],
        smem_in=(0,),
        bytes_=weight.size * 8,
    )


def add_row(lhs, w_ref, acc, slot, batch):
    rows = lhs.shape[0]
    for a, b in PAIRS:
        y = jnp.dot(lhs, w_ref[:, a * LANES : b * LANES], preferred_element_type=F32)
        for t in range(a, b):
            i, j = divmod(t, 3)
            z = y[:, (t - a) * LANES : (t - a + 1) * LANES]
            at = slot + 2 - i
            if j == 0:
                acc[at, batch:] += z[: rows - batch]
            elif j == 1:
                acc[at] += z
            else:
                acc[at, : rows - batch] += z[batch:]


def start_acc(acc, carry_ref):
    for slot in range(acc.shape[0]):
        if carry_ref is not None and slot < 2:
            acc[slot] = carry_ref[slot]
        else:
            acc[slot] = jnp.zeros(acc.shape[1:], F32)


def emitted(r0, count, side):
    first = 0 if r0 == 0 else r0 - 1
    last = side if r0 + count == side else r0 + count - 1
    return first, last, first - (r0 - 1)


def chunk_stats(acc, slot0, first, count, ext, side, batch, prev_ref, mean_only_ref=None):
    zero = jnp.zeros((batch, LANES), F32)

    def sums(k, carry):
        s, n = carry
        for c in range(side):
            m = pixel_mask(ext, first + k, c)
            s = s + m * acc[slot0 + k, c * batch : (c + 1) * batch, :]
            n = n + m
        return s, n

    s, n = lax.fori_loop(0, count, sums, (zero, zero))
    s = jnp.sum(s, axis=0, keepdims=True)
    n = jnp.sum(n, axis=0, keepdims=True)
    return s / jnp.maximum(n, 1.0), n


def merge_rows(mean_a, m2_a, n_a, mean_b, m2_b, n_b):
    n = n_a + n_b
    safe = jnp.maximum(n, 1.0)
    delta = mean_a - mean_b
    mean = (n_a * mean_a + n_b * mean_b) / safe
    return mean, m2_a + m2_b + delta * delta * (n_a * n_b / safe), n


def conv_forward_body(kind, r0, count, side, batch, blocks, *refs):
    refs = list(refs)
    ext_ref = refs.pop(0)
    w_ref = refs.pop(0)
    if kind == "images":
        sources = [refs.pop(0)]
        affine_ref = None
    else:
        sources = [refs.pop(0) for _ in range(blocks)]
        affine_ref = refs.pop(0)
    carry_ref = prev_ref = None
    if r0:
        carry_ref, prev_ref = refs.pop(0), refs.pop(0)
    h_ref, stat_ref = refs.pop(0), refs.pop(0)
    low_ref = refs.pop(0) if kind == "images" else None
    act_ref = refs.pop(0) if kind != "images" else None
    last_chunk = r0 + count == side
    carry_out = None if last_chunk else refs.pop(0)
    acc, row = refs[0], refs[1] if kind == "images" else None
    sem = refs[2] if kind == "images" else None
    width = blocks * LANES
    ext = ext_ref[...]
    start_acc(acc, carry_ref)

    if kind == "images":
        x_hbm = sources[0]

        def fetch(t, slot):
            return pltpu.make_async_copy(x_hbm.at[r0 + t], row.at[slot], sem.at[slot])

        fetch(0, 0).start()

        @pl.loop(0, count)
        def _(t):
            slot = lax.rem(t, 2)

            @pl.when(t + 1 < count)
            def _():
                fetch(t + 1, 1 - slot).start()

            fetch(t, slot).wait()
            pieces = []
            for c in range(side):
                m = pixel_mask(ext, r0 + t, c).astype(BF16)
                x = row[slot, c]
                pieces.append(
                    jnp.concatenate([x[:, k * LANES : (k + 1) * LANES] * m for k in range(blocks)], axis=1)
                )
            add_row(jnp.concatenate(pieces, axis=0), w_ref, acc, t, batch)
    else:

        @pl.loop(0, count)
        def _(t):
            for k in range(blocks):
                scale = affine_ref[k, 0:1, :]
                shift = affine_ref[k, 1:2, :]
                for c in range(side):
                    m = pixel_mask(ext, r0 + t, c)
                    z = sources[k][t, c].astype(F32) * scale + shift
                    act_ref[t, c, :, k * LANES : (k + 1) * LANES] = (gelu(z) * m).astype(BF16)
            add_row(act_ref[t].reshape(side * batch, width), w_ref, acc, t, batch)

    first, last, slot0 = emitted(r0, count, side)
    rows = last - first
    mean, n = chunk_stats(acc, slot0, first, rows, ext, side, batch, prev_ref)

    def squares(k, total):
        for c in range(side):
            m = pixel_mask(ext, first + k, c)
            h = acc[slot0 + k, c * batch : (c + 1) * batch, :]
            d = h - mean
            h_ref[k, c] = h
            if low_ref is not None:
                low_ref[k, c] = d.astype(BF16)
            total = total + m * (d * d)
        return total

    m2 = lax.fori_loop(0, rows, squares, jnp.zeros((batch, LANES), F32))
    m2 = jnp.sum(m2, axis=0, keepdims=True)
    whole = (mean, m2, n)
    if prev_ref is not None:
        whole = merge_rows(mean, m2, n, prev_ref[0:1], prev_ref[1:2], prev_ref[2:3])
    stat_ref[0:1] = whole[0]
    stat_ref[1:2] = whole[1]
    stat_ref[2:3] = whole[2]
    stat_ref[3:4] = mean
    stat_ref[4:8] = jnp.zeros((4, LANES), F32)
    if carry_out is not None:
        carry_out[0] = acc[count]
        carry_out[1] = acc[count + 1]


def conv_forward(kind, r0, count, ext, weights, sources, affine, carry, prev):
    side, batch = sources[0].shape[1], sources[0].shape[2]
    width = weights.shape[0]
    blocks = width // LANES
    first, last, _ = emitted(r0, count, side)
    rows = last - first
    ins = [ext, weights] + list(sources)
    if kind != "images":
        ins.append(affine)
    if r0:
        ins += [carry, prev]
    outs = [((rows, side, batch, LANES), F32), ((8, LANES), F32)]
    scratch = [pltpu.VMEM((count + 2, side * batch, LANES), F32)]
    any_in = ()
    if kind == "images":
        outs.append(((rows, side, batch, LANES), BF16))
        scratch += [pltpu.VMEM((2, side, batch, width), BF16), pltpu.SemaphoreType.DMA((2,))]
        any_in = (2,)
    else:
        outs.append(((count, side, batch, width), BF16))
    if r0 + count != side:
        outs.append(((2, side * batch, LANES), F32))
    return call(
        functools.partial(conv_forward_body, kind, r0, count, side, batch, blocks),
        outs,
        ins,
        scratch,
        flops=2 * count * side * batch * width * 9 * LANES,
        bytes_=count * side * batch * width * 2,
        any_in=any_in,
    )


def conv_back_body(kind, r0, count, side, batch, blocks, h_split, *refs):
    refs = list(refs)
    ext_ref, w_ref = refs.pop(0), refs.pop(0)
    sources = [refs.pop(0) for _ in range(blocks)]
    carry_ref = refs.pop(0) if r0 else None
    first, last, slot0 = emitted(r0, count, side)
    rows = last - first
    if kind == "active":
        affine_ref = refs.pop(0)
        prev_ref = refs.pop(0) if r0 else None
        parts = [s for s in segments(h_split) if s[1] > first and s[0] < last]
        h_refs = {s[2][0][0]: refs.pop(0) for s in parts}
        out_ref, sum_ref = refs.pop(0), refs.pop(0)
    else:
        grad_ref = refs.pop(0)
        if r0:
            refs.pop(0)
        out_hbm = refs.pop(0)
    carry_out = None if r0 + count == side else refs.pop(0)
    acc, lhs_ref = refs.pop(0), refs.pop(0)
    ext = ext_ref[...]
    start_acc(acc, carry_ref)

    @pl.loop(0, count)
    def _(t):
        lhs = jnp.concatenate([sources[k][t].reshape(side * batch, LANES) for k in range(blocks)], axis=1)
        add_row(lhs, w_ref, acc, t, batch)

    if carry_out is not None:
        carry_out[0] = acc[count]
        carry_out[1] = acc[count + 1]
    if kind == "active":
        scale, shift = affine_ref[0:1, :], affine_ref[1:2, :]
        rscale, offset = affine_ref[2:3, :], affine_ref[3:4, :]
        zero = jnp.zeros((batch, LANES), F32)
        total = (zero, zero)
        for start, stop, where in parts:
            index, base = where[0]
            lo, hi = max(start, first), min(stop, last)

            def one(r, carry, index=index, base=base):
                ds, dn = carry
                for c in range(side):
                    m = pixel_mask(ext, r, c)
                    h = h_refs[index][r - base, c]
                    _, slope = gelu_both(h * scale + shift)
                    dz = acc[slot0 + r - first, c * batch : (c + 1) * batch, :] * m * slope
                    out_ref[r - first, c] = dz
                    ds = ds + dz
                    dn = dn + dz * (h * rscale + offset)
                return ds, dn

            total = lax.fori_loop(lo, hi, one, total)
        ds = jnp.sum(total[0], axis=0, keepdims=True)
        dn = jnp.sum(total[1], axis=0, keepdims=True)
        if prev_ref is not None:
            ds = ds + prev_ref[0:1]
            dn = dn + prev_ref[1:2]
        sum_ref[0:1] = ds
        sum_ref[1:2] = dn
        sum_ref[2:8] = jnp.zeros((6, LANES), F32)
    else:
        stage, sem = refs.pop(0), refs.pop(0)

        @pl.loop(0, rows)
        def _(k):
            for c in range(side):
                m = pixel_mask(ext, first + k, c)
                stage[k, c] = m * (grad_ref[k, c] + acc[slot0 + k, c * batch : (c + 1) * batch, :])
            pltpu.make_async_copy(stage.at[k], out_hbm.at[first + k], sem.at[k]).start()

        @pl.loop(0, rows)
        def _(k):
            pltpu.make_async_copy(stage.at[k], out_hbm.at[first + k], sem.at[k]).wait()


def conv_back(kind, r0, count, ext, weights, sources, carry, extra, h_split=None, prev=None, target=None):
    side, batch = sources[0].shape[1], sources[0].shape[2]
    blocks = len(sources)
    first, last, _ = emitted(r0, count, side)
    rows = last - first
    ins = [ext, weights] + list(sources)
    if r0:
        ins.append(carry)
    scratch = [pltpu.VMEM((count + 2, side * batch, LANES), F32), pltpu.VMEM((8, LANES), F32)]
    aliases, any_in, any_out = {}, (), ()
    if kind == "active":
        affine, h_parts = extra
        ins.append(affine)
        if r0:
            ins.append(prev)
        for s in segments(h_split):
            if s[1] > first and s[0] < last:
                ins.append(h_parts[s[2][0][0]])
        outs = [((rows, side, batch, LANES), F32), ((8, LANES), F32)]
    else:
        ins.append(extra)
        if r0:
            any_in = (len(ins),)
            aliases = {len(ins): 0}
            ins.append(target)
        outs = [((side, side, batch, LANES), F32)]
        any_out = (0,)
        scratch += [pltpu.VMEM((rows, side, batch, LANES), F32), pltpu.SemaphoreType.DMA((rows,))]
    if r0 + count != side:
        outs.append(((2, side * batch, LANES), F32))
    return call(
        functools.partial(conv_back_body, kind, r0, count, side, batch, blocks, h_split),
        outs,
        ins,
        scratch,
        flops=2 * count * side * batch * blocks * LANES * 9 * LANES,
        bytes_=count * side * batch * blocks * LANES * 2,
        aliases=aliases,
        any_in=any_in,
        any_out=any_out,
    )


def weight_grad_body(kind, side, batch, blocks, splits, *refs):
    refs = list(refs)
    chan_ref = refs.pop(0)
    ext_ref = refs.pop(0)
    x_refs = [refs.pop(0) for _ in splits[0]]
    g_refs = [refs.pop(0) for _ in splits[1]]
    out_ref, acc, gs = refs
    chan = chan_ref[0]
    ext = ext_ref[...]
    rows = side * batch
    gs[0] = jnp.zeros((rows, LANES), BF16)
    gs[side + 1] = jnp.zeros((rows, LANES), BF16)
    at = 0
    for ref, size in zip(g_refs, splits[1]):
        for k in range(size):
            gs[at + k + 1] = ref[k].reshape(rows, LANES)
        at += size
    acc[...] = jnp.zeros(acc.shape, F32)
    edge = jnp.zeros((batch, LANES), BF16)
    at = 0
    for ref, size in zip(x_refs, splits[0]):

        @pl.loop(at, at + size)
        def _(r, ref=ref, at=at):
            if kind == "images":
                pieces = []
                for c in range(side):
                    m = pixel_mask(ext, r, c).astype(BF16)
                    x = ref[r - at, c]
                    pieces.append(
                        jnp.concatenate([x[:, k * LANES : (k + 1) * LANES] * m for k in range(blocks)], axis=1)
                    )
                x = jnp.concatenate(pieces, axis=0)
            else:
                x = ref[r - at].reshape(rows, blocks * LANES)
            parts = []
            for i in range(3):
                g = gs[r + 2 - i]
                parts.append(jnp.concatenate([g[batch:], edge], axis=0))
                parts.append(g)
                parts.append(jnp.concatenate([edge, g[: rows - batch]], axis=0))
            wide = jnp.concatenate(parts, axis=1)
            acc[...] += lax.dot_general(
                x, wide, (((0,), (0,)), ((), ())), preferred_element_type=F32
            )

        at += size
    for k in range(blocks):
        if kind == "images":
            rows_out = pl.ds(k * LANES, LANES)
        else:
            rows_out = pl.ds(pl.multiple_of(jnp.bitwise_xor(chan, k) * LANES, LANES), LANES)
        for t in range(9):
            out_ref[t, rows_out, :] = acc[k * LANES : (k + 1) * LANES, t * LANES : (t + 1) * LANES]


def weight_grad(kind, chan, ext, xs, gs):
    side, batch, width = xs[0].shape[1], xs[0].shape[2], xs[0].shape[3]
    blocks = width // LANES
    splits = ([x.shape[0] for x in xs], [g.shape[0] for g in gs])
    return call(
        functools.partial(weight_grad_body, kind, side, batch, blocks, splits),
        [((9, width, LANES), F32)],
        [chan, ext] + list(xs) + list(gs),
        [pltpu.VMEM((width, 9 * LANES), F32), pltpu.VMEM((side + 2, side * batch, LANES), BF16)],
        flops=2 * side * side * batch * width * 9 * LANES,
        bytes_=side * side * batch * width * 2,
        smem_in=(0,),
    )[0]


def block_end_body(side, batch, h_split, out_split, *refs):
    refs = list(refs)
    chan_ref, ext_ref, affine_ref, images_hbm, cot_ref = refs[:5]
    refs = refs[5:]
    h_refs = [refs.pop(0) for _ in h_split]
    out_ref = refs.pop(0)
    grad_refs = [refs.pop(0) for _ in out_split]
    sum_ref, own, sem = refs
    lanes = pl.ds(pl.multiple_of(chan_ref[0] * LANES, LANES), LANES)
    copy = pltpu.make_async_copy(images_hbm.at[:, :, :, lanes], own, sem)
    copy.start()
    copy.wait()
    ext = ext_ref[...]
    scale, shift = affine_ref[0:1, :], affine_ref[1:2, :]
    rscale, offset = affine_ref[2:3, :], affine_ref[3:4, :]
    zero = jnp.zeros((batch, LANES), F32)
    total = (zero, zero)
    for start, stop, ((hi, hb), (gi, gb)) in segments(h_split, out_split):

        def one(r, carry, hi=hi, hb=hb, gi=gi, gb=gb):
            ds, dn = carry
            for c in range(side):
                m = pixel_mask(ext, r, c)
                h = h_refs[hi][r - hb, c]
                pre = h * scale + shift + own[r, c].astype(F32) * m
                value, slope = gelu_both(pre)
                out_ref[r, c] = (value * m).astype(BF16)
                dz = cot_ref[r, c].astype(F32) * m * slope
                grad_refs[gi][r - gb, c] = dz
                ds = ds + dz
                dn = dn + dz * (h * rscale + offset)
            return ds, dn

        total = lax.fori_loop(start, stop, one, total)
    sum_ref[0:1] = jnp.sum(total[0], axis=0, keepdims=True)
    sum_ref[1:2] = jnp.sum(total[1], axis=0, keepdims=True)
    sum_ref[2:8] = jnp.zeros((6, LANES), F32)


def block_end(chan, ext, affine, images, cotangent, h_parts, out_split):
    side, batch = images.shape[1], images.shape[2]
    h_split = [h.shape[0] for h in h_parts]
    outs = [((side, side, batch, LANES), BF16)]
    outs += [((n, side, batch, LANES), F32) for n in out_split]
    outs.append(((8, LANES), F32))
    return call(
        functools.partial(block_end_body, side, batch, h_split, out_split),
        outs,
        [chan, ext, affine, images, cotangent] + list(h_parts),
        [pltpu.VMEM((side, side, batch, LANES), BF16), pltpu.SemaphoreType.DMA],
        flops=side * side * batch * LANES * 100,
        bytes_=side * side * batch * LANES * 20,
        smem_in=(0,),
        any_in=(3,),
    )


def norm_back_body(side, batch, splits, *refs):
    refs = list(refs)
    ext_ref, coef_ref = refs.pop(0), refs.pop(0)
    h_refs = [refs.pop(0) for _ in splits[0]]
    dz_refs = [refs.pop(0) for _ in splits[1]]
    out_refs = [refs.pop(0) for _ in splits[2]]
    ext = ext_ref[...]
    a, b, c0 = coef_ref[0:1, :], coef_ref[1:2, :], coef_ref[2:3, :]
    for start, stop, ((hi, hb), (zi, zb), (oi, ob)) in segments(*splits):

        @pl.loop(start, stop)
        def _(r, hi=hi, hb=hb, zi=zi, zb=zb, oi=oi, ob=ob):
            for c in range(side):
                m = pixel_mask(ext, r, c)
                grad = a * dz_refs[zi][r - zb, c] - (h_refs[hi][r - hb, c] * b + c0)
                out_refs[oi][r - ob, c] = (m * grad).astype(BF16)


def norm_back(ext, coef, h_parts, dz_parts, out_split):
    side, batch = h_parts[0].shape[1], h_parts[0].shape[2]
    splits = ([h.shape[0] for h in h_parts], [z.shape[0] for z in dz_parts], list(out_split))
    return call(
        functools.partial(norm_back_body, side, batch, splits),
        [((n, side, batch, LANES), BF16) for n in out_split],
        [ext, coef] + list(h_parts) + list(dz_parts),
        flops=side * side * batch * LANES * 8,
        bytes_=side * side * batch * LANES * 10,
    )


def swap(x, axis, size, k):
    return lax.ppermute(x, axis, [(i, i ^ k) for i in range(size)])


def sum_over(x, axis, size):
    k = 1
    while k < size:
        x = x + swap(x, axis, size, k)
        k *= 2
    return x


def merge_over(stats, axis, size):
    k = 1
    while k < size:
        other = swap(stats, axis, size, k)
        stats = jnp.stack(merge_rows(stats[0], stats[1], stats[2], other[0], other[1], other[2]))
        k *= 2
    return stats


def gather_blocks(x, size):
    far = swap(x, "chan", size, 2)
    near = swap(x, "chan", size, 1)
    return [x, near, far, swap(far, "chan", size, 1)]


def reduce_grad(grad, size):
    index = lax.axis_index("dp")
    current = grad.reshape(-1, LANES)
    k = 1
    while k < size:
        half = current.shape[0] // 2
        low, high = current[:half], current[half:]
        upper = (index // k) % 2 == 1
        keep = jnp.where(upper, high, low)
        send = jnp.where(upper, low, high).astype(BF16)
        current = keep + swap(send, "dp", size, k).astype(F32)
        k *= 2
    squares = jnp.sum(current * current)
    current = current.astype(BF16)
    while k > 1:
        k //= 2
        other = swap(current, "dp", size, k)
        upper = (index // k) % 2 == 1
        current = jnp.where(upper, jnp.concatenate([other, current]), jnp.concatenate([current, other]))
    return current.astype(F32).reshape(grad.shape), squares


def layer_affine(stats, gain, shift):
    center, spread = stats[0], stats[1] / stats[2]
    rscale = lax.rsqrt(spread + EPSILON)
    scale = rscale * gain
    return jnp.stack([scale, shift - center * scale, rscale, -center * rscale])


def back_coef(affine, sums, count):
    scale, rscale, offset = affine[0], affine[2], affine[3]
    shift_grad, gain_grad = sums[0] / count, sums[1] / count
    return jnp.stack([scale, scale * rscale * gain_grad, scale * (shift_grad + offset * gain_grad)])


def shards(
    dp, ch, images, groups, cotangent, weight_one, gain_one, shift_one, weight_two, gain_two, shift_two, moment_one, moment_two
):
    side = images.shape[1]
    images = jnp.transpose(images, (1, 2, 0, 3))
    cotangent = jnp.transpose(cotangent, (1, 2, 0, 3))
    batch = images.shape[2]
    chan = lax.axis_index("chan").astype(jnp.int32).reshape(1)
    ext = jnp.broadcast_to((5 + 2 * groups)[:, None], (batch, LANES))
    third = side // 3
    conv_in = (third + 1, third, side - 2 * third - 1)
    flow = (third, third, side - 2 * third)
    flow_out = (third - 1, third, side - 2 * third + 1)

    wb_one, wt_one, sq_one = prep(weight_one, chan, False)
    wb_two, wt_two, sq_two = prep(weight_two, chan, True)

    h_one, low_one, means, carry, stat = [], [], [], None, None
    for r0, count in zip(chunk_starts(side, conv_in), conv_in):
        out = conv_forward("images", r0, count, ext, wb_one, [images], None, carry, stat)
        h, stat, low = out[:3]
        carry = out[3] if len(out) > 3 else None
        h_one.append(h)
        low_one.append(gather_blocks(low, ch))
        means.append(stat[3])
    stats_one = merge_over(stat[:3], "dp", dp)
    affine_one = layer_affine(stats_one, gain_one, shift_one)
    count_all = stats_one[2]
    params = jnp.stack([affine_one[0]] + [m * affine_one[0] + affine_one[1] for m in means])
    near = swap(params, "chan", ch, 1)
    both = jnp.stack([params, near])
    both = jnp.concatenate([both, swap(both, "chan", ch, 2)])

    h_two, act, carry, stat = [], [], None, None
    for q, (r0, count) in enumerate(zip(chunk_starts(side, flow), flow)):
        affine = jnp.stack([both[:, 0], both[:, 1 + q]], axis=1)
        out = conv_forward("blocks", r0, count, ext, wb_two, low_one[q], affine, carry, stat)
        h, stat, a = out[:3]
        carry = out[3] if len(out) > 3 else None
        h_two.append(h)
        act.append(a)
    stats_two = merge_over(stat[:3], "dp", dp)
    affine_two = layer_affine(stats_two, gain_two, shift_two)

    wt = jnp.stack([wt_one, wt_two], axis=1)
    wt, _ = lax.optimization_barrier((wt, stat))
    wt = [wt[0]] + [swap(wt[k], "chan", ch, k) for k in range(1, ch)]
    wt_one = jnp.concatenate([w[0] for w in wt])
    wt_two = jnp.concatenate([w[1] for w in wt])

    out = block_end(chan, ext, affine_two, images, cotangent, h_two, flow_out)
    block_output, grad_pre, sums = out[0], out[1:-1], out[-1]
    sums_two = sum_over(sums[:2], "dp", dp)
    grad_two = norm_back(ext, back_coef(affine_two, sums_two, count_all), h_two, grad_pre, flow)
    gathered = [gather_blocks(g, ch) for g in grad_two]
    weight_two_grad = weight_grad("act", chan, ext, act, grad_two)
    dz_one, carry, sums = [], None, None
    for q, (r0, count) in enumerate(zip(chunk_starts(side, flow), flow)):
        out = conv_back(
            "active", r0, count, ext, wt_two, gathered[q], carry, (affine_one, h_one), flow, sums
        )
        dz, sums = out[:2]
        carry = out[2] if len(out) > 2 else None
        dz_one.append(dz)
    sums_one = sum_over(sums[:2], "dp", dp)
    grad_one = norm_back(ext, back_coef(affine_one, sums_one, count_all), h_one, dz_one, flow)
    gathered = [gather_blocks(g, ch) for g in grad_one]
    weight_one_grad = weight_grad("images", chan, ext, [images], grad_one)
    input_grad, carry = None, None
    for q, (r0, count) in enumerate(zip(chunk_starts(side, flow), flow)):
        out = conv_back(
            "input", r0, count, ext, wt_one, gathered[q], carry, grad_pre[q], target=input_grad
        )
        input_grad = out[0]
        carry = out[1] if len(out) > 1 else None

    weight_two_grad, square_two = reduce_grad(weight_two_grad, dp)
    weight_one_grad, square_one = reduce_grad(weight_one_grad, dp)
    own = jnp.stack([jnp.sum(sq_one) / dp, jnp.sum(sq_two) / dp, square_one, square_two])
    norms = jnp.sqrt(sum_over(sum_over(own, "dp", dp), "chan", ch))
    weight_norms, grad_norms = norms[:2], norms[2:]
    trust = TRUST_COEF * weight_norms / (grad_norms + DECAY * weight_norms)
    moment_one_new = MOMENTUM * moment_one + LEARN_RATE * trust[0] * (weight_one_grad + DECAY * weight_one)
    moment_two_new = MOMENTUM * moment_two + LEARN_RATE * trust[1] * (weight_two_grad + DECAY * weight_two)
    return (
        jnp.transpose(block_output, (2, 0, 1, 3)),
        jnp.transpose(input_grad, (2, 0, 1, 3)),
        weight_one_grad,
        sums_one[1],
        sums_one[0],
        weight_two_grad,
        sums_two[1],
        sums_two[0],
        moment_one_new,
        moment_two_new,
        weight_norms,
        grad_norms,
    )


def solution(mesh):
    full, rows, both = P("dp", None, None, None), P("dp"), P("dp", None, None, "chan")
    weight, channel = P(None, None, "chan"), P("chan")
    return jax.shard_map(
        functools.partial(shards, mesh.shape["dp"], mesh.shape["chan"]),
        mesh=mesh,
        in_specs=(full, rows, both, weight, channel, channel, weight, channel, channel, weight, weight),
        out_specs=(both, both, weight, channel, channel, weight, channel, channel, weight, weight, P(), P()),
        check_vma=False,
    )
```

```python
import functools

import jax
import jax.numpy as jnp
from jax import lax
from jax.experimental import pallas as pl
from jax.experimental.pallas import tpu as pltpu
from jax.sharding import PartitionSpec as P

EPSILON = 1e-05
MOMENTUM = 0.9
LEARN_RATE = 8.0
TRUST_COEF = 0.001
DECAY = 5e-05
GELU_A = 0.7978845608028654
GELU_B = 0.7978845608028654 * 0.044715
F32 = jnp.float32
BF16 = jnp.bfloat16
LANES = 128
TAPS = 9
PAIRS = ((0, 2), (2, 4), (4, 6), (6, 8), (8, 9))
VMEM_BYTES = 60 * 1024 * 1024
DMA = pltpu.SemaphoreType.DMA


def mask_at(ext, r, c):
    if isinstance(r, int) and max(r, c) < 5:
        return None
    return jnp.where(ext > jnp.maximum(r, c), 1.0, 0.0).astype(F32)


def times(x, m):
    return x if m is None else x * m


def gelu(v):
    t = jnp.tanh(v * (GELU_A + GELU_B * (v * v)))
    half = 0.5 * v
    return half + half * t


def gelu_both(v):
    sq = v * v
    t = jnp.tanh(v * (GELU_A + GELU_B * sq))
    half = 0.5 * v
    value = half + half * t
    slope = 0.5 + 0.5 * t + (half - half * (t * t)) * (GELU_A + (3.0 * GELU_B) * sq)
    return value, slope


def call(name, body, outs, ins, scratch=(), aliases=None):
    spec = {"a": pl.BlockSpec(memory_space=pl.ANY), "s": pl.BlockSpec(memory_space=pltpu.SMEM)}
    n_in, n_out, n_scratch = len(ins), len(outs), len(scratch)
    in_places = [k for k, (_, w) in enumerate(ins) if w == "v"]
    out_places = [k for k, (_, _, w) in enumerate(outs) if w == "v"]

    def whole(*refs):
        args = list(refs[: n_in + n_out + n_scratch])
        buffers, sems = list(refs[n_in + n_out + n_scratch : -1]), refs[-1]
        loads, stores = [], []
        for k in in_places:
            loads.append(pltpu.make_async_copy(refs[k], buffers[0], sems.at[len(loads)]))
            args[k] = buffers.pop(0)
            loads[-1].start()
        for k in out_places:
            stores.append(
                pltpu.make_async_copy(buffers[0], refs[n_in + k], sems.at[len(loads) + len(stores)])
            )
            args[n_in + k] = buffers.pop(0)

        def ready():
            for copy in loads:
                copy.wait()

        waits = body(ready, *args) or []
        for copy in stores:
            copy.start()
        for copy in stores + waits:
            copy.wait()

    extra = [pltpu.VMEM(ins[k][0].shape, ins[k][0].dtype) for k in in_places]
    extra += [pltpu.VMEM(outs[k][0], outs[k][1]) for k in out_places]
    extra.append(DMA((max(1, len(in_places) + len(out_places)),)))
    return pl.pallas_call(
        whole,
        name=name,
        out_shape=[jax.ShapeDtypeStruct(s, d) for s, d, _ in outs],
        in_specs=[spec["s" if w == "s" else "a"] for _, w in ins],
        out_specs=[spec["a"] for _ in outs],
        scratch_shapes=list(scratch) + extra,
        input_output_aliases=aliases or {},
        compiler_params=pltpu.CompilerParams(vmem_limit_bytes=VMEM_BYTES),
        cost_estimate=pl.CostEstimate(flops=0, bytes_accessed=0, transcendentals=0),
    )(*[x for x, _ in ins])


class Takes:
    def __init__(self, refs):
        self.refs = list(refs)

    def __call__(self, n=None):
        if n is None:
            return self.refs.pop(0)
        return [self.refs.pop(0) for _ in range(n)]


def prep_body(blocks, ready, chan_ref, one_ref, two_ref, wb_ref, wt_ref, sq_ref):
    ready()
    chan = chan_ref[0]
    sq_ref[...] = jnp.zeros(sq_ref.shape, F32)
    for layer, w_ref in enumerate((one_ref, two_ref)):
        total = jnp.zeros((1, LANES), F32)
        for k in range(blocks):
            rows = pl.ds(pl.multiple_of(jnp.bitwise_xor(chan, k) * LANES, LANES), LANES)
            for t in range(TAPS):
                piece = w_ref[t, rows, :]
                total = total + jnp.sum(piece * piece, axis=0, keepdims=True)
                if layer:
                    wb_ref[k * LANES : (k + 1) * LANES, t * LANES : (t + 1) * LANES] = piece.astype(BF16)
                flip = TAPS - 1 - t
                wt_ref[k, layer, :, flip * LANES : (flip + 1) * LANES] = piece.T.astype(BF16)
        sq_ref[layer : layer + 1] = total


def prep(weight_one, weight_two, chan):
    width = weight_one.shape[1]
    blocks = width // LANES
    return call(
        "prep",
        functools.partial(prep_body, blocks),
        [
            ((width, TAPS * LANES), BF16, "v"),
            ((blocks, 2, LANES, TAPS * LANES), BF16, "v"),
            ((8, LANES), F32, "v"),
        ],
        [(chan, "s"), (weight_one, "v"), (weight_two, "v")],
    )


def add_row(lhs_ref, w_ref, acc, slot, batch):
    rows = lhs_ref.shape[0]
    for a, b in PAIRS:
        y = jnp.dot(lhs_ref[...], w_ref[:, a * LANES : b * LANES], preferred_element_type=F32)
        for t in range(a, b):
            i, j = divmod(t, 3)
            z = y[:, (t - a) * LANES : (t - a + 1) * LANES]
            at = slot + 2 - i
            if j == 0:
                acc[at, batch:] += z[: rows - batch]
            elif j == 1:
                acc[at] += z
            else:
                acc[at, : rows - batch] += z[batch:]


def start_acc(acc, carry_ref):
    for slot in range(acc.shape[0]):
        if carry_ref is not None and slot < 2:
            acc[slot] = carry_ref[slot]
        else:
            acc[slot] = jnp.zeros(acc.shape[1:], F32)


def emitted(r0, count, side):
    first = 0 if r0 == 0 else r0 - 1
    last = side if r0 + count == side else r0 + count - 1
    return first, last, first - (r0 - 1)


def ready_rows(t, r0, count, side):
    r = r0 + t
    rows = [r - 1] if r > 0 else []
    return rows + [r] if r == side - 1 else rows


class Stats:
    def __init__(self, ext, side, batch):
        self.ext, self.side, self.batch = ext, side, batch
        self.ref = None
        zero = jnp.zeros((batch, LANES), F32)
        self.s1, self.s2, self.n = zero, zero, zero

    def row(self, acc, slot, r, low_ref=None):
        batch = self.batch
        if self.ref is None:
            s = n = jnp.zeros((batch, LANES), F32)
            for c in range(self.side):
                m = mask_at(self.ext, r, c)
                s = s + times(acc[slot, c * batch : (c + 1) * batch], m)
                n = n + (1.0 if m is None else m)
            n = jnp.sum(n, axis=0, keepdims=True)
            self.ref = jnp.sum(s, axis=0, keepdims=True) / jnp.maximum(n, 1.0)
        for c in range(self.side):
            m = mask_at(self.ext, r, c)
            d = acc[slot, c * batch : (c + 1) * batch] - self.ref
            if low_ref is not None:
                low_ref[c * batch : (c + 1) * batch] = d.astype(BF16)
            masked = times(d, m)
            self.s1 = self.s1 + masked
            self.s2 = self.s2 + masked * d
            self.n = self.n + (1.0 if m is None else m)

    def store(self, stat_ref, prev_ref, chunk):
        s1, s2, n = (jnp.sum(x, axis=0, keepdims=True) for x in (self.s1, self.s2, self.n))
        safe = jnp.maximum(n, 1.0)
        whole = (self.ref + s1 / safe, s2 - s1 * s1 / safe, n)
        stat_ref[...] = jnp.zeros(stat_ref.shape, F32) if prev_ref is None else prev_ref[...]
        if prev_ref is not None:
            whole = merge_rows(*(prev_ref[k : k + 1] for k in range(3)), *whole)
        for k in range(3):
            stat_ref[k : k + 1] = whole[k]
        stat_ref[3 + chunk : 4 + chunk] = self.ref


def merge_rows(mean_a, m2_a, n_a, mean_b, m2_b, n_b):
    n = n_a + n_b
    safe = jnp.maximum(n, 1.0)
    delta = mean_a - mean_b
    mean = (n_a * mean_a + n_b * mean_b) / safe
    return mean, m2_a + m2_b + delta * delta * (n_a * n_b / safe), n


def conv_forward_body(kind, chunk, r0, count, side, batch, blocks, ready, place_ref, *refs):
    take = Takes(refs)
    ext_ref, w_in = take(), take()
    images = kind == "images"
    sources = take(1 if images else blocks)
    params = None if images else take(blocks)
    carry_ref = prev_ref = None
    if r0:
        carry_ref, prev_ref = take(), take()
        take(1 if images else 2)
    h_hbm, stat_ref = take(), take()
    low_hbm = take() if images else None
    act_hbm = None if images else take()
    wb_hbm = take() if images and r0 == 0 else None
    last_chunk = r0 + count == side
    carry_out = None if last_chunk else take()
    acc = take()
    raw, in_sem, out_sem = take(), take(), take()
    lhs = take(count)
    waits = []

    def send(src, dst, sem):
        copy = pltpu.make_async_copy(src, dst, sem)
        copy.start()
        waits.append(copy)

    fetches = []
    if images:
        for t in range(count):
            fetches.append([pltpu.make_async_copy(sources[0].at[r0 + t], raw.at[t], in_sem.at[t])])
    else:
        for t in range(count):
            fetches.append(
                [
                    pltpu.make_async_copy(sources[k].at[t], raw.at[k, t], in_sem.at[t * blocks + k])
                    for k in range(blocks)
                ]
            )
    for group in fetches[:1]:
        for copy in group:
            copy.start()
    if images and r0 == 0:
        w_raw, w_sem, wb, wb_sem = take(), take(), take(), take()
        taps = [pltpu.make_async_copy(w_in.at[t], w_raw.at[t], w_sem.at[t]) for t in range(TAPS)]
        for copy in taps:
            copy.start()
    for group in fetches[1:]:
        for copy in group:
            copy.start()
    ready()
    ext = ext_ref[...]
    start_acc(acc, carry_ref)
    if images and r0 == 0:
        for t in range(TAPS):
            taps[t].wait()
            wb[:, t * LANES : (t + 1) * LANES] = w_raw[t].astype(BF16)
        send(wb, wb_hbm, wb_sem)
        w_ref = wb
    else:
        w_ref = w_in
    low = take() if images else None

    def stage(t):
        for copy in fetches[t]:
            copy.wait()
        for c in range(side):
            part = slice(c * batch, (c + 1) * batch)
            m = mask_at(ext, r0 + t, c)
            for k in range(blocks):
                lanes = slice(k * LANES, (k + 1) * LANES)
                if images:
                    x = raw[t, part, lanes]
                    lhs[t][part, lanes] = x if m is None else x * m.astype(BF16)
                else:
                    z = raw[k, t, part].astype(F32) * params[k][0:1] + params[k][5 + chunk : 6 + chunk]
                    lhs[t][part, lanes] = times(gelu(z), m).astype(BF16)
        if not images:
            for k in range(blocks):
                to = pl.ds(pl.multiple_of(jnp.bitwise_xor(place_ref[0], k) * LANES, LANES), LANES)
                send(
                    lhs[t].at[:, k * LANES : (k + 1) * LANES],
                    act_hbm.at[r0 + t, :, to],
                    out_sem.at[2 * (count + 1) + t * blocks + k],
                )

    first, last, slot0 = emitted(r0, count, side)
    stats = Stats(ext, side, batch)

    def finish(t):
        for r in ready_rows(t, r0, count, side):
            slot, k = r - (r0 - 1), r - first
            send(acc.at[slot], h_hbm.at[r], out_sem.at[k])
            stats.row(acc, slot, r, low.at[k] if images else None)
            if images:
                send(low.at[k], low_hbm.at[k], out_sem.at[count + 1 + k])

    stage(0)
    for t in range(count):
        if t + 1 < count:
            stage(t + 1)
        add_row(lhs[t], w_ref, acc, t, batch)
        finish(t)
    stats.store(stat_ref, prev_ref, chunk)
    if carry_out is not None:
        carry_out[0] = acc[count]
        carry_out[1] = acc[count + 1]
    return waits


def conv_forward(kind, chunk, r0, count, side, batch, place, ext, weights, sources, params, carry, prev, targets):
    images = kind == "images"
    pixels = side * batch
    width = sources[0].shape[2] if images else LANES * len(sources)
    blocks = width // LANES
    first, last, _ = emitted(r0, count, side)
    rows = last - first
    ins = [(place, "s"), (ext, "v"), (weights, "a" if images and r0 == 0 else "v")] + [(x, "a") for x in sources]
    if not images:
        ins += [(p, "v") for p in params]
    aliases = {}
    if r0:
        ins += [(carry, "v"), (prev, "v")]
        aliases[len(ins)] = 0
        ins.append((targets[0], "a"))
        if not images:
            aliases[len(ins)] = 2
            ins.append((targets[1], "a"))
    outs = [((side, pixels, LANES), F32, "a"), ((8, LANES), F32, "v")]
    if images:
        outs.append(((rows, pixels, LANES), BF16, "a"))
    else:
        outs.append(((side, pixels, width), BF16, "a"))
    if images and r0 == 0:
        outs.append(((width, TAPS * LANES), BF16, "a"))
    if r0 + count != side:
        outs.append(((2, pixels, LANES), F32, "v"))
    scratch = [pltpu.VMEM((count + 2, pixels, LANES), F32)]
    scratch.append(pltpu.VMEM((count, pixels, width) if images else (blocks, count, pixels, LANES), BF16))
    scratch += [DMA((count if images else count * blocks,)), DMA((2 * (count + 1) + count * blocks,))]
    scratch += [pltpu.VMEM((pixels, width), BF16) for _ in range(count)]
    if images and r0 == 0:
        scratch += [pltpu.VMEM((TAPS, width, LANES), F32), DMA((TAPS,)), pltpu.VMEM((width, TAPS * LANES), BF16), DMA]
    if images:
        scratch.append(pltpu.VMEM((rows, pixels, LANES), BF16))
    return call(
        f"conv_{kind}_{r0}",
        functools.partial(conv_forward_body, kind, chunk, r0, count, side, batch, blocks),
        outs,
        ins,
        scratch,
        aliases,
    )


def conv_back_body(kind, r0, count, side, batch, blocks, ready, *refs):
    take = Takes(refs)
    ext_ref, w_ref = take(), take()
    sources = take(blocks)
    active = kind == "active"
    side_hbm = take()
    params_ref = take() if active else None
    carry_ref = prev_ref = None
    if r0:
        carry_ref = take()
        prev_ref = take() if active else None
        take()
    out_hbm = take()
    sum_ref = take() if active else None
    carry_out = None if r0 + count == side else take()
    acc, extra, stage, in_sem, side_sem, out_sem = take(6)
    lhs = take(count)
    first, last, slot0 = emitted(r0, count, side)
    waits = []
    fetches = [
        [
            pltpu.make_async_copy(
                sources[k].at[t], lhs[t].at[:, k * LANES : (k + 1) * LANES], in_sem.at[t * blocks + k]
            )
            for k in range(blocks)
        ]
        for t in range(count)
    ]
    for group in fetches:
        for copy in group:
            copy.start()
    others = [pltpu.make_async_copy(side_hbm.at[first + k], extra.at[k], side_sem.at[k]) for k in range(last - first)]
    for copy in others:
        copy.start()
    ready()
    ext = ext_ref[...]
    start_acc(acc, carry_ref)
    zero = jnp.zeros((batch, LANES), F32)
    total = [zero, zero]
    if active:
        scale, shift, rscale, offset = (params_ref[k : k + 1] for k in range(4))

    def finish(t):
        for r in ready_rows(t, r0, count, side):
            slot, k = r - (r0 - 1), r - first
            others[k].wait()
            for c in range(side):
                part = slice(c * batch, (c + 1) * batch)
                m = mask_at(ext, r, c)
                if active:
                    h = extra[k, part]
                    _, slope = gelu_both(h * scale + shift)
                    dz = times(acc[slot, part], m) * slope
                    stage[k, part] = dz
                    total[0] = total[0] + dz
                    total[1] = total[1] + dz * (h * rscale + offset)
                else:
                    stage[k, part] = times(extra[k, part] + acc[slot, part], m)
            copy = pltpu.make_async_copy(stage.at[k], out_hbm.at[r], out_sem.at[k])
            copy.start()
            waits.append(copy)

    for t in range(count):
        for copy in fetches[t]:
            copy.wait()
        add_row(lhs[t], w_ref, acc, t, batch)
        finish(t)
    if carry_out is not None:
        carry_out[0] = acc[count]
        carry_out[1] = acc[count + 1]
    if active:
        sum_ref[...] = jnp.zeros(sum_ref.shape, F32)
        for k in range(2):
            s = jnp.sum(total[k], axis=0, keepdims=True)
            sum_ref[k : k + 1] = s if prev_ref is None else s + prev_ref[k : k + 1]
    return waits


def conv_back(kind, r0, count, side, batch, ext, weights, sources, extra, params, carry, prev, target):
    blocks, pixels = len(sources), side * batch
    first, last, _ = emitted(r0, count, side)
    rows = last - first
    ins = [(ext, "v"), (weights, "v")] + [(x, "a") for x in sources] + [(extra, "a")]
    active = kind == "active"
    if active:
        ins.append((params, "v"))
    aliases = {}
    if r0:
        ins.append((carry, "v"))
        if active:
            ins.append((prev, "v"))
        aliases[len(ins)] = 0
        ins.append((target, "a"))
    outs = [((side, pixels, LANES), F32, "a")]
    if active:
        outs.append(((8, LANES), F32, "v"))
    if r0 + count != side:
        outs.append(((2, pixels, LANES), F32, "v"))
    scratch = [
        pltpu.VMEM((count + 2, pixels, LANES), F32),
        pltpu.VMEM((rows, pixels, LANES), F32),
        pltpu.VMEM((rows, pixels, LANES), F32),
        DMA((count * blocks,)),
        DMA((rows,)),
        DMA((rows,)),
    ]
    scratch += [pltpu.VMEM((pixels, blocks * LANES), BF16) for _ in range(count)]
    return call(
        f"back_{kind}_{r0}",
        functools.partial(conv_back_body, kind, r0, count, side, batch, blocks),
        outs,
        ins,
        scratch,
        aliases,
    )


def weight_grad_body(kind, side, batch, blocks, splits, ready, *refs):
    take = Takes(refs)
    place_ref, ext_ref, x_hbm = take(), take(), take()
    g_hbms = take(len(splits))
    keep_ref, send_ref, acc, gs, xs, g_sem, x_sem = take(7)
    upper = place_ref[1]
    rows = side * batch
    g_copies, at = [], 0
    for ref, size in zip(g_hbms, splits):
        for k in range(size):
            g_copies.append(pltpu.make_async_copy(ref.at[k], gs.at[at + 1], g_sem.at[at]))
            at += 1
    x_copies = [pltpu.make_async_copy(x_hbm.at[r], xs.at[r], x_sem.at[r]) for r in range(side)]
    for r in range(side):
        g_copies[r].start()
        x_copies[r].start()
    gs[0] = jnp.zeros((rows, LANES), BF16)
    gs[side + 1] = jnp.zeros((rows, LANES), BF16)
    acc[...] = jnp.zeros(acc.shape, F32)
    edge = jnp.zeros((batch, LANES), BF16)
    ready()
    ext = ext_ref[...]
    g_copies[0].wait()

    @pl.loop(0, side)
    def _(r):
        @pl.when(r + 1 < side)
        def _():
            pltpu.make_async_copy(gs.at[r + 2], gs.at[r + 2], g_sem.at[r + 1]).wait()

        pltpu.make_async_copy(x_hbm.at[r], xs.at[r], x_sem.at[r]).wait()
        if kind == "images":
            for c in range(side):
                m = mask_at(ext, r, c).astype(BF16)
                for k in range(blocks):
                    lanes = slice(k * LANES, (k + 1) * LANES)
                    xs[r, c * batch : (c + 1) * batch, lanes] = xs[r, c * batch : (c + 1) * batch, lanes] * m
        parts = []
        for i in range(3):
            g = gs[r + 2 - i]
            parts.append(jnp.concatenate([g[batch:], edge], axis=0))
            parts.append(g)
            parts.append(jnp.concatenate([edge, g[: rows - batch]], axis=0))
        wide = jnp.concatenate(parts, axis=1)
        acc[...] += lax.dot_general(xs[r], wide, (((0,), (0,)), ((), ())), preferred_element_type=F32)

    half = TAPS * blocks // 2
    for t in range(TAPS):
        for k in range(blocks):
            place = t * blocks + k
            value = acc[k * LANES : (k + 1) * LANES, t * LANES : (t + 1) * LANES]
            at = slice(place % half * LANES, (place % half + 1) * LANES)
            kept = upper == (1 if place >= half else 0)

            @pl.when(kept)
            def _(value=value, at=at):
                keep_ref[at] = value

            @pl.when(jnp.logical_not(kept))
            def _(value=value, at=at):
                send_ref[at] = value.astype(BF16)


def weight_grad(kind, place, ext, x, gs, side, batch):
    width, pixels = x.shape[2], side * batch
    blocks = width // LANES
    splits = [g.shape[0] for g in gs]
    half = TAPS * width // 2
    return call(
        f"wgrad_{kind}",
        functools.partial(weight_grad_body, kind, side, batch, blocks, splits),
        [((half, LANES), F32, "v"), ((half, LANES), BF16, "v")],
        [(place, "s"), (ext, "v"), (x, "a")] + [(g, "a") for g in gs],
        [
            pltpu.VMEM((width, TAPS * LANES), F32),
            pltpu.VMEM((side + 2, pixels, LANES), BF16),
            pltpu.VMEM((side, pixels, width), BF16),
            DMA((side,)),
            DMA((side,)),
        ],
    )


def block_end_body(side, batch, ready, *refs):
    take = Takes(refs)
    place_ref, ext_ref, params_ref, images_hbm, cot_hbm, h_hbm = take(6)
    out_hbm, grad_hbm, sum_ref = take(3)
    own, cot, hs, outs, grads, sems = take(6)
    lanes = pl.ds(pl.multiple_of(place_ref[0] * LANES, LANES), LANES)

    def loads(r):
        return (
            pltpu.make_async_copy(images_hbm.at[r, :, lanes], own.at[r], sems.at[0, r]),
            pltpu.make_async_copy(cot_hbm.at[r], cot.at[r], sems.at[1, r]),
            pltpu.make_async_copy(h_hbm.at[r], hs.at[r], sems.at[2, r]),
        )

    def stores(r):
        return (
            pltpu.make_async_copy(outs.at[r], out_hbm.at[r], sems.at[3, r]),
            pltpu.make_async_copy(grads.at[r], grad_hbm.at[r], sems.at[4, r]),
        )

    for r in range(side):
        for copy in loads(r):
            copy.start()
    ready()
    ext = ext_ref[...]
    scale, shift, rscale, offset = (params_ref[k : k + 1] for k in range(4))
    zero = jnp.zeros((batch, LANES), F32)

    def one(r, carry):
        ds, dn = carry
        for copy in loads(r):
            copy.wait()
        for c in range(side):
            part = slice(c * batch, (c + 1) * batch)
            m = mask_at(ext, r, c)
            h = hs[r, part]
            value, slope = gelu_both(h * scale + shift + own[r, part].astype(F32) * m)
            outs[r, part] = (value * m).astype(BF16)
            dz = cot[r, part].astype(F32) * m * slope
            grads[r, part] = dz
            ds = ds + dz
            dn = dn + dz * (h * rscale + offset)
        for copy in stores(r):
            copy.start()
        return ds, dn

    ds, dn = lax.fori_loop(0, side, one, (zero, zero))
    sum_ref[...] = jnp.zeros(sum_ref.shape, F32)
    sum_ref[0:1] = jnp.sum(ds, axis=0, keepdims=True)
    sum_ref[1:2] = jnp.sum(dn, axis=0, keepdims=True)
    return [copy for r in range(side) for copy in stores(r)]


def block_end(place, ext, params, images, cotangent, h, side, batch):
    shape = (side, side * batch, LANES)
    return call(
        "block_end",
        functools.partial(block_end_body, side, batch),
        [(shape, BF16, "a"), (shape, F32, "a"), ((8, LANES), F32, "v")],
        [(place, "s"), (ext, "v"), (params, "v"), (images, "a"), (cotangent, "a"), (h, "a")],
        [pltpu.VMEM(shape, d) for d in (BF16, BF16, F32, BF16, F32)] + [DMA((5, side))],
    )


def norm_back_body(side, batch, splits, ready, *refs):
    take = Takes(refs)
    ext_ref, params_ref, sums_ref, h_hbm, dz_hbm = take(5)
    out_hbms = take(len(splits))
    hs, dzs, outs, sems = take(4)

    def loads(r):
        return (
            pltpu.make_async_copy(h_hbm.at[r], hs.at[r], sems.at[0, r]),
            pltpu.make_async_copy(dz_hbm.at[r], dzs.at[r], sems.at[1, r]),
        )

    for r in range(side):
        for copy in loads(r):
            copy.start()
    ready()
    ext = ext_ref[...]
    scale, _, rscale, offset, n = (params_ref[k : k + 1] for k in range(5))
    shift_grad, gain_grad = sums_ref[0:1] / n, sums_ref[1:2] / n
    b = scale * rscale * gain_grad
    c0 = scale * (shift_grad + offset * gain_grad)
    waits, at = [], 0
    for out_hbm, size in zip(out_hbms, splits):

        @pl.loop(at, at + size)
        def _(r, out_hbm=out_hbm, at=at):
            for copy in loads(r):
                copy.wait()
            for c in range(side):
                part = slice(c * batch, (c + 1) * batch)
                m = mask_at(ext, r, c)
                outs[r, part] = (m * (scale * dzs[r, part] - (hs[r, part] * b + c0))).astype(BF16)
            pltpu.make_async_copy(outs.at[r], out_hbm.at[r - at], sems.at[2, r]).start()

        waits += [(out_hbm, r, r - at) for r in range(at, at + size)]
        at += size
    return [pltpu.make_async_copy(outs.at[r], out_hbm.at[k], sems.at[2, r]) for out_hbm, r, k in waits]


def norm_back(ext, params, sums, h, dz, splits, side, batch):
    pixels = side * batch
    shape = (side, pixels, LANES)
    return call(
        "norm_back",
        functools.partial(norm_back_body, side, batch, tuple(splits)),
        [((n, pixels, LANES), BF16, "a") for n in splits],
        [(ext, "v"), (params, "v"), (sums, "v"), (h, "a"), (dz, "a")],
        [pltpu.VMEM(shape, d) for d in (F32, F32, BF16)] + [DMA((3, side))],
    )


def as_rows(values):
    row = lax.broadcasted_iota(jnp.int32, (8, LANES), 0)
    out = jnp.zeros((8, LANES), F32)
    for k, value in enumerate(values):
        out = jnp.where(row == k, value, out)
    return out


def merge(a, b):
    merged = merge_rows(*(a[k : k + 1] for k in range(3)), *(b[k : k + 1] for k in range(3)))
    return as_rows(list(merged) + [a[k : k + 1] for k in range(3, 6)])


def affine(a, gain, shift):
    center, n = a[0:1], a[2:3]
    rscale = lax.rsqrt(a[1:2] / n + EPSILON)
    scale = rscale * gain
    rows = [scale, shift - center * scale, rscale, -center * rscale, n]
    return as_rows(rows + [(a[3 + q : 4 + q] - center) * scale + shift for q in range(3)])


def swap(x, axis, size, k):
    return lax.ppermute(x, axis, [(i, i ^ k) for i in range(size)])


def after(x, *others):
    return lax.optimization_barrier((x,) + others)[0]


def sum_over(x, axis, size):
    k = 1
    while k < size:
        x = x + swap(x, axis, size, k)
        k *= 2
    return x


def layer_params(stat, gain, shift, size, ties):
    gain, shift = gain.reshape(1, LANES), shift.reshape(1, LANES)
    k, step = 1, 0
    while k < size:
        if step in ties:
            stat = after(stat, *ties[step])
        stat = merge(stat, swap(stat, "dp", size, k))
        k *= 2
        step += 1
    return affine(stat, gain, shift)


def gather_blocks(x, size):
    far = swap(x, "chan", size, 2)
    near = swap(x, "chan", size, 1)
    return [x, near, far, swap(far, "chan", size, 1)]


def scatter_grad(keep, send, size, index, ties):
    k, step = 1, 0
    while k < size:
        if step in ties:
            send = after(send, ties[step])
        step += 1
        current = keep + swap(send, "dp", size, k).astype(F32)
        k *= 2
        if k >= size:
            return current
        half = current.shape[0] // 2
        low, high = current[:half], current[half:]
        upper = (index // k) % 2 == 1
        keep = jnp.where(upper, high, low)
        send = jnp.where(upper, low, high).astype(BF16)
    return None


def gather_grad(part, size, index, last=None):
    current = part.astype(BF16)
    k = size
    while k > 1:
        k //= 2
        if k == 1 and last is not None:
            current = after(current, last)
        other = swap(current, "dp", size, k)
        upper = (index // k) % 2 == 1
        current = jnp.where(upper, jnp.concatenate([other, current]), jnp.concatenate([current, other]))
    return current.astype(F32)


def shards(
    dp, ch, images, groups, cotangent, weight_one, gain_one, shift_one, weight_two, gain_two, shift_two, moment_one, moment_two
):
    batch, side, _, width = images.shape
    pixels = side * batch
    images = jnp.transpose(images, (1, 2, 0, 3)).reshape(side, pixels, width)
    cotangent = jnp.transpose(cotangent, (1, 2, 0, 3)).reshape(side, pixels, LANES)
    chan, index = lax.axis_index("chan").astype(jnp.int32), lax.axis_index("dp").astype(jnp.int32)
    place = jnp.stack([chan, index % 2])
    ext = jnp.broadcast_to((5 + 2 * groups)[:, None], (batch, LANES))
    third = side // 3
    conv_in = (third + 1, third, side - 2 * third - 1)
    flow = (third, third, side - 2 * third)
    sizes = (side, batch)

    low, h_one, carry, stat, weights, r0 = [], None, None, None, weight_one, 0
    for q, count in enumerate(conv_in):
        out = conv_forward("images", q, r0, count, *sizes, place, ext, weights, [images], None, carry, stat, [h_one])
        h_one, stat, chunk = out[:3]
        if q == 0:
            weights = out[3]
        carry = out[-1]
        low.append(gather_blocks(chunk, ch))
        r0 += count
    wb_two, wt, squares = prep(weight_one, weight_two, place)
    params_one = layer_params(stat, gain_one, shift_one, dp, {0: (low[0][2],), 2: (low[1][2],)})
    near = swap(params_one, "chan", ch, 1)
    params = [params_one, near, swap(params_one, "chan", ch, 2), swap(near, "chan", ch, 2)]

    h_two = act = carry = stat = None
    r0 = 0
    for q, count in enumerate(flow):
        out = conv_forward("blocks", q, r0, count, *sizes, place, ext, wb_two, low[q], params, carry, stat, [h_two, act])
        h_two, stat, act = out[:3]
        carry = out[-1]
        r0 += count
    params_two = layer_params(stat, gain_two, shift_two, dp, {})

    wt = after(wt, stat)
    wt = [wt[0]] + [swap(wt[k], "chan", ch, k) for k in range(1, ch)]
    wt_one = jnp.concatenate([w[0] for w in wt])
    wt_two = jnp.concatenate([w[1] for w in wt])

    block_output, grad_pre, sums = block_end(place, ext, params_two, images, cotangent, h_two, *sizes)
    sums_two = sum_over(sums, "dp", dp)
    grad_two = norm_back(ext, params_two, sums_two, h_two, grad_pre, flow, *sizes)
    gathered = [gather_blocks(g, ch) for g in grad_two]
    grad_own = after(grad_two, gathered[0][2])
    keep_two, send_two = weight_grad("act", place, ext, act, grad_own, *sizes)
    dz_one = carry = sums = None
    r0 = 0
    for q, count in enumerate(flow):
        out = conv_back(
            "active", r0, count, *sizes, ext, wt_two, gathered[q], h_one, params_one, carry, sums, dz_one
        )
        dz_one, sums = out[:2]
        carry = out[-1]
        r0 += count
    part_two = scatter_grad(keep_two, send_two, dp, index, {})
    sums_one = sum_over(sums, "dp", dp)
    grad_one = norm_back(ext, params_one, sums_one, h_one, dz_one, flow, *sizes)
    gathered = [gather_blocks(g, ch) for g in grad_one]
    keep_one, send_one = weight_grad("images", place, ext, images, grad_one, *sizes)
    input_grad = carry = None
    r0 = 0
    carries = []
    for q, count in enumerate(flow):
        out = conv_back("input", r0, count, *sizes, ext, wt_one, gathered[q], grad_pre, None, carry, None, input_grad)
        input_grad = out[0]
        carry = out[-1]
        carries.append(carry)
        r0 += count
    part_one = scatter_grad(keep_one, send_one, dp, index, {1: carries[0], 2: carries[1]})
    squares = jnp.sum(squares, axis=1)
    own = jnp.stack([squares[0] / dp, squares[1] / dp, jnp.sum(part_one * part_one), jnp.sum(part_two * part_two)])
    norms = jnp.sqrt(sum_over(sum_over(own, "dp", dp), "chan", ch))
    weight_norms, grad_norms = norms[:2], norms[2:]
    trust = TRUST_COEF * weight_norms / (grad_norms + DECAY * weight_norms)
    weight_two_grad = gather_grad(part_two, dp, index).reshape(weight_two.shape)
    weight_one_grad = gather_grad(part_one, dp, index, input_grad).reshape(weight_one.shape)
    moment_one_new = MOMENTUM * moment_one + LEARN_RATE * trust[0] * (weight_one_grad + DECAY * weight_one)
    moment_two_new = MOMENTUM * moment_two + LEARN_RATE * trust[1] * (weight_two_grad + DECAY * weight_two)

    def as_images(x):
        return jnp.transpose(x.reshape(side, side, batch, LANES), (2, 0, 1, 3))

    return (
        as_images(block_output),
        as_images(input_grad),
        weight_one_grad,
        sums_one[1],
        sums_one[0],
        weight_two_grad,
        sums_two[1],
        sums_two[0],
        moment_one_new,
        moment_two_new,
        weight_norms,
        grad_norms,
    )


def solution(mesh):
    full, rows, both = P("dp", None, None, None), P("dp"), P("dp", None, None, "chan")
    weight, channel = P(None, None, "chan"), P("chan")
    return jax.shard_map(
        functools.partial(shards, mesh.shape["dp"], mesh.shape["chan"]),
        mesh=mesh,
        in_specs=(full, rows, both, weight, channel, channel, weight, channel, channel, weight, weight),
        out_specs=(both, both, weight, channel, channel, weight, channel, channel, weight, weight, P(), P()),
        check_vma=False,
    )
```

```python
import functools

import jax
import jax.numpy as jnp
from jax import lax
from jax.experimental import pallas as pl
from jax.experimental.pallas import tpu as pltpu
from jax.sharding import PartitionSpec as P

EPSILON = 1e-05
MOMENTUM = 0.9
LEARN_RATE = 8.0
TRUST_COEF = 0.001
DECAY = 5e-05
GELU_A = 0.7978845608028654
GELU_B = 0.7978845608028654 * 0.044715
F32 = jnp.float32
BF16 = jnp.bfloat16
LANES = 128
TAPS = 9
PAIRS = ((0, 2), (2, 4), (4, 6), (6, 8), (8, 9))
VMEM_BYTES = 12 * 1024 * 1024
DMA = pltpu.SemaphoreType.DMA


def mask_at(ext, r, c):
    if isinstance(r, int) and max(r, c) < 5:
        return None
    return jnp.where(ext > jnp.maximum(r, c), 1.0, 0.0).astype(F32)


def times(x, m):
    return x if m is None else x * m


def gelu(v):
    t = jnp.tanh(v * (GELU_A + GELU_B * (v * v)))
    half = 0.5 * v
    return half + half * t


def gelu_both(v):
    sq = v * v
    t = jnp.tanh(v * (GELU_A + GELU_B * sq))
    half = 0.5 * v
    value = half + half * t
    slope = 0.5 + 0.5 * t + (half - half * (t * t)) * (GELU_A + (3.0 * GELU_B) * sq)
    return value, slope


def call(name, body, outs, ins, scratch=()):
    spec = {
        "v": pl.BlockSpec(memory_space=pltpu.VMEM),
        "h": pl.BlockSpec(memory_space=pltpu.HBM),
        "s": pl.BlockSpec(memory_space=pltpu.SMEM),
    }
    return pl.pallas_call(
        body,
        name=name,
        out_shape=[jax.ShapeDtypeStruct(s, d) for s, d, _ in outs],
        in_specs=[spec[w] for _, w in ins],
        out_specs=[spec[w] for _, _, w in outs],
        scratch_shapes=list(scratch),
        compiler_params=pltpu.CompilerParams(vmem_limit_bytes=VMEM_BYTES),
        cost_estimate=pl.CostEstimate(flops=0, bytes_accessed=0, transcendentals=0),
    )(*[x for x, _ in ins])


def segments(*splits):
    ends = sorted({sum(s[: k + 1]) for s in splits for k in range(len(s))})
    result, start = [], 0
    for end in ends:
        result.append((start, end, [row_place(s, start) for s in splits]))
        start = end
    return result


def row_place(split, r):
    at = 0
    for index, size in enumerate(split):
        if r < at + size:
            return index, at
        at += size


class Takes:
    def __init__(self, refs):
        self.refs = list(refs)

    def __call__(self, n=None):
        if n is None:
            return self.refs.pop(0)
        return [self.refs.pop(0) for _ in range(n)]


def prep_body(blocks, chan_ref, one_ref, two_ref, wb_ref, wt_ref, sq_ref):
    chan = chan_ref[0]
    sq_ref[...] = jnp.zeros(sq_ref.shape, F32)
    for layer, w_ref in enumerate((one_ref, two_ref)):
        total = jnp.zeros((1, LANES), F32)
        for k in range(blocks):
            rows = pl.ds(pl.multiple_of(jnp.bitwise_xor(chan, k) * LANES, LANES), LANES)
            for t in range(TAPS):
                piece = w_ref[t, rows, :]
                total = total + jnp.sum(piece * piece, axis=0, keepdims=True)
                if layer:
                    wb_ref[k * LANES : (k + 1) * LANES, t * LANES : (t + 1) * LANES] = piece.astype(BF16)
                flip = TAPS - 1 - t
                wt_ref[k, layer, :, flip * LANES : (flip + 1) * LANES] = piece.T.astype(BF16)
        sq_ref[layer : layer + 1] = total


def prep(weight_one, weight_two, chan):
    width = weight_one.shape[1]
    blocks = width // LANES
    return call(
        "prep",
        functools.partial(prep_body, blocks),
        [
            ((width, TAPS * LANES), BF16, "v"),
            ((blocks, 2, LANES, TAPS * LANES), BF16, "v"),
            ((8, LANES), F32, "v"),
        ],
        [(chan, "s"), (weight_one, "v"), (weight_two, "v")],
    )


def add_row(lhs_ref, w_ref, acc, slot, batch):
    rows = lhs_ref.shape[0]
    for a, b in PAIRS:
        y = jnp.dot(lhs_ref[...], w_ref[:, a * LANES : b * LANES], preferred_element_type=F32)
        for t in range(a, b):
            i, j = divmod(t, 3)
            z = y[:, (t - a) * LANES : (t - a + 1) * LANES]
            at = slot + 2 - i
            if j == 0:
                acc[at, batch:] += z[: rows - batch]
            elif j == 1:
                acc[at] += z
            else:
                acc[at, : rows - batch] += z[batch:]


def start_acc(acc, carry_ref):
    for slot in range(acc.shape[0]):
        if carry_ref is not None and slot < 2:
            acc[slot] = carry_ref[slot]
        else:
            acc[slot] = jnp.zeros(acc.shape[1:], F32)


def emitted(r0, count, side):
    first = 0 if r0 == 0 else r0 - 1
    last = side if r0 + count == side else r0 + count - 1
    return first, last, first - (r0 - 1)


def ready_rows(t, r0, count, side):
    r = r0 + t
    rows = [r - 1] if r > 0 else []
    return rows + [r] if r == side - 1 else rows


class Stats:
    def __init__(self, ext, side, batch):
        self.ext, self.side, self.batch = ext, side, batch
        self.ref = None
        zero = jnp.zeros((batch, LANES), F32)
        self.s1, self.s2, self.n = zero, zero, zero

    def row(self, acc, slot, r, low_ref=None):
        batch = self.batch
        if self.ref is None:
            s = n = jnp.zeros((batch, LANES), F32)
            for c in range(self.side):
                m = mask_at(self.ext, r, c)
                s = s + times(acc[slot, c * batch : (c + 1) * batch], m)
                n = n + (1.0 if m is None else m)
            n = jnp.sum(n, axis=0, keepdims=True)
            self.ref = jnp.sum(s, axis=0, keepdims=True) / jnp.maximum(n, 1.0)
        for c in range(self.side):
            m = mask_at(self.ext, r, c)
            d = acc[slot, c * batch : (c + 1) * batch] - self.ref
            if low_ref is not None:
                low_ref[c * batch : (c + 1) * batch] = d.astype(BF16)
            masked = times(d, m)
            self.s1 = self.s1 + masked
            self.s2 = self.s2 + masked * d
            self.n = self.n + (1.0 if m is None else m)

    def store(self, stat_ref, prev_ref, chunk):
        s1, s2, n = (jnp.sum(x, axis=0, keepdims=True) for x in (self.s1, self.s2, self.n))
        safe = jnp.maximum(n, 1.0)
        whole = (self.ref + s1 / safe, s2 - s1 * s1 / safe, n)
        stat_ref[...] = jnp.zeros(stat_ref.shape, F32) if prev_ref is None else prev_ref[...]
        if prev_ref is not None:
            whole = merge_rows(*(prev_ref[k : k + 1] for k in range(3)), *whole)
        for k in range(3):
            stat_ref[k : k + 1] = whole[k]
        stat_ref[3 + chunk : 4 + chunk] = self.ref


def merge_rows(mean_a, m2_a, n_a, mean_b, m2_b, n_b):
    n = n_a + n_b
    safe = jnp.maximum(n, 1.0)
    delta = mean_a - mean_b
    mean = (n_a * mean_a + n_b * mean_b) / safe
    return mean, m2_a + m2_b + delta * delta * (n_a * n_b / safe), n


def conv_images_body(chunk, r0, count, side, batch, blocks, *refs):
    take = Takes(refs)
    ext_ref, w_in, x_hbm = take(3)
    carry_ref, prev_ref = take(2) if r0 else (None, None)
    h_ref, stat_ref, low_ref = take(3)
    w_ref = take() if r0 == 0 else w_in
    carry_out = None if r0 + count == side else take()
    acc, raw, x_sem = take(3)
    lhs = take(count)
    fetches = [pltpu.make_async_copy(x_hbm.at[r0 + t], raw.at[t], x_sem.at[t]) for t in range(count)]
    fetches[0].start()
    if r0 == 0:
        w_raw, w_sem = take(2)
        taps = [pltpu.make_async_copy(w_in.at[t], w_raw.at[t], w_sem.at[t]) for t in range(TAPS)]
        for copy in taps:
            copy.start()
    for copy in fetches[1:]:
        copy.start()
    ext = ext_ref[...]
    start_acc(acc, carry_ref)
    if r0 == 0:
        for t in range(TAPS):
            taps[t].wait()
            w_ref[:, t * LANES : (t + 1) * LANES] = w_raw[t].astype(BF16)

    def stage(t):
        fetches[t].wait()
        for c in range(side):
            part = slice(c * batch, (c + 1) * batch)
            m = mask_at(ext, r0 + t, c)
            for k in range(blocks):
                lanes = slice(k * LANES, (k + 1) * LANES)
                x = raw[t, part, lanes]
                lhs[t][part, lanes] = x if m is None else x * m.astype(BF16)

    first, last, _ = emitted(r0, count, side)
    stats = Stats(ext, side, batch)
    stage(0)
    for t in range(count):
        if t + 1 < count:
            stage(t + 1)
        add_row(lhs[t], w_ref, acc, t, batch)
        for r in ready_rows(t, r0, count, side):
            h_ref[r - first] = acc[r - (r0 - 1)]
            stats.row(acc, r - (r0 - 1), r, low_ref.at[r - first])
    stats.store(stat_ref, prev_ref, chunk)
    if carry_out is not None:
        carry_out[0] = acc[count]
        carry_out[1] = acc[count + 1]


def conv_images(chunk, r0, count, side, batch, ext, weights, images, carry, prev):
    pixels, width = side * batch, images.shape[2]
    first, last, _ = emitted(r0, count, side)
    rows = last - first
    ins = [(ext, "v"), (weights, "v" if r0 else "h"), (images, "h")]
    if r0:
        ins += [(carry, "v"), (prev, "v")]
    outs = [((rows, pixels, LANES), F32, "v"), ((8, LANES), F32, "v"), ((rows, pixels, LANES), BF16, "v")]
    if r0 == 0:
        outs.append(((width, TAPS * LANES), BF16, "v"))
    if r0 + count != side:
        outs.append(((2, pixels, LANES), F32, "v"))
    scratch = [pltpu.VMEM((count + 2, pixels, LANES), F32), pltpu.VMEM((count, pixels, width), BF16), DMA((count,))]
    scratch += [pltpu.VMEM((pixels, width), BF16) for _ in range(count)]
    if r0 == 0:
        scratch += [pltpu.VMEM((TAPS, width, LANES), F32), DMA((TAPS,))]
    return call(
        f"conv_one_{r0}",
        functools.partial(conv_images_body, chunk, r0, count, side, batch, width // LANES),
        outs,
        ins,
        scratch,
    )


def conv_active_body(chunk, r0, count, side, batch, blocks, *refs):
    take = Takes(refs)
    place_ref, ext_ref, w_ref = take(3)
    sources, params = take(blocks), take(blocks)
    carry_ref, prev_ref = take(2) if r0 else (None, None)
    h_ref, stat_ref, act_ref = take(3)
    carry_out = None if r0 + count == side else take()
    acc = take()
    lhs = take(count)
    ext = ext_ref[...]
    start_acc(acc, carry_ref)

    def stage(t):
        for k in range(blocks):
            scale, shift = params[k][0:1], params[k][5 + chunk : 6 + chunk]
            for c in range(side):
                part = slice(c * batch, (c + 1) * batch)
                z = sources[k][t, part].astype(F32) * scale + shift
                low = times(gelu(z), mask_at(ext, r0 + t, c)).astype(BF16)
                lhs[t][part, k * LANES : (k + 1) * LANES] = low
                act_ref[t, part, k * LANES : (k + 1) * LANES] = low

    first, last, _ = emitted(r0, count, side)
    stats = Stats(ext, side, batch)
    stage(0)
    for t in range(count):
        if t + 1 < count:
            stage(t + 1)
        add_row(lhs[t], w_ref, acc, t, batch)
        for r in ready_rows(t, r0, count, side):
            h_ref[r - first] = acc[r - (r0 - 1)]
            stats.row(acc, r - (r0 - 1), r)
    stats.store(stat_ref, prev_ref, chunk)
    if carry_out is not None:
        carry_out[0] = acc[count]
        carry_out[1] = acc[count + 1]


def conv_active(chunk, r0, count, side, batch, place, ext, weights, sources, params, carry, prev):
    blocks, pixels = len(sources), side * batch
    width = LANES * blocks
    first, last, _ = emitted(r0, count, side)
    ins = [(place, "s"), (ext, "v"), (weights, "v")] + [(x, "v") for x in sources] + [(p, "v") for p in params]
    if r0:
        ins += [(carry, "v"), (prev, "v")]
    outs = [((last - first, pixels, LANES), F32, "v"), ((8, LANES), F32, "v"), ((count, pixels, width), BF16, "v")]
    if r0 + count != side:
        outs.append(((2, pixels, LANES), F32, "v"))
    scratch = [pltpu.VMEM((count + 2, pixels, LANES), F32)]
    scratch += [pltpu.VMEM((pixels, width), BF16) for _ in range(count)]
    return call(
        f"conv_two_{r0}",
        functools.partial(conv_active_body, chunk, r0, count, side, batch, blocks),
        outs,
        ins,
        scratch,
    )


def conv_back_body(kind, r0, count, side, batch, blocks, h_split, *refs):
    take = Takes(refs)
    ext_ref, w_ref = take(2)
    sources = take(blocks)
    first, last, _ = emitted(r0, count, side)
    active = kind == "active"
    carry_ref = prev_ref = params_ref = None
    if active:
        params_ref = take()
        h_used = sorted({row_place(h_split, r)[0] for r in range(first, last)})
        h_refs = dict(zip(h_used, take(len(h_used))))
    else:
        extra = take()
    if r0:
        carry_ref = take()
        prev_ref = take() if active else None
    out_ref = take()
    sum_ref = take() if active else None
    carry_out = None if r0 + count == side else take()
    acc = take()
    lhs = take(count)
    ext = ext_ref[...]
    start_acc(acc, carry_ref)
    zero = jnp.zeros((batch, LANES), F32)
    total = [zero, zero]
    if active:
        scale, shift, rscale, offset = (params_ref[k : k + 1] for k in range(4))

    def stage(t):
        for k in range(blocks):
            lhs[t][:, k * LANES : (k + 1) * LANES] = sources[k][t]

    def finish(t):
        for r in ready_rows(t, r0, count, side):
            slot, k = r - (r0 - 1), r - first
            for c in range(side):
                part = slice(c * batch, (c + 1) * batch)
                m = mask_at(ext, r, c)
                if active:
                    index, base = row_place(h_split, r)
                    h = h_refs[index][r - base, part]
                    _, slope = gelu_both(h * scale + shift)
                    dz = times(acc[slot, part], m) * slope
                    out_ref[k, part] = dz
                    total[0] = total[0] + dz
                    total[1] = total[1] + dz * (h * rscale + offset)
                else:
                    out_ref[k, part] = times(extra[k, part] + acc[slot, part], m)

    stage(0)
    for t in range(count):
        if t + 1 < count:
            stage(t + 1)
        add_row(lhs[t], w_ref, acc, t, batch)
        finish(t)
    if carry_out is not None:
        carry_out[0] = acc[count]
        carry_out[1] = acc[count + 1]
    if active:
        sum_ref[...] = jnp.zeros(sum_ref.shape, F32)
        for k in range(2):
            s = jnp.sum(total[k], axis=0, keepdims=True)
            sum_ref[k : k + 1] = s if prev_ref is None else s + prev_ref[k : k + 1]


def conv_back(kind, r0, count, side, batch, ext, weights, sources, extra, params, carry, prev):
    blocks, pixels = len(sources), side * batch
    first, last, _ = emitted(r0, count, side)
    rows = last - first
    active = kind == "active"
    ins = [(ext, "v"), (weights, "v")] + [(x, "v") for x in sources]
    h_split = None
    if active:
        h_split = [h.shape[0] for h in extra]
        ins.append((params, "v"))
        ins += [(extra[k], "v") for k in sorted({row_place(h_split, r)[0] for r in range(first, last)})]
    else:
        ins.append((extra, "v"))
    if r0:
        ins.append((carry, "v"))
        if active:
            ins.append((prev, "v"))
    outs = [((rows, pixels, LANES), F32, "v")]
    if active:
        outs.append(((8, LANES), F32, "v"))
    if r0 + count != side:
        outs.append(((2, pixels, LANES), F32, "v"))
    scratch = [pltpu.VMEM((count + 2, pixels, LANES), F32)]
    scratch += [pltpu.VMEM((pixels, blocks * LANES), BF16) for _ in range(count)]
    return call(
        f"back_{kind}_{r0}",
        functools.partial(conv_back_body, kind, r0, count, side, batch, blocks, h_split),
        outs,
        ins,
        scratch,
    )


def weight_grad_body(kind, side, batch, blocks, splits, *refs):
    take = Takes(refs)
    place_ref, ext_ref = take(2)
    x_refs, g_refs = take(len(splits[0])), take(len(splits[1]))
    keep_ref, send_ref, acc, gs, masked = take(5)
    upper = place_ref[1]
    rows = side * batch
    ext = ext_ref[...]
    gs[0] = jnp.zeros((rows, LANES), BF16)
    gs[side + 1] = jnp.zeros((rows, LANES), BF16)
    for r in range(side):
        index, base = row_place(splits[1], r)
        gs[r + 1] = g_refs[index][r - base]
    acc[...] = jnp.zeros(acc.shape, F32)
    edge = jnp.zeros((batch, LANES), BF16)
    for start, stop, ((xi, xb),) in segments(splits[0]):

        @pl.loop(start, stop)
        def _(r, xi=xi, xb=xb):
            if kind == "images":
                for c in range(side):
                    part = slice(c * batch, (c + 1) * batch)
                    m = mask_at(ext, r, c).astype(BF16)
                    for k in range(blocks):
                        lanes = slice(k * LANES, (k + 1) * LANES)
                        masked[part, lanes] = x_refs[xi][r - xb, part, lanes] * m
                x = masked[...]
            else:
                x = x_refs[xi][r - xb]
            parts = []
            for i in range(3):
                g = gs[r + 2 - i]
                parts.append(jnp.concatenate([g[batch:], edge], axis=0))
                parts.append(g)
                parts.append(jnp.concatenate([edge, g[: rows - batch]], axis=0))
            wide = jnp.concatenate(parts, axis=1)
            acc[...] += lax.dot_general(x, wide, (((0,), (0,)), ((), ())), preferred_element_type=F32)

    half = TAPS * blocks // 2
    for t in range(TAPS):
        for k in range(blocks):
            place = t * blocks + k
            lanes = slice(t * LANES, (t + 1) * LANES)
            if kind == "images":
                value = acc[k * LANES : (k + 1) * LANES, lanes]
            else:
                other = jnp.bitwise_xor(place_ref[0], k)
                value = acc[pl.ds(pl.multiple_of(other * LANES, LANES), LANES), lanes]
            at = slice(place % half * LANES, (place % half + 1) * LANES)
            kept = upper == (1 if place >= half else 0)

            @pl.when(kept)
            def _(value=value, at=at):
                keep_ref[at] = value

            @pl.when(jnp.logical_not(kept))
            def _(value=value, at=at):
                send_ref[at] = value.astype(BF16)


def weight_grad(kind, place, ext, xs, gs, side, batch):
    width, pixels = xs[0].shape[2], side * batch
    blocks = width // LANES
    splits = ([x.shape[0] for x in xs], [g.shape[0] for g in gs])
    half = TAPS * width // 2
    return call(
        f"wgrad_{kind}",
        functools.partial(weight_grad_body, kind, side, batch, blocks, splits),
        [((half, LANES), F32, "v"), ((half, LANES), BF16, "v")],
        [(place, "s"), (ext, "v")] + [(x, "v") for x in xs] + [(g, "v") for g in gs],
        [
            pltpu.VMEM((width, TAPS * LANES), F32),
            pltpu.VMEM((side + 2, pixels, LANES), BF16),
            pltpu.VMEM((pixels, width), BF16),
        ],
    )


def block_end_body(side, batch, split, *refs):
    take = Takes(refs)
    place_ref, ext_ref, params_ref, images_ref, cot_ref = take(5)
    h_refs = take(len(split))
    out_hbm = take()
    grad_refs = take(len(split))
    sum_ref, outs, sems = take(3)
    lanes = pl.ds(pl.multiple_of(place_ref[0] * LANES, LANES), LANES)
    ext = ext_ref[...]
    scale, shift, rscale, offset = (params_ref[k : k + 1] for k in range(4))
    zero = jnp.zeros((batch, LANES), F32)
    total = (zero, zero)

    def store(r):
        return pltpu.make_async_copy(outs.at[r], out_hbm.at[r], sems.at[r])

    for start, stop, ((index, base),) in segments(split):

        def one(r, carry, index=index, base=base):
            ds, dn = carry
            for c in range(side):
                part = slice(c * batch, (c + 1) * batch)
                m = mask_at(ext, r, c)
                h = h_refs[index][r - base, part]
                value, slope = gelu_both(h * scale + shift + images_ref[r, part, lanes].astype(F32) * m)
                outs[r, part] = (value * m).astype(BF16)
                dz = cot_ref[r, part].astype(F32) * m * slope
                grad_refs[index][r - base, part] = dz
                ds = ds + dz
                dn = dn + dz * (h * rscale + offset)
            store(r).start()
            return ds, dn

        total = lax.fori_loop(start, stop, one, total)
    sum_ref[...] = jnp.zeros(sum_ref.shape, F32)
    sum_ref[0:1] = jnp.sum(total[0], axis=0, keepdims=True)
    sum_ref[1:2] = jnp.sum(total[1], axis=0, keepdims=True)
    for r in range(side):
        store(r).wait()


def block_end(place, ext, params, images, cotangent, hs, side, batch):
    pixels = side * batch
    shape = (side, pixels, LANES)
    split = [h.shape[0] for h in hs]
    outs = [(shape, BF16, "h")] + [((n, pixels, LANES), F32, "v") for n in split] + [((8, LANES), F32, "v")]
    return call(
        "block_end",
        functools.partial(block_end_body, side, batch, split),
        outs,
        [(place, "s"), (ext, "v"), (params, "v"), (images, "v"), (cotangent, "v")] + [(h, "v") for h in hs],
        [pltpu.VMEM(shape, BF16), DMA((side,))],
    )


def norm_back_body(side, batch, splits, *refs):
    take = Takes(refs)
    ext_ref, params_ref, sums_ref = take(3)
    h_refs, dz_refs, out_refs = (take(len(s)) for s in splits)
    ext = ext_ref[...]
    scale, _, rscale, offset, n = (params_ref[k : k + 1] for k in range(5))
    shift_grad, gain_grad = sums_ref[0:1] / n, sums_ref[1:2] / n
    b = scale * rscale * gain_grad
    c0 = scale * (shift_grad + offset * gain_grad)
    for start, stop, ((hi, hb), (zi, zb), (oi, ob)) in segments(*splits):

        @pl.loop(start, stop)
        def _(r, hi=hi, hb=hb, zi=zi, zb=zb, oi=oi, ob=ob):
            for c in range(side):
                part = slice(c * batch, (c + 1) * batch)
                m = mask_at(ext, r, c)
                grad = scale * dz_refs[zi][r - zb, part] - (h_refs[hi][r - hb, part] * b + c0)
                out_refs[oi][r - ob, part] = (m * grad).astype(BF16)


def norm_back(ext, params, sums, hs, dzs, flow, side, batch):
    splits = ([h.shape[0] for h in hs], [z.shape[0] for z in dzs], list(flow))
    return call(
        "norm_back",
        functools.partial(norm_back_body, side, batch, splits),
        [((n, side * batch, LANES), BF16, "v") for n in flow],
        [(ext, "v"), (params, "v"), (sums, "v")] + [(x, "v") for x in list(hs) + list(dzs)],
    )


def as_rows(values):
    row = lax.broadcasted_iota(jnp.int32, (8, LANES), 0)
    out = jnp.zeros((8, LANES), F32)
    for k, value in enumerate(values):
        out = jnp.where(row == k, value, out)
    return out


def merge(a, b):
    merged = merge_rows(*(a[k : k + 1] for k in range(3)), *(b[k : k + 1] for k in range(3)))
    return as_rows(list(merged) + [a[k : k + 1] for k in range(3, 6)])


def affine(a, gain, shift):
    center, n = a[0:1], a[2:3]
    rscale = lax.rsqrt(a[1:2] / n + EPSILON)
    scale = rscale * gain
    rows = [scale, shift - center * scale, rscale, -center * rscale, n]
    return as_rows(rows + [(a[3 + q : 4 + q] - center) * scale + shift for q in range(3)])


def swap(x, axis, size, k):
    return lax.ppermute(x, axis, [(i, i ^ k) for i in range(size)])


def after(x, *others):
    return lax.optimization_barrier((x,) + others)[0]


def sum_over(x, axis, size):
    k = 1
    while k < size:
        x = x + swap(x, axis, size, k)
        k *= 2
    return x


def layer_params(stat, gain, shift, size, ties):
    gain, shift = gain.reshape(1, LANES), shift.reshape(1, LANES)
    k, step = 1, 0
    while k < size:
        if step in ties:
            stat = after(stat, *ties[step])
        stat = merge(stat, swap(stat, "dp", size, k))
        k *= 2
        step += 1
    return affine(stat, gain, shift)


def gather_blocks(x, size):
    far = swap(x, "chan", size, 2)
    near = swap(x, "chan", size, 1)
    return [x, near, far, swap(far, "chan", size, 1)]


def scatter_grad(keep, send, size, index, ties):
    k, step = 1, 0
    while k < size:
        if step in ties:
            send = after(send, ties[step])
        step += 1
        current = keep + swap(send, "dp", size, k).astype(F32)
        k *= 2
        if k >= size:
            return current
        half = current.shape[0] // 2
        low, high = current[:half], current[half:]
        upper = (index // k) % 2 == 1
        keep = jnp.where(upper, high, low)
        send = jnp.where(upper, low, high).astype(BF16)
    return None


def gather_grad(part, size, index, last=None):
    current = part.astype(BF16)
    k = size
    while k > 1:
        k //= 2
        if k == 1 and last is not None:
            current = after(current, last)
        other = swap(current, "dp", size, k)
        upper = (index // k) % 2 == 1
        current = jnp.where(upper, jnp.concatenate([other, current]), jnp.concatenate([current, other]))
    return current.astype(F32)


def shards(
    dp, ch, images, groups, cotangent, weight_one, gain_one, shift_one, weight_two, gain_two, shift_two, moment_one, moment_two
):
    batch, side, _, width = images.shape
    pixels = side * batch
    images = jnp.transpose(images, (1, 2, 0, 3)).reshape(side, pixels, width)
    cotangent = jnp.transpose(cotangent, (1, 2, 0, 3)).reshape(side, pixels, LANES)
    chan, index = lax.axis_index("chan").astype(jnp.int32), lax.axis_index("dp").astype(jnp.int32)
    place = jnp.stack([chan, index % 2])
    ext = jnp.broadcast_to((5 + 2 * groups)[:, None], (batch, LANES))
    third = side // 3
    conv_in = (third + 1, third, side - 2 * third - 1)
    flow = (third, third, side - 2 * third)
    sizes = (side, batch)

    low, h_one, carry, stat, weights, r0 = [], [], None, None, weight_one, 0
    for q, count in enumerate(conv_in):
        out = conv_images(q, r0, count, *sizes, ext, weights, images, carry, stat)
        h, stat, chunk = out[:3]
        if q == 0:
            weights = out[3]
        carry = out[-1]
        h_one.append(h)
        low.append(gather_blocks(chunk, ch))
        r0 += count
    wb_two, wt, squares = prep(weight_one, weight_two, place)
    params_one = layer_params(stat, gain_one, shift_one, dp, {0: (low[0][2],), 2: (low[1][2],)})
    near = swap(params_one, "chan", ch, 1)
    params = [params_one, near, swap(params_one, "chan", ch, 2), swap(near, "chan", ch, 2)]

    h_two, act, carry, stat, r0 = [], [], None, None, 0
    for q, count in enumerate(flow):
        out = conv_active(q, r0, count, *sizes, place, ext, wb_two, low[q], params, carry, stat)
        h, stat, rows = out[:3]
        h_two.append(h)
        act.append(rows)
        carry = out[-1]
        r0 += count
    params_two = layer_params(stat, gain_two, shift_two, dp, {})

    wt = after(wt, stat)
    wt = [wt[0]] + [swap(wt[k], "chan", ch, k) for k in range(1, ch)]
    wt_one = jnp.concatenate([w[0] for w in wt])
    wt_two = jnp.concatenate([w[1] for w in wt])

    out = block_end(place, ext, params_two, images, cotangent, h_two, *sizes)
    block_output, grad_pre, sums = out[0], out[1:-1], out[-1]
    sums_two = sum_over(sums, "dp", dp)
    grad_two = norm_back(ext, params_two, sums_two, h_two, grad_pre, flow, *sizes)
    gathered = [gather_blocks(g, ch) for g in grad_two]
    grad_own = after(grad_two, gathered[0][2])
    keep_two, send_two = weight_grad("act", place, ext, act, grad_own, *sizes)
    dz_one, carry, sums, r0 = [], None, None, 0
    for q, count in enumerate(flow):
        out = conv_back("active", r0, count, *sizes, ext, wt_two, gathered[q], h_one, params_one, carry, sums)
        dz, sums = out[:2]
        dz_one.append(dz)
        carry = out[-1]
        r0 += count
    part_two = scatter_grad(keep_two, send_two, dp, index, {})
    sums_one = sum_over(sums, "dp", dp)
    grad_one = norm_back(ext, params_one, sums_one, h_one, dz_one, flow, *sizes)
    gathered = [gather_blocks(g, ch) for g in grad_one]
    keep_one, send_one = weight_grad("images", place, ext, [images], grad_one, *sizes)
    input_rows, carries, carry, r0 = [], [], None, 0
    for q, count in enumerate(flow):
        out = conv_back("input", r0, count, *sizes, ext, wt_one, gathered[q], grad_pre[q], None, carry, None)
        input_rows.append(out[0])
        carry = out[-1]
        carries.append(carry)
        r0 += count
    input_grad = jnp.concatenate(input_rows)
    part_one = scatter_grad(keep_one, send_one, dp, index, {1: carries[0], 2: carries[1]})
    squares = jnp.sum(squares, axis=1)
    own = jnp.stack([squares[0] / dp, squares[1] / dp, jnp.sum(part_one * part_one), jnp.sum(part_two * part_two)])
    norms = jnp.sqrt(sum_over(sum_over(own, "dp", dp), "chan", ch))
    weight_norms, grad_norms = norms[:2], norms[2:]
    trust = TRUST_COEF * weight_norms / (grad_norms + DECAY * weight_norms)
    weight_two_grad = gather_grad(part_two, dp, index).reshape(weight_two.shape)
    weight_one_grad = gather_grad(part_one, dp, index, input_grad).reshape(weight_one.shape)
    moment_one_new = MOMENTUM * moment_one + LEARN_RATE * trust[0] * (weight_one_grad + DECAY * weight_one)
    moment_two_new = MOMENTUM * moment_two + LEARN_RATE * trust[1] * (weight_two_grad + DECAY * weight_two)

    def as_images(x):
        return jnp.transpose(x.reshape(side, side, batch, LANES), (2, 0, 1, 3))

    return (
        as_images(block_output),
        as_images(input_grad),
        weight_one_grad,
        sums_one[1],
        sums_one[0],
        weight_two_grad,
        sums_two[1],
        sums_two[0],
        moment_one_new,
        moment_two_new,
        weight_norms,
        grad_norms,
    )


def solution(mesh):
    full, rows, both = P("dp", None, None, None), P("dp"), P("dp", None, None, "chan")
    weight, channel = P(None, None, "chan"), P("chan")
    return jax.shard_map(
        functools.partial(shards, mesh.shape["dp"], mesh.shape["chan"]),
        mesh=mesh,
        in_specs=(full, rows, both, weight, channel, channel, weight, channel, channel, weight, weight),
        out_specs=(both, both, weight, channel, channel, weight, channel, channel, weight, weight, P(), P()),
        check_vma=False,
    )
```

```python
import functools

import jax
import jax.numpy as jnp
from jax import lax
from jax.experimental import pallas as pl
from jax.experimental.pallas import tpu as pltpu
from jax.sharding import PartitionSpec as P

EPSILON = 1e-05
MOMENTUM = 0.9
LEARN_RATE = 8.0
TRUST_COEF = 0.001
DECAY = 5e-05
GELU_A = 0.7978845608028654
GELU_B = 0.7978845608028654 * 0.044715
F32 = jnp.float32
BF16 = jnp.bfloat16
LANES = 128
TAPS = 9
PAIRS = ((0, 2), (2, 4), (4, 6), (6, 8), (8, 9))
VMEM_LEAST = 12 * 1024 * 1024
VMEM_OPERANDS = 7 * 1024 * 1024
DMA = pltpu.SemaphoreType.DMA


def mask_at(ext, r, c):
    if isinstance(r, int) and max(r, c) < 5:
        return None
    return jnp.where(ext > jnp.maximum(r, c), 1.0, 0.0).astype(F32)


def times(x, m):
    return x if m is None else x * m


def gelu(v):
    t = jnp.tanh(v * (GELU_A + GELU_B * (v * v)))
    half = 0.5 * v
    return half + half * t


def gelu_both(v):
    sq = v * v
    t = jnp.tanh(v * (GELU_A + GELU_B * sq))
    half = 0.5 * v
    value = half + half * t
    slope = 0.5 + 0.5 * t + (half - half * (t * t)) * (GELU_A + (3.0 * GELU_B) * sq)
    return value, slope


def call(name, body, outs, ins, scratch=()):
    spec = {
        "v": pl.BlockSpec(memory_space=pltpu.VMEM),
        "h": pl.BlockSpec(memory_space=pltpu.HBM),
        "s": pl.BlockSpec(memory_space=pltpu.SMEM),
    }
    return pl.pallas_call(
        body,
        name=name,
        out_shape=[jax.ShapeDtypeStruct(s, d) for s, d, _ in outs],
        in_specs=[spec[w] for _, w in ins],
        out_specs=[spec[w] for _, _, w in outs],
        scratch_shapes=list(scratch),
        compiler_params=pltpu.CompilerParams(vmem_limit_bytes=max(VMEM_LEAST, VMEM_OPERANDS + room(scratch))),
        cost_estimate=pl.CostEstimate(flops=0, bytes_accessed=0, transcendentals=0),
    )(*[pltpu.with_memory_space_constraint(x, pltpu.HBM) if w == "h" else x for x, w in ins])


def segments(*splits):
    ends = sorted({sum(s[: k + 1]) for s in splits for k in range(len(s))})
    result, start = [], 0
    for end in ends:
        result.append((start, end, [row_place(s, start) for s in splits]))
        start = end
    return result


def row_place(split, r):
    at = 0
    for index, size in enumerate(split):
        if r < at + size:
            return index, at
        at += size


def room(scratch):
    total = 0
    for x in scratch:
        if hasattr(x, "memory_space") and x.memory_space == pltpu.VMEM:
            size = jnp.dtype(x.dtype).itemsize
            for n in x.shape:
                size *= n
            total += size
    return total


class Takes:
    def __init__(self, refs):
        self.refs = list(refs)

    def __call__(self, n=None):
        if n is None:
            return self.refs.pop(0)
        return [self.refs.pop(0) for _ in range(n)]


def prep_body(blocks, chan_ref, one_ref, two_ref, wb_ref, sq_ref, *wt_refs):
    chan = chan_ref[0]
    sq_ref[...] = jnp.zeros(sq_ref.shape, F32)
    for layer, w_ref in enumerate((one_ref, two_ref)):
        total = jnp.zeros((1, LANES), F32)
        for k in range(blocks):
            rows = pl.ds(pl.multiple_of(jnp.bitwise_xor(chan, k) * LANES, LANES), LANES)
            for t in range(TAPS):
                piece = w_ref[t, rows, :]
                total = total + jnp.sum(piece * piece, axis=0, keepdims=True)
                if layer:
                    wb_ref[k * LANES : (k + 1) * LANES, t * LANES : (t + 1) * LANES] = piece.astype(BF16)
                flip = TAPS - 1 - t
                wt_refs[layer * blocks + k][:, flip * LANES : (flip + 1) * LANES] = piece.T.astype(BF16)
        sq_ref[layer : layer + 1] = total


def prep(weight_one, weight_two, chan):
    width = weight_one.shape[1]
    blocks = width // LANES
    return call(
        "prep",
        functools.partial(prep_body, blocks),
        [
            ((width, TAPS * LANES), BF16, "v"),
            ((8, LANES), F32, "v"),
        ]
        + [((LANES, TAPS * LANES), BF16, "v")] * (2 * blocks),
        [(chan, "s"), (weight_one, "v"), (weight_two, "v")],
    )


def add_row(lhs_ref, w_ref, acc, slot, batch):
    rows = lhs_ref.shape[0]
    for a, b in PAIRS:
        y = jnp.dot(lhs_ref[...], w_ref[:, a * LANES : b * LANES], preferred_element_type=F32)
        for t in range(a, b):
            i, j = divmod(t, 3)
            z = y[:, (t - a) * LANES : (t - a + 1) * LANES]
            at = slot + 2 - i
            if j == 0:
                acc[at, batch:] += z[: rows - batch]
            elif j == 1:
                acc[at] += z
            else:
                acc[at, : rows - batch] += z[batch:]


def start_acc(acc, carry_ref):
    for slot in range(acc.shape[0]):
        if carry_ref is not None and slot < 2:
            acc[slot] = carry_ref[slot]
        else:
            acc[slot] = jnp.zeros(acc.shape[1:], F32)


def emitted(r0, count, side):
    first = 0 if r0 == 0 else r0 - 1
    last = side if r0 + count == side else r0 + count - 1
    return first, last, first - (r0 - 1)


def ready_rows(t, r0, count, side):
    r = r0 + t
    rows = [r - 1] if r > 0 else []
    return rows + [r] if r == side - 1 else rows


class Stats:
    def __init__(self, ext, side, batch):
        self.ext, self.side, self.batch = ext, side, batch
        self.ref = None
        zero = jnp.zeros((batch, LANES), F32)
        self.s1, self.s2, self.n = zero, zero, zero

    def row(self, acc, slot, r, low_ref=None):
        batch = self.batch
        if self.ref is None:
            s = n = jnp.zeros((batch, LANES), F32)
            for c in range(self.side):
                m = mask_at(self.ext, r, c)
                s = s + times(acc[slot, c * batch : (c + 1) * batch], m)
                n = n + (1.0 if m is None else m)
            n = jnp.sum(n, axis=0, keepdims=True)
            self.ref = jnp.sum(s, axis=0, keepdims=True) / jnp.maximum(n, 1.0)
        for c in range(self.side):
            m = mask_at(self.ext, r, c)
            d = acc[slot, c * batch : (c + 1) * batch] - self.ref
            if low_ref is not None:
                low_ref[c * batch : (c + 1) * batch] = d.astype(BF16)
            masked = times(d, m)
            self.s1 = self.s1 + masked
            self.s2 = self.s2 + masked * d
            self.n = self.n + (1.0 if m is None else m)

    def store(self, stat_ref, prev_ref, chunk):
        s1, s2, n = (jnp.sum(x, axis=0, keepdims=True) for x in (self.s1, self.s2, self.n))
        safe = jnp.maximum(n, 1.0)
        whole = (self.ref + s1 / safe, s2 - s1 * s1 / safe, n)
        stat_ref[...] = jnp.zeros(stat_ref.shape, F32) if prev_ref is None else prev_ref[...]
        if prev_ref is not None:
            whole = merge_rows(*(prev_ref[k : k + 1] for k in range(3)), *whole)
        for k in range(3):
            stat_ref[k : k + 1] = whole[k]
        stat_ref[3 + chunk : 4 + chunk] = self.ref


def merge_rows(mean_a, m2_a, n_a, mean_b, m2_b, n_b):
    n = n_a + n_b
    safe = jnp.maximum(n, 1.0)
    delta = mean_a - mean_b
    mean = (n_a * mean_a + n_b * mean_b) / safe
    return mean, m2_a + m2_b + delta * delta * (n_a * n_b / safe), n


def conv_images_body(chunk, r0, count, side, batch, blocks, *refs):
    take = Takes(refs)
    place_ref, ext_ref, w_in, x_hbm = take(4)
    carry_ref, prev_ref = take(2) if r0 else (None, None)
    h_ref, stat_ref, low_ref, own_ref = take(4)
    w_ref = take() if r0 == 0 else w_in
    carry_out = None if r0 + count == side else take()
    acc, raw, x_sem = take(3)
    lhs = take(count)
    fetches = [pltpu.make_async_copy(x_hbm.at[r0 + t], raw.at[t], x_sem.at[t]) for t in range(count)]
    fetches[0].start()
    if r0 == 0:
        w_raw, w_sem = take(2)
        taps = [pltpu.make_async_copy(w_in.at[t], w_raw.at[t], w_sem.at[t]) for t in range(TAPS)]
        for copy in taps:
            copy.start()
    for copy in fetches[1:]:
        copy.start()
    ext = ext_ref[...]
    start_acc(acc, carry_ref)
    if r0 == 0:
        for t in range(TAPS):
            taps[t].wait()
            w_ref[:, t * LANES : (t + 1) * LANES] = w_raw[t].astype(BF16)

    mine = pl.ds(pl.multiple_of(place_ref[0] * LANES, LANES), LANES)

    def stage(t):
        fetches[t].wait()
        for c in range(side):
            part = slice(c * batch, (c + 1) * batch)
            m = mask_at(ext, r0 + t, c)
            x = raw[t, part, mine]
            own_ref[t, part] = x if m is None else x * m.astype(BF16)
            for k in range(blocks):
                lanes = slice(k * LANES, (k + 1) * LANES)
                x = raw[t, part, lanes]
                lhs[t][part, lanes] = x if m is None else x * m.astype(BF16)

    first, last, _ = emitted(r0, count, side)
    stats = Stats(ext, side, batch)
    stage(0)
    for t in range(count):
        if t + 1 < count:
            stage(t + 1)
        add_row(lhs[t], w_ref, acc, t, batch)
        for r in ready_rows(t, r0, count, side):
            h_ref[r - first] = acc[r - (r0 - 1)]
            stats.row(acc, r - (r0 - 1), r, low_ref.at[r - first])
    stats.store(stat_ref, prev_ref, chunk)
    if carry_out is not None:
        carry_out[0] = acc[count]
        carry_out[1] = acc[count + 1]


def conv_images(chunk, r0, count, side, batch, place, ext, weights, images, carry, prev):
    pixels, width = side * batch, images.shape[2]
    first, last, _ = emitted(r0, count, side)
    rows = last - first
    ins = [(place, "s"), (ext, "v"), (weights, "v" if r0 else "h"), (images, "h")]
    if r0:
        ins += [(carry, "v"), (prev, "v")]
    outs = [((rows, pixels, LANES), F32, "v"), ((8, LANES), F32, "v"), ((rows, pixels, LANES), BF16, "v")]
    outs.append(((count, pixels, LANES), BF16, "v"))
    if r0 == 0:
        outs.append(((width, TAPS * LANES), BF16, "v"))
    if r0 + count != side:
        outs.append(((2, pixels, LANES), F32, "v"))
    scratch = [pltpu.VMEM((count + 2, pixels, LANES), F32), pltpu.VMEM((count, pixels, width), BF16), DMA((count,))]
    scratch += [pltpu.VMEM((pixels, width), BF16) for _ in range(count)]
    if r0 == 0:
        scratch += [pltpu.VMEM((TAPS, width, LANES), F32), DMA((TAPS,))]
    return call(
        f"conv_one_{r0}",
        functools.partial(conv_images_body, chunk, r0, count, side, batch, width // LANES),
        outs,
        ins,
        scratch,
    )


def conv_active_body(chunk, r0, count, side, batch, blocks, *refs):
    take = Takes(refs)
    place_ref, ext_ref, w_ref = take(3)
    sources, params = take(blocks), take(blocks)
    carry_ref, prev_ref = take(2) if r0 else (None, None)
    h_ref, stat_ref, act_ref = take(3)
    carry_out = None if r0 + count == side else take()
    acc = take()
    lhs = take(count)
    ext = ext_ref[...]
    start_acc(acc, carry_ref)

    def stage(t):
        for k in range(blocks):
            scale, shift = params[k][0:1], params[k][5 + chunk : 6 + chunk]
            for c in range(side):
                part = slice(c * batch, (c + 1) * batch)
                z = sources[k][t, part].astype(F32) * scale + shift
                low = times(gelu(z), mask_at(ext, r0 + t, c)).astype(BF16)
                lhs[t][part, k * LANES : (k + 1) * LANES] = low
                act_ref[t, part, k * LANES : (k + 1) * LANES] = low

    first, last, _ = emitted(r0, count, side)
    stats = Stats(ext, side, batch)
    stage(0)
    for t in range(count):
        if t + 1 < count:
            stage(t + 1)
        add_row(lhs[t], w_ref, acc, t, batch)
        for r in ready_rows(t, r0, count, side):
            h_ref[r - first] = acc[r - (r0 - 1)]
            stats.row(acc, r - (r0 - 1), r)
    stats.store(stat_ref, prev_ref, chunk)
    if carry_out is not None:
        carry_out[0] = acc[count]
        carry_out[1] = acc[count + 1]


def conv_active(chunk, r0, count, side, batch, place, ext, weights, sources, params, carry, prev):
    blocks, pixels = len(sources), side * batch
    width = LANES * blocks
    first, last, _ = emitted(r0, count, side)
    ins = [(place, "s"), (ext, "v"), (weights, "v")] + [(x, "v") for x in sources] + [(p, "v") for p in params]
    if r0:
        ins += [(carry, "v"), (prev, "v")]
    outs = [((last - first, pixels, LANES), F32, "v"), ((8, LANES), F32, "v"), ((count, pixels, width), BF16, "v")]
    if r0 + count != side:
        outs.append(((2, pixels, LANES), F32, "v"))
    scratch = [pltpu.VMEM((count + 2, pixels, LANES), F32)]
    scratch += [pltpu.VMEM((pixels, width), BF16) for _ in range(count)]
    return call(
        f"conv_two_{r0}",
        functools.partial(conv_active_body, chunk, r0, count, side, batch, blocks),
        outs,
        ins,
        scratch,
    )


def conv_back_body(kind, r0, count, side, batch, blocks, h_split, splits, *refs):
    take = Takes(refs)
    ext_ref = take()
    wt_refs = take(blocks)
    sources = [take(blocks) for _ in splits]
    first, last, _ = emitted(r0, count, side)
    active = kind == "active"
    carry_ref = prev_ref = params_ref = None
    if active:
        params_ref = take()
        h_used = sorted({row_place(h_split, r)[0] for r in range(first, last)})
        h_refs = dict(zip(h_used, take(len(h_used))))
    else:
        extras = take(len(h_split))
    if r0:
        carry_ref = take()
        prev_ref = take() if active else None
    out_ref = take()
    sum_ref = take() if active else None
    carry_out = None if r0 + count == side else take()
    acc, w_ref = take(2)
    in_sem, w_sem = take(2)
    lhs = take(3)
    chunks = [row_place(splits, t) for t in range(count)]
    fetches = [
        [
            pltpu.make_async_copy(
                sources[chunks[t][0]][k].at[t - chunks[t][1]], lhs[t % 3].at[:, k * LANES : (k + 1) * LANES], in_sem.at[t * blocks + k]
            )
            for k in range(blocks)
        ]
        for t in range(count)
    ]
    weights = [
        pltpu.make_async_copy(wt_refs[k], w_ref.at[k * LANES : (k + 1) * LANES], w_sem.at[k]) for k in range(blocks)
    ]
    for copy in weights + fetches[0] + fetches[1]:
        copy.start()
    ext = ext_ref[...]
    start_acc(acc, carry_ref)
    zero = jnp.zeros((batch, LANES), F32)
    total = [zero, zero]
    if active:
        scale, shift, rscale, offset = (params_ref[k : k + 1] for k in range(4))

    def finish(t):
        for r in ready_rows(t, r0, count, side):
            slot, k = r - (r0 - 1), r - first
            for c in range(side):
                part = slice(c * batch, (c + 1) * batch)
                m = mask_at(ext, r, c)
                if active:
                    index, base = row_place(h_split, r)
                    h = h_refs[index][r - base, part]
                    _, slope = gelu_both(h * scale + shift)
                    dz = times(acc[slot, part], m) * slope
                    out_ref[k, part] = dz
                    total[0] = total[0] + dz
                    total[1] = total[1] + dz * (h * rscale + offset)
                else:
                    index, base = row_place(h_split, r)
                    out_ref[k, part] = times(extras[index][r - base, part] + acc[slot, part], m)

    for copy in weights:
        copy.wait()
    for t in range(count):
        for copy in fetches[t]:
            copy.wait()
        if t + 2 < count:
            for copy in fetches[t + 2]:
                copy.start()
        add_row(lhs[t % 3], w_ref, acc, t, batch)
        finish(t)
    if carry_out is not None:
        carry_out[0] = acc[count]
        carry_out[1] = acc[count + 1]
    if active:
        sum_ref[...] = jnp.zeros(sum_ref.shape, F32)
        for k in range(2):
            s = jnp.sum(total[k], axis=0, keepdims=True)
            sum_ref[k : k + 1] = s if prev_ref is None else s + prev_ref[k : k + 1]


def conv_back(kind, r0, count, side, batch, ext, weights, sources, extra, params, carry, prev):
    blocks, pixels = len(weights), side * batch
    splits = [x[0].shape[0] for x in sources]
    first, last, _ = emitted(r0, count, side)
    rows = last - first
    active = kind == "active"
    ins = [(ext, "v")] + [(x, "h") for x in list(weights) + [x for chunk in sources for x in chunk]]
    h_split = [h.shape[0] for h in extra]
    if active:
        ins.append((params, "v"))
        ins += [(extra[k], "v") for k in sorted({row_place(h_split, r)[0] for r in range(first, last)})]
    else:
        ins += [(x, "v") for x in extra]
    if r0:
        ins.append((carry, "v"))
        if active:
            ins.append((prev, "v"))
    outs = [((rows, pixels, LANES), F32, "v")]
    if active:
        outs.append(((8, LANES), F32, "v"))
    if r0 + count != side:
        outs.append(((2, pixels, LANES), F32, "v"))
    scratch = [pltpu.VMEM((count + 2, pixels, LANES), F32), pltpu.VMEM((blocks * LANES, TAPS * LANES), BF16)]
    scratch += [DMA((count * blocks,)), DMA((blocks,))]
    scratch += [pltpu.VMEM((pixels, blocks * LANES), BF16) for _ in range(3)]
    return call(
        f"back_{kind}_{r0}",
        functools.partial(conv_back_body, kind, r0, count, side, batch, blocks, h_split, splits),
        outs,
        ins,
        scratch,
    )


def weight_grad_body(kind, side, batch, blocks, splits, ways, *refs):
    take = Takes(refs)
    place_ref, ext_ref = take(2)
    x_refs, g_refs = take(len(splits[0])), take(len(splits[1]))
    keep_ref, *send_refs = take(ways)
    acc, gs, masked = take(3)
    raw, x_sem = take(2) if kind == "images" else (None, None)
    mine = place_ref[1]
    rows = side * batch
    def fetch(r):
        slot = lax.rem(r, 3)
        return pltpu.make_async_copy(x_refs[0].at[r], raw.at[slot], x_sem.at[slot])

    if kind == "images":
        fetch(0).start()
        fetch(1).start()
    ext = ext_ref[...]
    gs[0] = jnp.zeros((rows, LANES), BF16)
    gs[side + 1] = jnp.zeros((rows, LANES), BF16)
    for r in range(side):
        index, base = row_place(splits[1], r)
        gs[r + 1] = g_refs[index][r - base]
    acc[...] = jnp.zeros(acc.shape, F32)
    edge = jnp.zeros((batch, LANES), BF16)
    for start, stop, ((xi, xb),) in segments(splits[0]):

        @pl.loop(start, stop)
        def _(r, xi=xi, xb=xb):
            if kind == "images":

                @pl.when(r + 2 < side)
                def _():
                    fetch(r + 2).start()

                fetch(r).wait()
                for c in range(side):
                    part = slice(c * batch, (c + 1) * batch)
                    m = mask_at(ext, r, c).astype(BF16)
                    for k in range(blocks):
                        lanes = slice(k * LANES, (k + 1) * LANES)
                        masked[part, lanes] = raw[lax.rem(r, 3), part, lanes] * m
                x = masked[...]
            else:
                x = x_refs[xi][r - xb]
            parts = []
            for i in range(3):
                g = gs[r + 2 - i]
                parts.append(jnp.concatenate([g[batch:], edge], axis=0))
                parts.append(g)
                parts.append(jnp.concatenate([edge, g[: rows - batch]], axis=0))
            wide = jnp.concatenate(parts, axis=1)
            acc[...] += lax.dot_general(x, wide, (((0,), (0,)), ((), ())), preferred_element_type=F32)

    share = TAPS * blocks // ways
    for t in range(TAPS):
        for k in range(blocks):
            unit, lanes = t * blocks + k, slice(t * LANES, (t + 1) * LANES)
            if kind == "images":
                value = acc[k * LANES : (k + 1) * LANES, lanes]
            else:
                other = jnp.bitwise_xor(place_ref[0], k)
                value = acc[pl.ds(pl.multiple_of(other * LANES, LANES), LANES), lanes]
            at = slice(unit % share * LANES, (unit % share + 1) * LANES)
            distance = jnp.bitwise_xor(mine, unit // share)

            @pl.when(distance == 0)
            def _(value=value, at=at):
                keep_ref[at] = value

            for d in range(1, ways):

                @pl.when(distance == d)
                def _(value=value, at=at, d=d):
                    send_refs[d - 1][at] = value.astype(BF16)


def weight_grad(kind, place, ext, xs, gs, ways, side, batch):
    width, pixels = xs[0].shape[2], side * batch
    blocks = width // LANES
    splits = ([x.shape[0] for x in xs], [g.shape[0] for g in gs])
    share = TAPS * width // ways
    return call(
        f"wgrad_{kind}",
        functools.partial(weight_grad_body, kind, side, batch, blocks, splits, ways),
        [((share, LANES), F32, "v")] + [((share, LANES), BF16, "v")] * (ways - 1),
        [(place, "s"), (ext, "v")] + [(x, "h" if kind == "images" else "v") for x in xs] + [(g, "v") for g in gs],
        [
            pltpu.VMEM((width, TAPS * LANES), F32),
            pltpu.VMEM((side + 2, pixels, LANES), BF16),
            pltpu.VMEM((pixels, width), BF16),
        ]
        + ([pltpu.VMEM((3, pixels, width), BF16), DMA((3,))] if kind == "images" else []),
    )


def block_end_body(side, batch, split, own_split, grad_split, *refs):
    take = Takes(refs)
    ext_ref, params_ref, cot_ref = take(3)
    h_refs, own_refs = take(len(split)), take(len(own_split))
    out_hbm = take()
    grad_refs = take(len(grad_split))
    sum_ref, outs, sems = take(3)
    ext = ext_ref[...]
    scale, shift, rscale, offset = (params_ref[k : k + 1] for k in range(4))
    zero = jnp.zeros((batch, LANES), F32)
    total = (zero, zero)

    def store(r):
        return pltpu.make_async_copy(outs.at[r], out_hbm.at[r], sems.at[r])

    for start, stop, ((index, base), (wi, wb), (gi, gb)) in segments(split, own_split, grad_split):

        def one(r, carry, index=index, base=base, wi=wi, wb=wb, gi=gi, gb=gb):
            ds, dn = carry
            for c in range(side):
                part = slice(c * batch, (c + 1) * batch)
                m = mask_at(ext, r, c)
                h = h_refs[index][r - base, part]
                value, slope = gelu_both(h * scale + shift + own_refs[wi][r - wb, part].astype(F32))
                outs[r, part] = (value * m).astype(BF16)
                dz = cot_ref[r, part].astype(F32) * m * slope
                grad_refs[gi][r - gb, part] = dz
                ds = ds + dz
                dn = dn + dz * (h * rscale + offset)
            store(r).start()
            return ds, dn

        total = lax.fori_loop(start, stop, one, total)
    sum_ref[...] = jnp.zeros(sum_ref.shape, F32)
    sum_ref[0:1] = jnp.sum(total[0], axis=0, keepdims=True)
    sum_ref[1:2] = jnp.sum(total[1], axis=0, keepdims=True)
    for r in range(side):
        store(r).wait()


def block_end(ext, params, cotangent, hs, owns, grad_split, side, batch):
    pixels = side * batch
    shape = (side, pixels, LANES)
    split, own_split = [h.shape[0] for h in hs], [x.shape[0] for x in owns]
    outs = [(shape, BF16, "h")] + [((n, pixels, LANES), F32, "v") for n in grad_split] + [((8, LANES), F32, "v")]
    return call(
        "block_end",
        functools.partial(block_end_body, side, batch, split, own_split, grad_split),
        outs,
        [(ext, "v"), (params, "v"), (cotangent, "v")] + [(x, "v") for x in list(hs) + list(owns)],
        [pltpu.VMEM(shape, BF16), DMA((side,))],
    )


def norm_back_body(side, batch, splits, *refs):
    take = Takes(refs)
    ext_ref, params_ref, sums_ref = take(3)
    h_refs, dz_refs, out_refs = (take(len(s)) for s in splits)
    ext = ext_ref[...]
    scale, _, rscale, offset, n = (params_ref[k : k + 1] for k in range(5))
    shift_grad, gain_grad = sums_ref[0:1] / n, sums_ref[1:2] / n
    b = scale * rscale * gain_grad
    c0 = scale * (shift_grad + offset * gain_grad)
    for start, stop, ((hi, hb), (zi, zb), (oi, ob)) in segments(*splits):

        @pl.loop(start, stop)
        def _(r, hi=hi, hb=hb, zi=zi, zb=zb, oi=oi, ob=ob):
            for c in range(side):
                part = slice(c * batch, (c + 1) * batch)
                m = mask_at(ext, r, c)
                grad = scale * dz_refs[zi][r - zb, part] - (h_refs[hi][r - hb, part] * b + c0)
                out_refs[oi][r - ob, part] = (m * grad).astype(BF16)


def norm_back(ext, params, sums, hs, dzs, flow, side, batch):
    splits = ([h.shape[0] for h in hs], [z.shape[0] for z in dzs], list(flow))
    return call(
        "norm_back",
        functools.partial(norm_back_body, side, batch, splits),
        [((n, side * batch, LANES), BF16, "v") for n in flow],
        [(ext, "v"), (params, "v"), (sums, "v")] + [(x, "v") for x in list(hs) + list(dzs)],
    )


def as_rows(values):
    row = lax.broadcasted_iota(jnp.int32, (8, LANES), 0)
    out = jnp.zeros((8, LANES), F32)
    for k, value in enumerate(values):
        out = jnp.where(row == k, value, out)
    return out


def merge(a, b):
    merged = merge_rows(*(a[k : k + 1] for k in range(3)), *(b[k : k + 1] for k in range(3)))
    return as_rows(list(merged) + [a[k : k + 1] for k in range(3, 6)])


def affine(a, gain, shift):
    center, n = a[0:1], a[2:3]
    rscale = lax.rsqrt(a[1:2] / n + EPSILON)
    scale = rscale * gain
    rows = [scale, shift - center * scale, rscale, -center * rscale, n]
    return as_rows(rows + [(a[3 + q : 4 + q] - center) * scale + shift for q in range(3)])


def swap(x, axis, size, k):
    return lax.ppermute(x, axis, [(i, i ^ k) for i in range(size)])


def after(x, *others):
    return lax.optimization_barrier((x,) + others)[0]


class Sum:
    def __init__(self, x, size, add=None):
        self.x, self.size, self.k = x, size, 1
        self.add = add or (lambda a, b: a + b)

    def step(self, start=(), end=()):
        if self.k < self.size:
            x = after(self.x, *start) if start else self.x
            other = swap(x, "dp", self.size, self.k)
            self.x = self.add(self.x, after(other, *end) if end else other)
            self.k *= 2
        return self.x

    def end(self):
        while self.k < self.size:
            self.step()
        return self.x


class Scatter:
    def __init__(self, keep, sends, size, index):
        self.keep, self.sends, self.size, self.index = keep, sends, size, index
        self.k = None

    def step(self, start=(), end=()):
        if self.k is None:
            sends = self.sends
            if start:
                sends = lax.optimization_barrier(tuple(sends) + tuple(start))[: len(sends)]
            others = tuple(swap(x, "dp", self.size, d + 1) for d, x in enumerate(sends))
            if end:
                others = lax.optimization_barrier(others + tuple(end))[: len(sends)]
            for other in others:
                self.keep = self.keep + other.astype(F32)
            self.k = len(sends) + 1
        elif self.k < self.size:
            half = self.keep.shape[0] // 2
            low, high = self.keep[:half], self.keep[half:]
            upper = (self.index // self.k) % 2 == 1
            send = jnp.where(upper, low, high).astype(BF16)
            other = swap(after(send, *start) if start else send, "dp", self.size, self.k)
            self.keep = jnp.where(upper, high, low) + (after(other, *end) if end else other).astype(F32)
            self.k *= 2
        return self.keep

    def end(self):
        while self.k is None or self.k < self.size:
            self.step()
        return self.keep


class Gather:
    def __init__(self, part, size, ways, index, at_once):
        self.x, self.size, self.ways, self.index, self.at_once = part.astype(BF16), size, ways, index, at_once
        self.ks, k = [], size
        while k > ways:
            k //= 2
            self.ks.append(k)
        if at_once:
            self.ks.append(0)
        else:
            while k > 1:
                k //= 2
                self.ks.append(ways // (2 * k))

    def step(self, start=(), end=()):
        if not self.ks:
            return self.x
        x = after(self.x, *start) if start else self.x
        k = self.ks.pop(0)
        if k:
            other = swap(x, "dp", self.size, k)
            other = after(other, *end) if end else other
            upper = (self.index // k) % 2 == 1
            self.x = jnp.where(upper, jnp.concatenate([other, self.x]), jnp.concatenate([self.x, other]))
        else:
            others = tuple(swap(x, "dp", self.size, d) for d in range(1, self.ways))
            if end:
                others = lax.optimization_barrier(others + tuple(end))[: self.ways - 1]
            mine = self.index % self.ways
            self.x = jnp.concatenate([lax.select_n(mine ^ j, self.x, *others) for j in range(self.ways)])
        return self.x

    def end(self):
        while self.ks:
            self.step()
        return self.x.astype(F32)


class Blocks:
    def __init__(self, x, size, late=False):
        self.own, self.size = x, size
        self.far = swap(x, "chan", size, 2)
        self.near = None if late else swap(x, "chan", size, 1)

    def end(self, *others):
        if self.near is None:
            self.near = swap(after(self.own, *others), "chan", self.size, 1)
        far = after(self.far, *others) if others else self.far
        return [self.own, self.near, far, swap(far, "chan", self.size, 1)]


def sum_chan(x, size):
    k = 1
    while k < size:
        x = x + swap(x, "chan", size, k)
        k *= 2
    return x


def moment_step(weight, grad, moment, weight_norm, grad_norm):
    trust = TRUST_COEF * weight_norm / (grad_norm + DECAY * weight_norm)
    return MOMENTUM * moment + LEARN_RATE * trust * (grad + DECAY * weight)


def shards(
    dp, ch, images, groups, cotangent, weight_one, gain_one, shift_one, weight_two, gain_two, shift_two, moment_one, moment_two
):
    batch, side, _, width = images.shape
    pixels = side * batch
    images = jnp.transpose(images, (1, 2, 0, 3)).reshape(side, pixels, width)
    cotangent = jnp.transpose(cotangent, (1, 2, 0, 3)).reshape(side, pixels, LANES)
    chan, index = lax.axis_index("chan").astype(jnp.int32), lax.axis_index("dp").astype(jnp.int32)
    ways = min(4, dp)
    place = jnp.stack([chan, index % ways])
    ext = jnp.broadcast_to((5 + 2 * groups)[:, None], (batch, LANES))
    third = side // 3
    conv_in = (third + 1, third, side - 2 * third - 1)
    flow = (third, third, side - 2 * third)
    sizes = (side, batch)

    gains = [g.reshape(1, LANES) for g in (gain_one, shift_one, gain_two, shift_two)]

    low, h_one, owns, carry, stat, weights, r0 = [], [], [], None, None, weight_one, 0
    for q, count in enumerate(conv_in):
        out = conv_images(q, r0, count, *sizes, place, ext, weights, images, carry, stat)
        h, stat, chunk, own = out[:4]
        if q == 0:
            weights = out[4]
        carry = out[-1]
        h_one.append(h)
        owns.append(own)
        low.append(Blocks(chunk, ch))
        r0 += count
    wb_two, squares, *wt = prep(weight_one, weight_two, place)
    total = Sum(stat, dp, merge)
    total.step(start=(low[0].far,))
    total.step(start=(squares,))
    total.step(start=(low[1].far,))
    params_one = affine(total.end(), *gains[:2])
    params = Blocks(params_one, ch).end()

    h_two, act, carry, stat, r0 = [], [], None, None, 0
    for q, count in enumerate(flow):
        out = conv_active(q, r0, count, *sizes, place, ext, wb_two, low[q].end(), params, carry, stat)
        h, stat, rows = out[:3]
        if q == 0:
            wt_two = [after(w, stat) for w in wt[ch:]]
            wt_two = [wt_two[0]] + [swap(wt_two[k], "chan", ch, k) for k in range(1, ch)]
        h_two.append(h)
        act.append(rows)
        carry = out[-1]
        r0 += count
    params_two = affine(Sum(stat, dp, merge).end(), *gains[2:])

    out = block_end(ext, params_two, cotangent, h_two, owns, (side,), *sizes)
    block_output, grad_pre, sums = out
    sums_two = Sum(sums, dp).end()
    grad_two = norm_back(ext, params_two, after(sums_two, *wt_two[1:]), h_two, [grad_pre], (side,), *sizes)
    gathered = Blocks(grad_two[0], ch, True)
    keep, *sends = weight_grad("act", place, ext, act, grad_two, ways, *sizes)
    scatter = Scatter(keep, sends, dp, index)
    scatter.step()
    sources = gathered.end(scatter.keep)
    part_two = scatter.end()
    gather_two = Gather(part_two, dp, ways, index, True)
    dz_one, sums = conv_back("active", 0, side, *sizes, ext, wt_two, [sources], h_one, params_one, None, None)
    wt_one = [after(w, part_two) for w in wt[:ch]]
    wt_one = [wt_one[0]] + [swap(wt_one[k], "chan", ch, k) for k in range(1, ch)]
    total = Sum(sums, dp)
    total.step()
    gather_two.step(end=(sums,))
    sums_one = total.end()
    split = (third, side - third)
    grad_one = norm_back(ext, params_one, after(sums_one, gather_two.x, *wt_one[1:]), h_one, [dz_one], split, *sizes)
    gathered = [Blocks(g, ch, True) for g in grad_one]
    keep, *sends = weight_grad("images", place, ext, [images], grad_one, ways, *sizes)
    gather_two.step(start=(grad_one[0],), end=(keep,))
    scatter = Scatter(keep, sends, dp, index)
    scatter.step(start=(gathered[0].far,))
    sources = [g.end(scatter.keep) for g in gathered]
    weight_two_grad = gather_two.end().reshape(weight_two.shape)
    squares = jnp.sum(squares, axis=1)
    norms = jnp.sqrt(sum_chan(jnp.stack([squares[0], squares[1], jnp.sum(weight_two_grad * weight_two_grad)]), ch))
    part_one = scatter.end()
    gather_one = Gather(part_one, dp, ways, index, True)
    gather_one.step()
    input_grad = conv_back(
        "input", 0, side, *sizes, after(ext, gather_one.x), wt_one, sources, [grad_pre], None, None, None
    )[0]
    gather_one.step(end=(input_grad,))
    weight_one_grad = gather_one.end().reshape(weight_one.shape)
    norm_one = jnp.sqrt(sum_chan(jnp.sum(weight_one_grad * weight_one_grad).reshape(1), ch))
    weight_norms = norms[:2]
    grad_norms = jnp.concatenate([norm_one, norms[2:]])
    moment_two_new = moment_step(weight_two, weight_two_grad, moment_two, norms[1], norms[2])
    moment_one_new = moment_step(weight_one, weight_one_grad, moment_one, norms[0], norm_one[0])

    def as_images(x):
        return jnp.transpose(x.reshape(side, side, batch, LANES), (2, 0, 1, 3))

    return (
        as_images(block_output),
        as_images(input_grad),
        weight_one_grad,
        sums_one[1],
        sums_one[0],
        weight_two_grad,
        sums_two[1],
        sums_two[0],
        moment_one_new,
        moment_two_new,
        weight_norms,
        grad_norms,
    )


def solution(mesh):
    full, rows, both = P("dp", None, None, None), P("dp"), P("dp", None, None, "chan")
    weight, channel = P(None, None, "chan"), P("chan")
    return jax.shard_map(
        functools.partial(shards, mesh.shape["dp"], mesh.shape["chan"]),
        mesh=mesh,
        in_specs=(full, rows, both, weight, channel, channel, weight, channel, channel, weight, weight),
        out_specs=(both, both, weight, channel, channel, weight, channel, channel, weight, weight, P(), P()),
        check_vma=False,
    )
```

```python
import functools

import jax
import jax.numpy as jnp
from jax import lax
from jax.experimental import pallas as pl
from jax.experimental.pallas import tpu as pltpu
from jax.sharding import PartitionSpec as P

EPSILON = 1e-05
MOMENTUM = 0.9
LEARN_RATE = 8.0
TRUST_COEF = 0.001
DECAY = 5e-05
GELU_A = 0.7978845608028654
GELU_B = 0.7978845608028654 * 0.044715
F32 = jnp.float32
BF16 = jnp.bfloat16
LANES = 128
TAPS = 9
PAIRS = ((0, 2), (2, 4), (4, 6), (6, 8), (8, 9))
VMEM_LEAST = 12 * 1024 * 1024
VMEM_OPERANDS = 7 * 1024 * 1024
DMA = pltpu.SemaphoreType.DMA


def mask_at(ext, r, c):
    if isinstance(r, int) and max(r, c) < 5:
        return None
    return jnp.where(ext > jnp.maximum(r, c), 1.0, 0.0).astype(F32)


def times(x, m):
    return x if m is None else x * m


def gelu(v):
    t = jnp.tanh(v * (GELU_A + GELU_B * (v * v)))
    half = 0.5 * v
    return half + half * t


def gelu_both(v):
    sq = v * v
    t = jnp.tanh(v * (GELU_A + GELU_B * sq))
    half = 0.5 * v
    value = half + half * t
    slope = 0.5 + 0.5 * t + (half - half * (t * t)) * (GELU_A + (3.0 * GELU_B) * sq)
    return value, slope


def call(name, body, outs, ins, scratch=()):
    spec = {
        "a": pl.BlockSpec(memory_space=pl.ANY),
        "v": pl.BlockSpec(memory_space=pltpu.VMEM),
        "h": pl.BlockSpec(memory_space=pltpu.HBM),
        "s": pl.BlockSpec(memory_space=pltpu.SMEM),
    }
    return pl.pallas_call(
        body,
        name=name,
        out_shape=[jax.ShapeDtypeStruct(s, d) for s, d, _ in outs],
        in_specs=[spec[w] for _, w in ins],
        out_specs=[spec[w] for _, _, w in outs],
        scratch_shapes=list(scratch),
        compiler_params=pltpu.CompilerParams(vmem_limit_bytes=max(VMEM_LEAST, VMEM_OPERANDS + room(scratch))),
        cost_estimate=pl.CostEstimate(flops=0, bytes_accessed=0, transcendentals=0),
    )(*[pltpu.with_memory_space_constraint(x, pltpu.HBM) if w == "h" else x for x, w in ins])


def segments(*splits):
    ends = sorted({sum(s[: k + 1]) for s in splits for k in range(len(s))})
    result, start = [], 0
    for end in ends:
        result.append((start, end, [row_place(s, start) for s in splits]))
        start = end
    return result


def row_place(split, r):
    at = 0
    for index, size in enumerate(split):
        if r < at + size:
            return index, at
        at += size


def room(scratch):
    total = 0
    for x in scratch:
        if hasattr(x, "memory_space") and x.memory_space == pltpu.VMEM:
            size = jnp.dtype(x.dtype).itemsize
            for n in x.shape:
                size *= n
            total += size
    return total


class Takes:
    def __init__(self, refs):
        self.refs = list(refs)

    def __call__(self, n=None):
        if n is None:
            return self.refs.pop(0)
        return [self.refs.pop(0) for _ in range(n)]


def prep_body(blocks, chan_ref, one_ref, two_ref, wb_ref, sq_ref, *wt_refs):
    chan = chan_ref[0]
    sq_ref[...] = jnp.zeros(sq_ref.shape, F32)
    for layer, w_ref in enumerate((one_ref, two_ref)):
        total = jnp.zeros((1, LANES), F32)
        for k in range(blocks):
            rows = pl.ds(pl.multiple_of(jnp.bitwise_xor(chan, k) * LANES, LANES), LANES)
            for t in range(TAPS):
                piece = w_ref[t, rows, :]
                total = total + jnp.sum(piece * piece, axis=0, keepdims=True)
                if layer:
                    wb_ref[k * LANES : (k + 1) * LANES, t * LANES : (t + 1) * LANES] = piece.astype(BF16)
                flip = TAPS - 1 - t
                wt_refs[layer * blocks + k][:, flip * LANES : (flip + 1) * LANES] = piece.T.astype(BF16)
        sq_ref[layer : layer + 1] = total


def prep(weight_one, weight_two, chan):
    width = weight_one.shape[1]
    blocks = width // LANES
    return call(
        "prep",
        functools.partial(prep_body, blocks),
        [
            ((width, TAPS * LANES), BF16, "v"),
            ((8, LANES), F32, "v"),
        ]
        + [((LANES, TAPS * LANES), BF16, "v")] * (2 * blocks),
        [(chan, "s"), (weight_one, "v"), (weight_two, "v")],
    )


def add_row(lhs_ref, w_ref, acc, slot, batch):
    rows = lhs_ref.shape[0]
    for a, b in PAIRS:
        y = jnp.dot(lhs_ref[...], w_ref[:, a * LANES : b * LANES], preferred_element_type=F32)
        for t in range(a, b):
            i, j = divmod(t, 3)
            z = y[:, (t - a) * LANES : (t - a + 1) * LANES]
            at = slot + 2 - i
            if j == 0:
                acc[at, batch:] += z[: rows - batch]
            elif j == 1:
                acc[at] += z
            else:
                acc[at, : rows - batch] += z[batch:]


def start_acc(acc, carry_ref):
    for slot in range(acc.shape[0]):
        if carry_ref is not None and slot < 2:
            acc[slot] = carry_ref[slot]
        else:
            acc[slot] = jnp.zeros(acc.shape[1:], F32)


def emitted(r0, count, side):
    first = 0 if r0 == 0 else r0 - 1
    last = side if r0 + count == side else r0 + count - 1
    return first, last, first - (r0 - 1)


def ready_rows(t, r0, count, side):
    r = r0 + t
    rows = [r - 1] if r > 0 else []
    return rows + [r] if r == side - 1 else rows


class Stats:
    def __init__(self, ext, side, batch):
        self.ext, self.side, self.batch = ext, side, batch
        self.ref = None
        zero = jnp.zeros((batch, LANES), F32)
        self.s1, self.s2, self.n = zero, zero, zero

    def row(self, acc, slot, r, low_ref=None):
        batch = self.batch
        if self.ref is None:
            s = n = jnp.zeros((batch, LANES), F32)
            for c in range(self.side):
                m = mask_at(self.ext, r, c)
                s = s + times(acc[slot, c * batch : (c + 1) * batch], m)
                n = n + (1.0 if m is None else m)
            n = jnp.sum(n, axis=0, keepdims=True)
            self.ref = jnp.sum(s, axis=0, keepdims=True) / jnp.maximum(n, 1.0)
        for c in range(self.side):
            m = mask_at(self.ext, r, c)
            d = acc[slot, c * batch : (c + 1) * batch] - self.ref
            if low_ref is not None:
                low_ref[c * batch : (c + 1) * batch] = d.astype(BF16)
            masked = times(d, m)
            self.s1 = self.s1 + masked
            self.s2 = self.s2 + masked * d
            self.n = self.n + (1.0 if m is None else m)

    def store(self, stat_ref, prev_ref, chunk):
        s1, s2, n = (jnp.sum(x, axis=0, keepdims=True) for x in (self.s1, self.s2, self.n))
        safe = jnp.maximum(n, 1.0)
        whole = (self.ref + s1 / safe, s2 - s1 * s1 / safe, n)
        stat_ref[...] = jnp.zeros(stat_ref.shape, F32) if prev_ref is None else prev_ref[...]
        if prev_ref is not None:
            whole = merge_rows(*(prev_ref[k : k + 1] for k in range(3)), *whole)
        for k in range(3):
            stat_ref[k : k + 1] = whole[k]
        stat_ref[3 + chunk : 4 + chunk] = self.ref


def merge_rows(mean_a, m2_a, n_a, mean_b, m2_b, n_b):
    n = n_a + n_b
    safe = jnp.maximum(n, 1.0)
    delta = mean_a - mean_b
    mean = (n_a * mean_a + n_b * mean_b) / safe
    return mean, m2_a + m2_b + delta * delta * (n_a * n_b / safe), n


def conv_images_body(chunk, r0, count, side, batch, blocks, *refs):
    take = Takes(refs)
    place_ref, ext_ref, w_in, x_hbm = take(4)
    carry_ref, prev_ref = take(2) if r0 else (None, None)
    h_ref, stat_ref, low_ref, own_ref = take(4)
    w_ref = take() if r0 == 0 else w_in
    carry_out = None if r0 + count == side else take()
    acc, raw, x_sem = take(3)
    lhs = take(count)
    fetches = [pltpu.make_async_copy(x_hbm.at[r0 + t], raw.at[t], x_sem.at[t]) for t in range(count)]
    fetches[0].start()
    if r0 == 0:
        w_raw, w_sem = take(2)
        taps = [pltpu.make_async_copy(w_in.at[t], w_raw.at[t], w_sem.at[t]) for t in range(TAPS)]
        for copy in taps:
            copy.start()
    for copy in fetches[1:]:
        copy.start()
    ext = ext_ref[...]
    start_acc(acc, carry_ref)
    if r0 == 0:
        for t in range(TAPS):
            taps[t].wait()
            w_ref[:, t * LANES : (t + 1) * LANES] = w_raw[t].astype(BF16)

    mine = pl.ds(pl.multiple_of(place_ref[0] * LANES, LANES), LANES)

    def stage(t):
        fetches[t].wait()
        for c in range(side):
            part = slice(c * batch, (c + 1) * batch)
            m = mask_at(ext, r0 + t, c)
            x = raw[t, part, mine]
            own_ref[t, part] = x if m is None else x * m.astype(BF16)
            for k in range(blocks):
                lanes = slice(k * LANES, (k + 1) * LANES)
                x = raw[t, part, lanes]
                lhs[t][part, lanes] = x if m is None else x * m.astype(BF16)

    first, last, _ = emitted(r0, count, side)
    stats = Stats(ext, side, batch)
    stage(0)
    for t in range(count):
        if t + 1 < count:
            stage(t + 1)
        add_row(lhs[t], w_ref, acc, t, batch)
        for r in ready_rows(t, r0, count, side):
            h_ref[r - first] = acc[r - (r0 - 1)]
            stats.row(acc, r - (r0 - 1), r, low_ref.at[r - first])
    stats.store(stat_ref, prev_ref, chunk)
    if carry_out is not None:
        carry_out[0] = acc[count]
        carry_out[1] = acc[count + 1]


def conv_images(chunk, r0, count, side, batch, place, ext, weights, images, carry, prev):
    pixels, width = side * batch, images.shape[2]
    first, last, _ = emitted(r0, count, side)
    rows = last - first
    ins = [(place, "s"), (ext, "v"), (weights, "v" if r0 else "h"), (images, "h")]
    if r0:
        ins += [(carry, "v"), (prev, "v")]
    outs = [((rows, pixels, LANES), F32, "v"), ((8, LANES), F32, "v"), ((rows, pixels, LANES), BF16, "v")]
    outs.append(((count, pixels, LANES), BF16, "v"))
    if r0 == 0:
        outs.append(((width, TAPS * LANES), BF16, "v"))
    if r0 + count != side:
        outs.append(((2, pixels, LANES), F32, "v"))
    scratch = [pltpu.VMEM((count + 2, pixels, LANES), F32), pltpu.VMEM((count, pixels, width), BF16), DMA((count,))]
    scratch += [pltpu.VMEM((pixels, width), BF16) for _ in range(count)]
    if r0 == 0:
        scratch += [pltpu.VMEM((TAPS, width, LANES), F32), DMA((TAPS,))]
    return call(
        f"conv_one_{r0}",
        functools.partial(conv_images_body, chunk, r0, count, side, batch, width // LANES),
        outs,
        ins,
        scratch,
    )


def conv_active_body(chunk, r0, count, side, batch, blocks, *refs):
    take = Takes(refs)
    place_ref, ext_ref, w_ref = take(3)
    sources, params = take(blocks), take(blocks)
    carry_ref, prev_ref = take(2) if r0 else (None, None)
    h_ref, stat_ref, act_ref = take(3)
    carry_out = None if r0 + count == side else take()
    acc = take()
    lhs = take(count)
    ext = ext_ref[...]
    start_acc(acc, carry_ref)

    def stage(t):
        for k in range(blocks):
            scale, shift = params[k][0:1], params[k][5 + chunk : 6 + chunk]
            for c in range(side):
                part = slice(c * batch, (c + 1) * batch)
                z = sources[k][t, part].astype(F32) * scale + shift
                low = times(gelu(z), mask_at(ext, r0 + t, c)).astype(BF16)
                lhs[t][part, k * LANES : (k + 1) * LANES] = low
                act_ref[t, part, k * LANES : (k + 1) * LANES] = low

    first, last, _ = emitted(r0, count, side)
    stats = Stats(ext, side, batch)
    stage(0)
    for t in range(count):
        if t + 1 < count:
            stage(t + 1)
        add_row(lhs[t], w_ref, acc, t, batch)
        for r in ready_rows(t, r0, count, side):
            h_ref[r - first] = acc[r - (r0 - 1)]
            stats.row(acc, r - (r0 - 1), r)
    stats.store(stat_ref, prev_ref, chunk)
    if carry_out is not None:
        carry_out[0] = acc[count]
        carry_out[1] = acc[count + 1]


def conv_active(chunk, r0, count, side, batch, place, ext, weights, sources, params, carry, prev):
    blocks, pixels = len(sources), side * batch
    width = LANES * blocks
    first, last, _ = emitted(r0, count, side)
    ins = [(place, "s"), (ext, "v"), (weights, "v")] + [(x, "v") for x in sources] + [(p, "v") for p in params]
    if r0:
        ins += [(carry, "v"), (prev, "v")]
    outs = [((last - first, pixels, LANES), F32, "v"), ((8, LANES), F32, "v"), ((count, pixels, width), BF16, "v")]
    if r0 + count != side:
        outs.append(((2, pixels, LANES), F32, "v"))
    scratch = [pltpu.VMEM((count + 2, pixels, LANES), F32)]
    scratch += [pltpu.VMEM((pixels, width), BF16) for _ in range(count)]
    return call(
        f"conv_two_{r0}",
        functools.partial(conv_active_body, chunk, r0, count, side, batch, blocks),
        outs,
        ins,
        scratch,
    )


def conv_back_body(kind, r0, count, side, batch, blocks, h_split, splits, *refs):
    take = Takes(refs)
    ext_ref = take()
    wt_refs = take(blocks)
    sources = [take(blocks) for _ in splits]
    first, last, _ = emitted(r0, count, side)
    active = kind == "active"
    carry_ref = prev_ref = params_ref = None
    if active:
        params_ref = take()
        h_used = sorted({row_place(h_split, r)[0] for r in range(first, last)})
        h_refs = dict(zip(h_used, take(len(h_used))))
    else:
        extras = take(len(h_split))
    if r0:
        carry_ref = take()
        prev_ref = take() if active else None
    out_ref = take()
    sum_ref = take() if active else None
    carry_out = None if r0 + count == side else take()
    acc, w_ref = take(2)
    in_sem, w_sem = take(2)
    lhs = take(3)
    rows, out_sem = (out_ref, None) if active else take(2)
    h_rows, h_sem = take(2) if active else (None, None)
    stores = []
    chunks = [row_place(splits, t) for t in range(count)]
    fetches = [
        [
            pltpu.make_async_copy(
                sources[chunks[t][0]][k].at[t - chunks[t][1]], lhs[t % 3].at[:, k * LANES : (k + 1) * LANES], in_sem.at[t * blocks + k]
            )
            for k in range(blocks)
        ]
        for t in range(count)
    ]
    weights = [
        pltpu.make_async_copy(wt_refs[k], w_ref.at[k * LANES : (k + 1) * LANES], w_sem.at[k]) for k in range(blocks)
    ]
    for copy in weights + fetches[0] + fetches[1]:
        copy.start()
    ext = ext_ref[...]
    start_acc(acc, carry_ref)
    zero = jnp.zeros((batch, LANES), F32)
    total = [zero, zero]
    if active:
        scale, shift, rscale, offset = (params_ref[k : k + 1] for k in range(4))

    def h_fetch(r):
        index, base = row_place(h_split, r)
        return pltpu.make_async_copy(h_refs[index].at[r - base], h_rows.at[r % 3], h_sem.at[r % 3])

    if active:
        for r in range(first, min(first + 2, last)):
            h_fetch(r).start()

    def finish(r):
        slot, k = r - (r0 - 1), r - first
        for c in range(side):
            part = slice(c * batch, (c + 1) * batch)
            m = mask_at(ext, r, c)
            if active:
                h = h_rows[r % 3, part]
                _, slope = gelu_both(h * scale + shift)
                dz = times(acc[slot, part], m) * slope
                rows[k, part] = dz
                total[0] = total[0] + dz
                total[1] = total[1] + dz * (h * rscale + offset)
            else:
                index, base = row_place(h_split, r)
                rows[k, part] = times(extras[index][r - base, part] + acc[slot, part], m)
        if not active:
            stores.append(pltpu.make_async_copy(rows.at[k], out_ref.at[k], out_sem.at[k]))
            stores[-1].start()

    for copy in weights:
        copy.wait()
    ready = []
    for t in range(count + 1):
        if t < count:
            for copy in fetches[t]:
                copy.wait()
            if t + 2 < count:
                for copy in fetches[t + 2]:
                    copy.start()
        for r in ready:
            if active:
                h_fetch(r).wait()
                if r + 2 < last:
                    h_fetch(r + 2).start()
        if t < count:
            add_row(lhs[t % 3], w_ref, acc, t, batch)
        for r in ready:
            finish(r)
        ready = ready_rows(t, r0, count, side) if t < count else []
    if carry_out is not None:
        carry_out[0] = acc[count]
        carry_out[1] = acc[count + 1]
    if active:
        sum_ref[...] = jnp.zeros(sum_ref.shape, F32)
        for k in range(2):
            s = jnp.sum(total[k], axis=0, keepdims=True)
            sum_ref[k : k + 1] = s if prev_ref is None else s + prev_ref[k : k + 1]
    for copy in stores:
        copy.wait()


def conv_back(kind, r0, count, side, batch, ext, weights, sources, extra, params, carry, prev):
    blocks, pixels = len(weights), side * batch
    splits = [x[0].shape[0] for x in sources]
    first, last, _ = emitted(r0, count, side)
    rows = last - first
    active = kind == "active"
    ins = [(ext, "v")] + [(x, "h") for x in weights]
    ins += [(x, "h" if kind == "active" else "a") for chunk in sources for x in chunk]
    h_split = [h.shape[0] for h in extra]
    if active:
        ins.append((params, "v"))
        ins += [(extra[k], "h") for k in sorted({row_place(h_split, r)[0] for r in range(first, last)})]
    else:
        ins += [(x, "v") for x in extra]
    if r0:
        ins.append((carry, "v"))
        if active:
            ins.append((prev, "v"))
    outs = [((rows, pixels, LANES), F32, "v" if active else "h")]
    if active:
        outs.append(((8, LANES), F32, "v"))
    if r0 + count != side:
        outs.append(((2, pixels, LANES), F32, "v"))
    scratch = [pltpu.VMEM((count + 2, pixels, LANES), F32), pltpu.VMEM((blocks * LANES, TAPS * LANES), BF16)]
    scratch += [DMA((count * blocks,)), DMA((blocks,))]
    scratch += [pltpu.VMEM((pixels, blocks * LANES), BF16) for _ in range(3)]
    if active:
        scratch += [pltpu.VMEM((3, pixels, LANES), F32), DMA((3,))]
    else:
        scratch += [pltpu.VMEM((rows, pixels, LANES), F32), DMA((rows,))]
    return call(
        f"back_{kind}_{r0}",
        functools.partial(conv_back_body, kind, r0, count, side, batch, blocks, h_split, splits),
        outs,
        ins,
        scratch,
    )


def weight_grad_body(kind, side, batch, blocks, splits, ways, *refs):
    take = Takes(refs)
    place_ref, ext_ref = take(2)
    x_refs, g_refs = take(len(splits[0])), take(len(splits[1]))
    keep_ref, *send_refs = take(ways)
    acc, gs, masked = take(3)
    raw, x_sem = take(2) if kind == "images" else (None, None)
    mine = place_ref[1]
    rows = side * batch
    def fetch(r):
        slot = lax.rem(r, 3)
        return pltpu.make_async_copy(x_refs[0].at[r], raw.at[slot], x_sem.at[slot])

    if kind == "images":
        fetch(0).start()
        fetch(1).start()
    ext = ext_ref[...]
    gs[0] = jnp.zeros((rows, LANES), BF16)
    gs[side + 1] = jnp.zeros((rows, LANES), BF16)
    for r in range(side):
        index, base = row_place(splits[1], r)
        gs[r + 1] = g_refs[index][r - base]
    acc[...] = jnp.zeros(acc.shape, F32)
    edge = jnp.zeros((batch, LANES), BF16)
    for start, stop, ((xi, xb),) in segments(splits[0]):

        @pl.loop(start, stop)
        def _(r, xi=xi, xb=xb):
            if kind == "images":

                @pl.when(r + 2 < side)
                def _():
                    fetch(r + 2).start()

                fetch(r).wait()
                for c in range(side):
                    part = slice(c * batch, (c + 1) * batch)
                    m = mask_at(ext, r, c).astype(BF16)
                    for k in range(blocks):
                        lanes = slice(k * LANES, (k + 1) * LANES)
                        masked[part, lanes] = raw[lax.rem(r, 3), part, lanes] * m
                x = masked[...]
            else:
                x = x_refs[xi][r - xb]
            parts = []
            for i in range(3):
                g = gs[r + 2 - i]
                parts.append(jnp.concatenate([g[batch:], edge], axis=0))
                parts.append(g)
                parts.append(jnp.concatenate([edge, g[: rows - batch]], axis=0))
            wide = jnp.concatenate(parts, axis=1)
            acc[...] += lax.dot_general(x, wide, (((0,), (0,)), ((), ())), preferred_element_type=F32)

    share = TAPS * blocks // ways
    for t in range(TAPS):
        for k in range(blocks):
            unit, lanes = t * blocks + k, slice(t * LANES, (t + 1) * LANES)
            if kind == "images":
                value = acc[k * LANES : (k + 1) * LANES, lanes]
            else:
                other = jnp.bitwise_xor(place_ref[0], k)
                value = acc[pl.ds(pl.multiple_of(other * LANES, LANES), LANES), lanes]
            at = slice(unit % share * LANES, (unit % share + 1) * LANES)
            distance = jnp.bitwise_xor(mine, unit // share)

            @pl.when(distance == 0)
            def _(value=value, at=at):
                keep_ref[at] = value

            for d in range(1, ways):

                @pl.when(distance == d)
                def _(value=value, at=at, d=d):
                    send_refs[d - 1][at] = value.astype(BF16)


def weight_grad(kind, place, ext, xs, gs, ways, side, batch):
    width, pixels = xs[0].shape[2], side * batch
    blocks = width // LANES
    splits = ([x.shape[0] for x in xs], [g.shape[0] for g in gs])
    share = TAPS * width // ways
    return call(
        f"wgrad_{kind}",
        functools.partial(weight_grad_body, kind, side, batch, blocks, splits, ways),
        [((share, LANES), F32, "v")] + [((share, LANES), BF16, "v")] * (ways - 1),
        [(place, "s"), (ext, "v")] + [(x, "h" if kind == "images" else "v") for x in xs] + [(g, "v") for g in gs],
        [
            pltpu.VMEM((width, TAPS * LANES), F32),
            pltpu.VMEM((side + 2, pixels, LANES), BF16),
            pltpu.VMEM((pixels, width), BF16),
        ]
        + ([pltpu.VMEM((3, pixels, width), BF16), DMA((3,))] if kind == "images" else []),
    )


def block_end_body(side, batch, split, own_split, grad_split, *refs):
    take = Takes(refs)
    ext_ref, params_ref, cot_ref = take(3)
    h_refs, own_refs = take(len(split)), take(len(own_split))
    out_hbm = take()
    grad_refs = take(len(grad_split))
    sum_ref, outs, sems = take(3)
    ext = ext_ref[...]
    scale, shift, rscale, offset = (params_ref[k : k + 1] for k in range(4))
    zero = jnp.zeros((batch, LANES), F32)
    total = (zero, zero)

    def store(r):
        return pltpu.make_async_copy(outs.at[r], out_hbm.at[r], sems.at[r])

    for start, stop, ((index, base), (wi, wb), (gi, gb)) in segments(split, own_split, grad_split):

        def one(r, carry, index=index, base=base, wi=wi, wb=wb, gi=gi, gb=gb):
            ds, dn = carry
            for c in range(side):
                part = slice(c * batch, (c + 1) * batch)
                m = mask_at(ext, r, c)
                h = h_refs[index][r - base, part]
                value, slope = gelu_both(h * scale + shift + own_refs[wi][r - wb, part].astype(F32))
                outs[r, part] = (value * m).astype(BF16)
                dz = cot_ref[r, part].astype(F32) * m * slope
                grad_refs[gi][r - gb, part] = dz
                ds = ds + dz
                dn = dn + dz * (h * rscale + offset)
            store(r).start()
            return ds, dn

        total = lax.fori_loop(start, stop, one, total)
    sum_ref[...] = jnp.zeros(sum_ref.shape, F32)
    sum_ref[0:1] = jnp.sum(total[0], axis=0, keepdims=True)
    sum_ref[1:2] = jnp.sum(total[1], axis=0, keepdims=True)
    for r in range(side):
        store(r).wait()


def block_end(ext, params, cotangent, hs, owns, grad_split, side, batch):
    pixels = side * batch
    shape = (side, pixels, LANES)
    split, own_split = [h.shape[0] for h in hs], [x.shape[0] for x in owns]
    outs = [(shape, BF16, "h")] + [((n, pixels, LANES), F32, "v") for n in grad_split] + [((8, LANES), F32, "v")]
    return call(
        "block_end",
        functools.partial(block_end_body, side, batch, split, own_split, grad_split),
        outs,
        [(ext, "v"), (params, "v"), (cotangent, "v")] + [(x, "v") for x in list(hs) + list(owns)],
        [pltpu.VMEM(shape, BF16), DMA((side,))],
    )


def norm_back_body(side, batch, far_h, splits, *refs):
    take = Takes(refs)
    ext_ref, params_ref, sums_ref = take(3)
    h_refs, dz_refs, out_refs = (take(len(s)) for s in splits)
    gain_ref, shift_ref = take(2)
    if far_h:
        h_rows, h_sem = take(2)
        for r in range(side):
            index, base = row_place(splits[0], r)
            pltpu.make_async_copy(h_refs[index].at[r - base], h_rows.at[r], h_sem.at[r]).start()
    ext = ext_ref[...]
    scale, _, rscale, offset, n = (params_ref[k : k + 1] for k in range(5))
    shift_ref[...] = sums_ref[0:1]
    gain_ref[...] = sums_ref[1:2]
    shift_grad, gain_grad = sums_ref[0:1] / n, sums_ref[1:2] / n
    b = scale * rscale * gain_grad
    c0 = scale * (shift_grad + offset * gain_grad)
    for start, stop, ((hi, hb), (zi, zb), (oi, ob)) in segments(*splits):

        @pl.loop(start, stop)
        def _(r, hi=hi, hb=hb, zi=zi, zb=zb, oi=oi, ob=ob):
            if far_h:
                pltpu.make_async_copy(h_refs[hi].at[r - hb], h_rows.at[r], h_sem.at[r]).wait()
            for c in range(side):
                part = slice(c * batch, (c + 1) * batch)
                m = mask_at(ext, r, c)
                h = h_rows[r, part] if far_h else h_refs[hi][r - hb, part]
                grad = scale * dz_refs[zi][r - zb, part] - (h * b + c0)
                out_refs[oi][r - ob, part] = (m * grad).astype(BF16)


def norm_back(ext, params, sums, hs, dzs, flow, far_h, side, batch):
    splits = ([h.shape[0] for h in hs], [z.shape[0] for z in dzs], list(flow))
    return call(
        "norm_back",
        functools.partial(norm_back_body, side, batch, far_h, splits),
        [((n, side * batch, LANES), BF16, "v") for n in flow] + [((1, LANES), F32, "v")] * 2,
        [(ext, "v"), (params, "v"), (sums, "v")] + [(x, "h" if far_h else "v") for x in hs] + [(x, "v") for x in dzs],
        [pltpu.VMEM((side, side * batch, LANES), F32), DMA((side,))] if far_h else [],
    )


def as_rows(values):
    row = lax.broadcasted_iota(jnp.int32, (8, LANES), 0)
    out = jnp.zeros((8, LANES), F32)
    for k, value in enumerate(values):
        out = jnp.where(row == k, value, out)
    return out


def merge(a, b):
    merged = merge_rows(*(a[k : k + 1] for k in range(3)), *(b[k : k + 1] for k in range(3)))
    return as_rows(list(merged) + [a[k : k + 1] for k in range(3, 6)])


def affine(a, gain, shift):
    center, n = a[0:1], a[2:3]
    rscale = lax.rsqrt(a[1:2] / n + EPSILON)
    scale = rscale * gain
    rows = [scale, shift - center * scale, rscale, -center * rscale, n]
    return as_rows(rows + [(a[3 + q : 4 + q] - center) * scale + shift for q in range(3)])


def swap(x, axis, size, k):
    return lax.ppermute(x, axis, [(i, i ^ k) for i in range(size)])


def after(x, *others):
    return lax.optimization_barrier((x,) + others)[0]


class Sum:
    def __init__(self, x, size, add=None):
        self.x, self.size, self.k = x, size, 1
        self.add = add or (lambda a, b: a + b)

    def step(self, start=(), end=()):
        if self.k < self.size:
            x = after(self.x, *start) if start else self.x
            other = swap(x, "dp", self.size, self.k)
            self.x = self.add(self.x, after(other, *end) if end else other)
            self.k *= 2
        return self.x

    def end(self):
        while self.k < self.size:
            self.step()
        return self.x


class Scatter:
    def __init__(self, keep, sends, size, index):
        self.keep, self.sends, self.size, self.index = keep, sends, size, index
        self.k = None

    def step(self, start=(), end=()):
        if self.k is None:
            sends = self.sends
            if start:
                sends = lax.optimization_barrier(tuple(sends) + tuple(start))[: len(sends)]
            others = tuple(swap(x, "dp", self.size, d + 1) for d, x in enumerate(sends))
            if end:
                others = lax.optimization_barrier(others + tuple(end))[: len(sends)]
            for other in others:
                self.keep = self.keep + other.astype(F32)
            self.k = len(sends) + 1
        elif self.k < self.size:
            half = self.keep.shape[0] // 2
            low, high = self.keep[:half], self.keep[half:]
            upper = (self.index // self.k) % 2 == 1
            send = jnp.where(upper, low, high).astype(BF16)
            other = swap(after(send, *start) if start else send, "dp", self.size, self.k)
            self.keep = jnp.where(upper, high, low) + (after(other, *end) if end else other).astype(F32)
            self.k *= 2
        return self.keep

    def end(self):
        while self.k is None or self.k < self.size:
            self.step()
        return self.keep


class Gather:
    def __init__(self, part, size, ways, index, at_once):
        self.x, self.size, self.ways, self.index, self.at_once = part.astype(BF16), size, ways, index, at_once
        self.ks, k = [], size
        while k > ways:
            k //= 2
            self.ks.append(k)
        if at_once:
            self.ks.append(0)
        else:
            while k > 1:
                k //= 2
                self.ks.append(ways // (2 * k))

    def step(self, start=(), end=()):
        if not self.ks:
            return self.x
        x = after(self.x, *start) if start else self.x
        k = self.ks.pop(0)
        if k:
            other = swap(x, "dp", self.size, k)
            other = after(other, *end) if end else other
            upper = (self.index // k) % 2 == 1
            self.x = jnp.where(upper, jnp.concatenate([other, self.x]), jnp.concatenate([self.x, other]))
        else:
            others = tuple(swap(x, "dp", self.size, d) for d in range(1, self.ways))
            if end:
                others = lax.optimization_barrier(others + tuple(end))[: self.ways - 1]
            self.others = others
        return self.x

    def end(self, *late):
        while self.ks:
            self.step()
        if self.at_once:
            others = lax.optimization_barrier(self.others + late)[: self.ways - 1] if late else self.others
            mine = self.index % self.ways
            self.x = jnp.concatenate([lax.select_n(mine ^ j, self.x, *others) for j in range(self.ways)])
        return self.x.astype(F32)


class Blocks:
    def __init__(self, x, size, late=False):
        self.own, self.size = x, size
        self.far = swap(x, "chan", size, 2)
        self.near = None if late else swap(x, "chan", size, 1)

    def end(self, *others):
        if self.near is None:
            self.near = swap(after(self.own, *others), "chan", self.size, 1)
        far = after(self.far, *others) if others else self.far
        return [self.own, self.near, far, swap(far, "chan", self.size, 1)]


def sum_chan(x, size):
    k = 1
    while k < size:
        x = x + swap(x, "chan", size, k)
        k *= 2
    return x


def moment_step(weight, grad, moment, weight_norm, grad_norm):
    trust = TRUST_COEF * weight_norm / (grad_norm + DECAY * weight_norm)
    return MOMENTUM * moment + LEARN_RATE * trust * (grad + DECAY * weight)


def shards(
    dp, ch, images, groups, cotangent, weight_one, gain_one, shift_one, weight_two, gain_two, shift_two, moment_one, moment_two
):
    batch, side, _, width = images.shape
    pixels = side * batch
    images = jnp.transpose(images, (1, 2, 0, 3)).reshape(side, pixels, width)
    cotangent = jnp.transpose(cotangent, (1, 2, 0, 3)).reshape(side, pixels, LANES)
    chan, index = lax.axis_index("chan").astype(jnp.int32), lax.axis_index("dp").astype(jnp.int32)
    ways = min(4, dp)
    place = jnp.stack([chan, index % ways])
    ext = jnp.broadcast_to((5 + 2 * groups)[:, None], (batch, LANES))
    third = side // 3
    conv_in = (third + 1, third, side - 2 * third - 1)
    flow = (third, third, side - 2 * third)
    sizes = (side, batch)

    gains = [g.reshape(1, LANES) for g in (gain_one, shift_one, gain_two, shift_two)]

    low, h_one, owns, carry, stat, weights, r0 = [], [], [], None, None, weight_one, 0
    for q, count in enumerate(conv_in):
        out = conv_images(q, r0, count, *sizes, place, ext, weights, images, carry, stat)
        h, stat, chunk, own = out[:4]
        if q == 0:
            weights = out[4]
        carry = out[-1]
        h_one.append(h)
        owns.append(own)
        low.append(Blocks(chunk, ch))
        r0 += count
    wb_two, squares, *wt = prep(weight_one, weight_two, place)
    total = Sum(stat, dp, merge)
    total.step(start=(low[0].far,))
    total.step(start=(squares,))
    total.step(start=(low[1].far,))
    params_one = affine(total.end(), *gains[:2])
    params = Blocks(params_one, ch).end()

    h_two, act, carry, stat, r0 = [], [], None, None, 0
    for q, count in enumerate(flow):
        out = conv_active(q, r0, count, *sizes, place, ext, wb_two, low[q].end(), params, carry, stat)
        h, stat, rows = out[:3]
        if q == 0:
            wt_two = [after(w, stat) for w in wt[ch:]]
            wt_two = [wt_two[0]] + [swap(wt_two[k], "chan", ch, k) for k in range(1, ch)]
        h_two.append(h)
        act.append(rows)
        carry = out[-1]
        r0 += count
    params_two = affine(Sum(stat, dp, merge).end(), *gains[2:])

    out = block_end(ext, params_two, cotangent, h_two, owns, (side,), *sizes)
    block_output, grad_pre, sums = out
    sums_two = Sum(sums, dp).end()
    *grad_two, gain_two_grad, shift_two_grad = norm_back(ext, params_two, after(sums_two, *wt_two[1:]), h_two, [grad_pre], (side,), False, *sizes)
    gathered = Blocks(grad_two[0], ch, True)
    keep, *sends = weight_grad("act", place, ext, act, grad_two, ways, *sizes)
    scatter = Scatter(keep, sends, dp, index)
    scatter.step()
    sources = gathered.end(scatter.keep)
    wt_one = [after(w, scatter.keep) for w in wt[:ch]]
    wt_one = [wt_one[0]] + [swap(wt_one[k], "chan", ch, k) for k in range(1, ch)]
    dz_one, sums = conv_back("active", 0, side, *sizes, ext, wt_two, [sources], h_one, params_one, None, None)
    scatter.step(end=(sums,))
    part_two = scatter.end()
    gather_two = Gather(part_two, dp, ways, index, True)
    total = Sum(sums, dp)
    total.step()
    gather_two.step()
    sums_one = total.end()
    split = (third, side - third)
    *grad_one, gain_one_grad, shift_one_grad = norm_back(ext, params_one, after(sums_one, gather_two.x, *wt_one[1:]), h_one, [dz_one], split, True, *sizes)
    gathered = [Blocks(g, ch, True) for g in grad_one]
    keep, *sends = weight_grad("images", place, ext, [images], grad_one, ways, *sizes)
    gather_two.step(start=(grad_one[0],), end=(keep,))
    scatter = Scatter(keep, sends, dp, index)
    scatter.step(start=(gathered[0].far,))
    sources = [g.end(scatter.keep) for g in gathered]
    weight_two_grad = gather_two.end().reshape(weight_two.shape)
    squares = jnp.sum(squares, axis=1)
    norms = jnp.sqrt(sum_chan(jnp.stack([squares[0], squares[1], jnp.sum(weight_two_grad * weight_two_grad)]), ch))
    part_one = scatter.end()
    gather_one = Gather(part_one, dp, ways, index, True)
    gather_one.step()
    input_grad = conv_back(
        "input", 0, side, *sizes, after(ext, gather_one.x), wt_one, sources, [grad_pre], None, None, None
    )[0]
    gather_one.step(end=(input_grad,))
    moment_two_new = moment_step(weight_two, weight_two_grad, moment_two, norms[1], norms[2])
    weight_one_grad = gather_one.end().reshape(weight_one.shape)
    norm_one = jnp.sqrt(sum_chan(jnp.sum(weight_one_grad * weight_one_grad).reshape(1), ch))
    weight_norms = norms[:2]
    grad_norms = jnp.concatenate([norm_one, norms[2:]])
    moment_one_new = moment_step(weight_one, weight_one_grad, moment_one, norms[0], norm_one[0])

    def as_images(x):
        return jnp.transpose(x.reshape(side, side, batch, LANES), (2, 0, 1, 3))

    return (
        as_images(block_output),
        as_images(input_grad),
        weight_one_grad,
        gain_one_grad.reshape(LANES),
        shift_one_grad.reshape(LANES),
        weight_two_grad,
        gain_two_grad.reshape(LANES),
        shift_two_grad.reshape(LANES),
        moment_one_new,
        moment_two_new,
        weight_norms,
        grad_norms,
    )


def solution(mesh):
    full, rows, both = P("dp", None, None, None), P("dp"), P("dp", None, None, "chan")
    weight, channel = P(None, None, "chan"), P("chan")
    return jax.shard_map(
        functools.partial(shards, mesh.shape["dp"], mesh.shape["chan"]),
        mesh=mesh,
        in_specs=(full, rows, both, weight, channel, channel, weight, channel, channel, weight, weight),
        out_specs=(both, both, weight, channel, channel, weight, channel, channel, weight, weight, P(), P()),
        check_vma=False,
    )
```

```python
import functools

import jax
import jax.numpy as jnp
from jax import lax
from jax.experimental import pallas as pl
from jax.experimental.pallas import tpu as pltpu
from jax.sharding import PartitionSpec as P

EPSILON = 1e-05
MOMENTUM = 0.9
LEARN_RATE = 8.0
TRUST_COEF = 0.001
DECAY = 5e-05
GELU_A = 0.7978845608028654
GELU_B = 0.7978845608028654 * 0.044715
F32 = jnp.float32
BF16 = jnp.bfloat16
LANES = 128
TAPS = 9
PAIRS = ((0, 2), (2, 4), (4, 6), (6, 8), (8, 9))
VMEM_LEAST = 12 * 1024 * 1024
VMEM_OPERANDS = 7 * 1024 * 1024
DMA = pltpu.SemaphoreType.DMA


def mask_at(ext, r, c):
    if isinstance(r, int) and max(r, c) < 5:
        return None
    return jnp.where(ext > jnp.maximum(r, c), 1.0, 0.0).astype(F32)


def times(x, m):
    return x if m is None else x * m


def gelu(v):
    t = jnp.tanh(v * (GELU_A + GELU_B * (v * v)))
    half = 0.5 * v
    return half + half * t


def gelu_both(v):
    sq = v * v
    t = jnp.tanh(v * (GELU_A + GELU_B * sq))
    half = 0.5 * v
    value = half + half * t
    slope = 0.5 + 0.5 * t + (half - half * (t * t)) * (GELU_A + (3.0 * GELU_B) * sq)
    return value, slope


def call(name, body, outs, ins, scratch=()):
    spec = {
        "a": pl.BlockSpec(memory_space=pl.ANY),
        "v": pl.BlockSpec(memory_space=pltpu.VMEM),
        "h": pl.BlockSpec(memory_space=pltpu.HBM),
        "s": pl.BlockSpec(memory_space=pltpu.SMEM),
    }
    return pl.pallas_call(
        body,
        name=name,
        out_shape=[jax.ShapeDtypeStruct(s, d) for s, d, _ in outs],
        in_specs=[spec[w] for _, w in ins],
        out_specs=[spec[w] for _, _, w in outs],
        scratch_shapes=list(scratch),
        compiler_params=pltpu.CompilerParams(vmem_limit_bytes=max(VMEM_LEAST, VMEM_OPERANDS + room(scratch))),
        cost_estimate=pl.CostEstimate(flops=0, bytes_accessed=0, transcendentals=0),
    )(*[pltpu.with_memory_space_constraint(x, pltpu.HBM) if w == "h" else x for x, w in ins])


def segments(*splits):
    ends = sorted({sum(s[: k + 1]) for s in splits for k in range(len(s))})
    result, start = [], 0
    for end in ends:
        result.append((start, end, [row_place(s, start) for s in splits]))
        start = end
    return result


def row_place(split, r):
    at = 0
    for index, size in enumerate(split):
        if r < at + size:
            return index, at
        at += size


def room(scratch):
    total = 0
    for x in scratch:
        if hasattr(x, "memory_space") and x.memory_space == pltpu.VMEM:
            size = jnp.dtype(x.dtype).itemsize
            for n in x.shape:
                size *= n
            total += size
    return total


class Takes:
    def __init__(self, refs):
        self.refs = list(refs)

    def __call__(self, n=None):
        if n is None:
            return self.refs.pop(0)
        return [self.refs.pop(0) for _ in range(n)]


def prep_body(blocks, chan_ref, one_ref, two_ref, wb_ref, sq_ref, *wt_refs):
    chan = chan_ref[0]
    sq_ref[...] = jnp.zeros(sq_ref.shape, F32)
    for layer, w_ref in enumerate((one_ref, two_ref)):
        total = jnp.zeros((1, LANES), F32)
        for k in range(blocks):
            rows = pl.ds(pl.multiple_of(jnp.bitwise_xor(chan, k) * LANES, LANES), LANES)
            for t in range(TAPS):
                piece = w_ref[t, rows, :]
                total = total + jnp.sum(piece * piece, axis=0, keepdims=True)
                if layer:
                    wb_ref[k * LANES : (k + 1) * LANES, t * LANES : (t + 1) * LANES] = piece.astype(BF16)
                flip = TAPS - 1 - t
                wt_refs[layer * blocks + k][:, flip * LANES : (flip + 1) * LANES] = piece.T.astype(BF16)
        sq_ref[layer : layer + 1] = total


def prep(weight_one, weight_two, chan):
    width = weight_one.shape[1]
    blocks = width // LANES
    return call(
        "prep",
        functools.partial(prep_body, blocks),
        [
            ((width, TAPS * LANES), BF16, "v"),
            ((8, LANES), F32, "v"),
        ]
        + [((LANES, TAPS * LANES), BF16, "v")] * (2 * blocks),
        [(chan, "s"), (weight_one, "v"), (weight_two, "v")],
    )


def add_row(lhs_ref, w_ref, acc, slot, batch):
    rows = lhs_ref.shape[0]
    for a, b in PAIRS:
        y = jnp.dot(lhs_ref[...], w_ref[:, a * LANES : b * LANES], preferred_element_type=F32)
        for t in range(a, b):
            i, j = divmod(t, 3)
            z = y[:, (t - a) * LANES : (t - a + 1) * LANES]
            at = slot + 2 - i
            if j == 0:
                acc[at, batch:] += z[: rows - batch]
            elif j == 1:
                acc[at] += z
            else:
                acc[at, : rows - batch] += z[batch:]


def start_acc(acc, carry_ref):
    for slot in range(acc.shape[0]):
        if carry_ref is not None and slot < 2:
            acc[slot] = carry_ref[slot]
        else:
            acc[slot] = jnp.zeros(acc.shape[1:], F32)


def emitted(r0, count, side):
    first = 0 if r0 == 0 else r0 - 1
    last = side if r0 + count == side else r0 + count - 1
    return first, last, first - (r0 - 1)


def ready_rows(t, r0, count, side):
    r = r0 + t
    rows = [r - 1] if r > 0 else []
    return rows + [r] if r == side - 1 else rows


class Stats:
    def __init__(self, ext, side, batch):
        self.ext, self.side, self.batch = ext, side, batch
        self.ref = None
        zero = jnp.zeros((batch, LANES), F32)
        self.s1, self.s2, self.n = zero, zero, zero

    def row(self, acc, slot, r, low_ref=None):
        batch = self.batch
        if self.ref is None:
            s = n = jnp.zeros((batch, LANES), F32)
            for c in range(self.side):
                m = mask_at(self.ext, r, c)
                s = s + times(acc[slot, c * batch : (c + 1) * batch], m)
                n = n + (1.0 if m is None else m)
            n = jnp.sum(n, axis=0, keepdims=True)
            self.ref = jnp.sum(s, axis=0, keepdims=True) / jnp.maximum(n, 1.0)
        for c in range(self.side):
            m = mask_at(self.ext, r, c)
            d = acc[slot, c * batch : (c + 1) * batch] - self.ref
            if low_ref is not None:
                low_ref[c * batch : (c + 1) * batch] = d.astype(BF16)
            masked = times(d, m)
            self.s1 = self.s1 + masked
            self.s2 = self.s2 + masked * d
            self.n = self.n + (1.0 if m is None else m)

    def store(self, stat_ref, prev_ref, chunk):
        s1, s2, n = (jnp.sum(x, axis=0, keepdims=True) for x in (self.s1, self.s2, self.n))
        safe = jnp.maximum(n, 1.0)
        whole = (self.ref + s1 / safe, s2 - s1 * s1 / safe, n)
        stat_ref[...] = jnp.zeros(stat_ref.shape, F32) if prev_ref is None else prev_ref[...]
        if prev_ref is not None:
            whole = merge_rows(*(prev_ref[k : k + 1] for k in range(3)), *whole)
        for k in range(3):
            stat_ref[k : k + 1] = whole[k]
        stat_ref[3 + chunk : 4 + chunk] = self.ref


def merge_rows(mean_a, m2_a, n_a, mean_b, m2_b, n_b):
    n = n_a + n_b
    safe = jnp.maximum(n, 1.0)
    delta = mean_a - mean_b
    mean = (n_a * mean_a + n_b * mean_b) / safe
    return mean, m2_a + m2_b + delta * delta * (n_a * n_b / safe), n


def conv_images_body(chunk, r0, count, side, batch, blocks, *refs):
    take = Takes(refs)
    place_ref, ext_ref, w_in, x_hbm = take(4)
    carry_ref, prev_ref = take(2) if r0 else (None, None)
    h_ref, stat_ref, low_ref, own_ref = take(4)
    w_ref = take() if r0 == 0 else w_in
    carry_out = None if r0 + count == side else take()
    acc, raw, x_sem = take(3)
    lhs = take(count)
    fetches = [pltpu.make_async_copy(x_hbm.at[r0 + t], raw.at[t], x_sem.at[t]) for t in range(count)]
    fetches[0].start()
    if r0 == 0:
        w_raw, w_sem = take(2)
        taps = [pltpu.make_async_copy(w_in.at[t], w_raw.at[t], w_sem.at[t]) for t in range(TAPS)]
        for copy in taps:
            copy.start()
    for copy in fetches[1:]:
        copy.start()
    ext = ext_ref[...]
    start_acc(acc, carry_ref)
    if r0 == 0:
        for t in range(TAPS):
            taps[t].wait()
            w_ref[:, t * LANES : (t + 1) * LANES] = w_raw[t].astype(BF16)

    mine = pl.ds(pl.multiple_of(place_ref[0] * LANES, LANES), LANES)

    def stage(t):
        fetches[t].wait()
        for c in range(side):
            part = slice(c * batch, (c + 1) * batch)
            m = mask_at(ext, r0 + t, c)
            x = raw[t, part, mine]
            own_ref[t, part] = x if m is None else x * m.astype(BF16)
            for k in range(blocks):
                lanes = slice(k * LANES, (k + 1) * LANES)
                x = raw[t, part, lanes]
                lhs[t][part, lanes] = x if m is None else x * m.astype(BF16)

    first, last, _ = emitted(r0, count, side)
    stats = Stats(ext, side, batch)
    stage(0)
    for t in range(count):
        if t + 1 < count:
            stage(t + 1)
        add_row(lhs[t], w_ref, acc, t, batch)
        for r in ready_rows(t, r0, count, side):
            h_ref[r - first] = acc[r - (r0 - 1)]
            stats.row(acc, r - (r0 - 1), r, low_ref.at[r - first])
    stats.store(stat_ref, prev_ref, chunk)
    if carry_out is not None:
        carry_out[0] = acc[count]
        carry_out[1] = acc[count + 1]


def conv_images(chunk, r0, count, side, batch, place, ext, weights, images, carry, prev):
    pixels, width = side * batch, images.shape[2]
    first, last, _ = emitted(r0, count, side)
    rows = last - first
    ins = [(place, "s"), (ext, "v"), (weights, "v" if r0 else "h"), (images, "h")]
    if r0:
        ins += [(carry, "v"), (prev, "v")]
    outs = [((rows, pixels, LANES), F32, "v"), ((8, LANES), F32, "v"), ((rows, pixels, LANES), BF16, "v")]
    outs.append(((count, pixels, LANES), BF16, "v"))
    if r0 == 0:
        outs.append(((width, TAPS * LANES), BF16, "v"))
    if r0 + count != side:
        outs.append(((2, pixels, LANES), F32, "v"))
    scratch = [pltpu.VMEM((count + 2, pixels, LANES), F32), pltpu.VMEM((count, pixels, width), BF16), DMA((count,))]
    scratch += [pltpu.VMEM((pixels, width), BF16) for _ in range(count)]
    if r0 == 0:
        scratch += [pltpu.VMEM((TAPS, width, LANES), F32), DMA((TAPS,))]
    return call(
        f"conv_one_{r0}",
        functools.partial(conv_images_body, chunk, r0, count, side, batch, width // LANES),
        outs,
        ins,
        scratch,
    )


def conv_active_body(chunk, r0, count, side, batch, blocks, *refs):
    take = Takes(refs)
    place_ref, ext_ref, w_ref = take(3)
    sources, params = take(blocks), take(blocks)
    carry_ref, prev_ref = take(2) if r0 else (None, None)
    h_ref, stat_ref, act_ref = take(3)
    carry_out = None if r0 + count == side else take()
    acc = take()
    lhs = take(count)
    ext = ext_ref[...]
    start_acc(acc, carry_ref)

    def stage(t):
        for k in range(blocks):
            scale, shift = params[k][0:1], params[k][5 + chunk : 6 + chunk]
            for c in range(side):
                part = slice(c * batch, (c + 1) * batch)
                z = sources[k][t, part].astype(F32) * scale + shift
                low = times(gelu(z), mask_at(ext, r0 + t, c)).astype(BF16)
                lhs[t][part, k * LANES : (k + 1) * LANES] = low
                act_ref[t, part, k * LANES : (k + 1) * LANES] = low

    first, last, _ = emitted(r0, count, side)
    stats = Stats(ext, side, batch)
    stage(0)
    for t in range(count):
        if t + 1 < count:
            stage(t + 1)
        add_row(lhs[t], w_ref, acc, t, batch)
        for r in ready_rows(t, r0, count, side):
            h_ref[r - first] = acc[r - (r0 - 1)]
            stats.row(acc, r - (r0 - 1), r)
    stats.store(stat_ref, prev_ref, chunk)
    if carry_out is not None:
        carry_out[0] = acc[count]
        carry_out[1] = acc[count + 1]


def conv_active(chunk, r0, count, side, batch, place, ext, weights, sources, params, carry, prev):
    blocks, pixels = len(sources), side * batch
    width = LANES * blocks
    first, last, _ = emitted(r0, count, side)
    ins = [(place, "s"), (ext, "v"), (weights, "v")] + [(x, "v") for x in sources] + [(p, "v") for p in params]
    if r0:
        ins += [(carry, "v"), (prev, "v")]
    outs = [((last - first, pixels, LANES), F32, "v"), ((8, LANES), F32, "v"), ((count, pixels, width), BF16, "v")]
    if r0 + count != side:
        outs.append(((2, pixels, LANES), F32, "v"))
    scratch = [pltpu.VMEM((count + 2, pixels, LANES), F32)]
    scratch += [pltpu.VMEM((pixels, width), BF16) for _ in range(count)]
    return call(
        f"conv_two_{r0}",
        functools.partial(conv_active_body, chunk, r0, count, side, batch, blocks),
        outs,
        ins,
        scratch,
    )


def conv_back_body(kind, r0, count, side, batch, blocks, h_split, splits, *refs):
    take = Takes(refs)
    ext_ref = take()
    wt_refs = take(blocks)
    sources = [take(blocks) for _ in splits]
    first, last, _ = emitted(r0, count, side)
    active = kind == "active"
    carry_ref = prev_ref = params_ref = None
    if active:
        params_ref = take()
        h_used = sorted({row_place(h_split, r)[0] for r in range(first, last)})
        h_refs = dict(zip(h_used, take(len(h_used))))
    else:
        extras = take(len(h_split))
    if r0:
        carry_ref = take()
        prev_ref = take() if active else None
    out_ref = take()
    sum_ref = take() if active else None
    carry_out = None if r0 + count == side else take()
    acc, w_ref = take(2)
    in_sem, w_sem = take(2)
    lhs = take(3)
    rows, out_sem = (out_ref, None) if active else take(2)
    h_rows, h_sem = take(2) if active else (None, None)
    stores = []
    chunks = [row_place(splits, t) for t in range(count)]
    fetches = [
        [
            pltpu.make_async_copy(
                sources[chunks[t][0]][k].at[t - chunks[t][1]], lhs[t % 3].at[:, k * LANES : (k + 1) * LANES], in_sem.at[t * blocks + k]
            )
            for k in range(blocks)
        ]
        for t in range(count)
    ]
    weights = [
        pltpu.make_async_copy(wt_refs[k], w_ref.at[k * LANES : (k + 1) * LANES], w_sem.at[k]) for k in range(blocks)
    ]
    for copy in weights + fetches[0] + fetches[1]:
        copy.start()
    ext = ext_ref[...]
    start_acc(acc, carry_ref)
    zero = jnp.zeros((batch, LANES), F32)
    total = [zero, zero]
    if active:
        scale, shift, rscale, offset = (params_ref[k : k + 1] for k in range(4))

    def h_fetch(r):
        index, base = row_place(h_split, r)
        return pltpu.make_async_copy(h_refs[index].at[r - base], h_rows.at[r % 3], h_sem.at[r % 3])

    if active:
        for r in range(first, min(first + 2, last)):
            h_fetch(r).start()

    def finish(r):
        slot, k = r - (r0 - 1), r - first
        for c in range(side):
            part = slice(c * batch, (c + 1) * batch)
            m = mask_at(ext, r, c)
            if active:
                h = h_rows[r % 3, part]
                _, slope = gelu_both(h * scale + shift)
                dz = times(acc[slot, part], m) * slope
                rows[k, part] = dz
                total[0] = total[0] + dz
                total[1] = total[1] + dz * (h * rscale + offset)
            else:
                index, base = row_place(h_split, r)
                rows[k, part] = times(extras[index][r - base, part] + acc[slot, part], m)
        if not active:
            stores.append(pltpu.make_async_copy(rows.at[k], out_ref.at[k], out_sem.at[k]))
            stores[-1].start()

    for copy in weights:
        copy.wait()
    ready = []
    for t in range(count + 1):
        if t < count:
            for copy in fetches[t]:
                copy.wait()
            if t + 2 < count:
                for copy in fetches[t + 2]:
                    copy.start()
        for r in ready:
            if active:
                h_fetch(r).wait()
                if r + 2 < last:
                    h_fetch(r + 2).start()
        if t < count:
            add_row(lhs[t % 3], w_ref, acc, t, batch)
        for r in ready:
            finish(r)
        ready = ready_rows(t, r0, count, side) if t < count else []
    if carry_out is not None:
        carry_out[0] = acc[count]
        carry_out[1] = acc[count + 1]
    if active:
        sum_ref[...] = jnp.zeros(sum_ref.shape, F32)
        for k in range(2):
            s = jnp.sum(total[k], axis=0, keepdims=True)
            sum_ref[k : k + 1] = s if prev_ref is None else s + prev_ref[k : k + 1]
    for copy in stores:
        copy.wait()


def conv_back(kind, r0, count, side, batch, ext, weights, sources, extra, params, carry, prev):
    blocks, pixels = len(weights), side * batch
    splits = [x[0].shape[0] for x in sources]
    first, last, _ = emitted(r0, count, side)
    rows = last - first
    active = kind == "active"
    ins = [(ext, "v")] + [(x, "h") for x in weights]
    ins += [(x, "h" if kind == "active" else "a") for chunk in sources for x in chunk]
    h_split = [h.shape[0] for h in extra]
    if active:
        ins.append((params, "v"))
        ins += [(extra[k], "h") for k in sorted({row_place(h_split, r)[0] for r in range(first, last)})]
    else:
        ins += [(x, "v") for x in extra]
    if r0:
        ins.append((carry, "v"))
        if active:
            ins.append((prev, "v"))
    outs = [((rows, pixels, LANES), F32, "v" if active else "h")]
    if active:
        outs.append(((8, LANES), F32, "v"))
    if r0 + count != side:
        outs.append(((2, pixels, LANES), F32, "v"))
    scratch = [pltpu.VMEM((count + 2, pixels, LANES), F32), pltpu.VMEM((blocks * LANES, TAPS * LANES), BF16)]
    scratch += [DMA((count * blocks,)), DMA((blocks,))]
    scratch += [pltpu.VMEM((pixels, blocks * LANES), BF16) for _ in range(3)]
    if active:
        scratch += [pltpu.VMEM((3, pixels, LANES), F32), DMA((3,))]
    else:
        scratch += [pltpu.VMEM((rows, pixels, LANES), F32), DMA((rows,))]
    return call(
        f"back_{kind}_{r0}",
        functools.partial(conv_back_body, kind, r0, count, side, batch, blocks, h_split, splits),
        outs,
        ins,
        scratch,
    )


def weight_grad_body(kind, side, batch, blocks, splits, ways, *refs):
    take = Takes(refs)
    place_ref, ext_ref = take(2)
    x_refs, g_refs = take(len(splits[0])), take(len(splits[1]))
    keep_ref, *send_refs = take(ways)
    acc, gs, masked = take(3)
    raw, x_sem = take(2) if kind == "images" else (None, None)
    mine = place_ref[1]
    rows = side * batch
    def fetch(r):
        slot = lax.rem(r, 3)
        return pltpu.make_async_copy(x_refs[0].at[r], raw.at[slot], x_sem.at[slot])

    if kind == "images":
        fetch(0).start()
        fetch(1).start()
    ext = ext_ref[...]
    gs[0] = jnp.zeros((rows, LANES), BF16)
    gs[side + 1] = jnp.zeros((rows, LANES), BF16)
    for r in range(side):
        index, base = row_place(splits[1], r)
        gs[r + 1] = g_refs[index][r - base]
    acc[...] = jnp.zeros(acc.shape, F32)
    edge = jnp.zeros((batch, LANES), BF16)
    for start, stop, ((xi, xb),) in segments(splits[0]):

        @pl.loop(start, stop)
        def _(r, xi=xi, xb=xb):
            if kind == "images":

                @pl.when(r + 2 < side)
                def _():
                    fetch(r + 2).start()

                fetch(r).wait()
                for c in range(side):
                    part = slice(c * batch, (c + 1) * batch)
                    m = mask_at(ext, r, c).astype(BF16)
                    for k in range(blocks):
                        lanes = slice(k * LANES, (k + 1) * LANES)
                        masked[part, lanes] = raw[lax.rem(r, 3), part, lanes] * m
                x = masked[...]
            else:
                x = x_refs[xi][r - xb]
            parts = []
            for i in range(3):
                g = gs[r + 2 - i]
                parts.append(jnp.concatenate([g[batch:], edge], axis=0))
                parts.append(g)
                parts.append(jnp.concatenate([edge, g[: rows - batch]], axis=0))
            wide = jnp.concatenate(parts, axis=1)
            acc[...] += lax.dot_general(x, wide, (((0,), (0,)), ((), ())), preferred_element_type=F32)

    share = TAPS * blocks // ways
    for t in range(TAPS):
        for k in range(blocks):
            unit, lanes = t * blocks + k, slice(t * LANES, (t + 1) * LANES)
            if kind == "images":
                value = acc[k * LANES : (k + 1) * LANES, lanes]
            else:
                other = jnp.bitwise_xor(place_ref[0], k)
                value = acc[pl.ds(pl.multiple_of(other * LANES, LANES), LANES), lanes]
            at = slice(unit % share * LANES, (unit % share + 1) * LANES)
            distance = jnp.bitwise_xor(mine, unit // share)

            @pl.when(distance == 0)
            def _(value=value, at=at):
                keep_ref[at] = value

            for d in range(1, ways):

                @pl.when(distance == d)
                def _(value=value, at=at, d=d):
                    send_refs[d - 1][at] = value.astype(BF16)


def weight_grad(kind, place, ext, xs, gs, ways, side, batch):
    width, pixels = xs[0].shape[2], side * batch
    blocks = width // LANES
    splits = ([x.shape[0] for x in xs], [g.shape[0] for g in gs])
    share = TAPS * width // ways
    return call(
        f"wgrad_{kind}",
        functools.partial(weight_grad_body, kind, side, batch, blocks, splits, ways),
        [((share, LANES), F32, "v")] + [((share, LANES), BF16, "v")] * (ways - 1),
        [(place, "s"), (ext, "v")] + [(x, "h" if kind == "images" else "v") for x in xs] + [(g, "v") for g in gs],
        [
            pltpu.VMEM((width, TAPS * LANES), F32),
            pltpu.VMEM((side + 2, pixels, LANES), BF16),
            pltpu.VMEM((pixels, width), BF16),
        ]
        + ([pltpu.VMEM((3, pixels, width), BF16), DMA((3,))] if kind == "images" else []),
    )


def block_end_body(side, batch, split, own_split, grad_split, *refs):
    take = Takes(refs)
    ext_ref, params_ref, cot_ref = take(3)
    h_refs, own_refs = take(len(split)), take(len(own_split))
    out_hbm = take()
    grad_refs = take(len(grad_split))
    sum_ref, outs, sems = take(3)
    ext = ext_ref[...]
    scale, shift, rscale, offset = (params_ref[k : k + 1] for k in range(4))
    zero = jnp.zeros((batch, LANES), F32)
    total = (zero, zero)

    def store(r):
        return pltpu.make_async_copy(outs.at[r], out_hbm.at[r], sems.at[r])

    for start, stop, ((index, base), (wi, wb), (gi, gb)) in segments(split, own_split, grad_split):

        def one(r, carry, index=index, base=base, wi=wi, wb=wb, gi=gi, gb=gb):
            ds, dn = carry
            for c in range(side):
                part = slice(c * batch, (c + 1) * batch)
                m = mask_at(ext, r, c)
                h = h_refs[index][r - base, part]
                value, slope = gelu_both(h * scale + shift + own_refs[wi][r - wb, part].astype(F32))
                outs[r, part] = (value * m).astype(BF16)
                dz = cot_ref[r, part].astype(F32) * m * slope
                grad_refs[gi][r - gb, part] = dz
                ds = ds + dz
                dn = dn + dz * (h * rscale + offset)
            store(r).start()
            return ds, dn

        total = lax.fori_loop(start, stop, one, total)
    sum_ref[...] = jnp.zeros(sum_ref.shape, F32)
    sum_ref[0:1] = jnp.sum(total[0], axis=0, keepdims=True)
    sum_ref[1:2] = jnp.sum(total[1], axis=0, keepdims=True)
    for r in range(side):
        store(r).wait()


def block_end(ext, params, cotangent, hs, owns, grad_split, side, batch):
    pixels = side * batch
    shape = (side, pixels, LANES)
    split, own_split = [h.shape[0] for h in hs], [x.shape[0] for x in owns]
    outs = [(shape, BF16, "h")] + [((n, pixels, LANES), F32, "v") for n in grad_split] + [((8, LANES), F32, "v")]
    return call(
        "block_end",
        functools.partial(block_end_body, side, batch, split, own_split, grad_split),
        outs,
        [(ext, "v"), (params, "v"), (cotangent, "v")] + [(x, "v") for x in list(hs) + list(owns)],
        [pltpu.VMEM(shape, BF16), DMA((side,))],
    )


def norm_back_body(side, batch, far_h, splits, *refs):
    take = Takes(refs)
    ext_ref, params_ref, sums_ref = take(3)
    h_refs, dz_refs, out_refs = (take(len(s)) for s in splits)
    gain_ref, shift_ref = take(2)
    if far_h:
        h_rows, h_sem = take(2)
        for r in range(side):
            index, base = row_place(splits[0], r)
            pltpu.make_async_copy(h_refs[index].at[r - base], h_rows.at[r], h_sem.at[r]).start()
    ext = ext_ref[...]
    scale, _, rscale, offset, n = (params_ref[k : k + 1] for k in range(5))
    shift_ref[...] = sums_ref[0:1]
    gain_ref[...] = sums_ref[1:2]
    shift_grad, gain_grad = sums_ref[0:1] / n, sums_ref[1:2] / n
    b = scale * rscale * gain_grad
    c0 = scale * (shift_grad + offset * gain_grad)
    for start, stop, ((hi, hb), (zi, zb), (oi, ob)) in segments(*splits):

        @pl.loop(start, stop)
        def _(r, hi=hi, hb=hb, zi=zi, zb=zb, oi=oi, ob=ob):
            if far_h:
                pltpu.make_async_copy(h_refs[hi].at[r - hb], h_rows.at[r], h_sem.at[r]).wait()
            for c in range(side):
                part = slice(c * batch, (c + 1) * batch)
                m = mask_at(ext, r, c)
                h = h_rows[r, part] if far_h else h_refs[hi][r - hb, part]
                grad = scale * dz_refs[zi][r - zb, part] - (h * b + c0)
                out_refs[oi][r - ob, part] = (m * grad).astype(BF16)


def norm_back(ext, params, sums, hs, dzs, flow, far_h, side, batch):
    splits = ([h.shape[0] for h in hs], [z.shape[0] for z in dzs], list(flow))
    return call(
        "norm_back",
        functools.partial(norm_back_body, side, batch, far_h, splits),
        [((n, side * batch, LANES), BF16, "v") for n in flow] + [((1, LANES), F32, "v")] * 2,
        [(ext, "v"), (params, "v"), (sums, "v")] + [(x, "h" if far_h else "v") for x in hs] + [(x, "v") for x in dzs],
        [pltpu.VMEM((side, side * batch, LANES), F32), DMA((side,))] if far_h else [],
    )


def as_rows(values):
    row = lax.broadcasted_iota(jnp.int32, (8, LANES), 0)
    out = jnp.zeros((8, LANES), F32)
    for k, value in enumerate(values):
        out = jnp.where(row == k, value, out)
    return out


def merge(a, b):
    merged = merge_rows(*(a[k : k + 1] for k in range(3)), *(b[k : k + 1] for k in range(3)))
    return as_rows(list(merged) + [a[k : k + 1] for k in range(3, 6)])


def affine(a, gain, shift):
    center, n = a[0:1], a[2:3]
    rscale = lax.rsqrt(a[1:2] / n + EPSILON)
    scale = rscale * gain
    rows = [scale, shift - center * scale, rscale, -center * rscale, n]
    return as_rows(rows + [(a[3 + q : 4 + q] - center) * scale + shift for q in range(3)])


def swap(x, axis, size, k):
    return lax.ppermute(x, axis, [(i, i ^ k) for i in range(size)])


def after(x, *others):
    return lax.optimization_barrier((x,) + others)[0]


class Sum:
    def __init__(self, x, size, add=None):
        self.x, self.size, self.k = x, size, 1
        self.add = add or (lambda a, b: a + b)

    def step(self, start=(), end=()):
        if self.k < self.size:
            x = after(self.x, *start) if start else self.x
            other = swap(x, "dp", self.size, self.k)
            self.x = self.add(self.x, after(other, *end) if end else other)
            self.k *= 2
        return self.x

    def end(self):
        while self.k < self.size:
            self.step()
        return self.x


class Scatter:
    def __init__(self, keep, sends, size, index):
        self.keep, self.sends, self.size, self.index = keep, sends, size, index
        self.k = None

    def step(self, start=(), end=()):
        if self.k is None:
            sends = self.sends
            if start:
                sends = lax.optimization_barrier(tuple(sends) + tuple(start))[: len(sends)]
            others = tuple(swap(x, "dp", self.size, d + 1) for d, x in enumerate(sends))
            if end:
                others = lax.optimization_barrier(others + tuple(end))[: len(sends)]
            for other in others:
                self.keep = self.keep + other.astype(F32)
            self.k = len(sends) + 1
        elif self.k < self.size:
            half = self.keep.shape[0] // 2
            low, high = self.keep[:half], self.keep[half:]
            upper = (self.index // self.k) % 2 == 1
            send = jnp.where(upper, low, high).astype(BF16)
            other = swap(after(send, *start) if start else send, "dp", self.size, self.k)
            self.keep = jnp.where(upper, high, low) + (after(other, *end) if end else other).astype(F32)
            self.k *= 2
        return self.keep

    def end(self):
        while self.k is None or self.k < self.size:
            self.step()
        return self.keep


class Gather:
    def __init__(self, part, size, ways, index, at_once):
        self.x, self.size, self.ways, self.index, self.at_once = part.astype(BF16), size, ways, index, at_once
        self.ks, k = [], size
        while k > ways:
            k //= 2
            self.ks.append(k)
        if at_once:
            self.ks.append(0)
        else:
            while k > 1:
                k //= 2
                self.ks.append(ways // (2 * k))

    def step(self, start=(), end=()):
        if not self.ks:
            return self.x
        x = after(self.x, *start) if start else self.x
        k = self.ks.pop(0)
        if k:
            other = swap(x, "dp", self.size, k)
            other = after(other, *end) if end else other
            upper = (self.index // k) % 2 == 1
            self.x = jnp.where(upper, jnp.concatenate([other, self.x]), jnp.concatenate([self.x, other]))
        else:
            others = tuple(swap(x, "dp", self.size, d) for d in range(1, self.ways))
            if end:
                others = lax.optimization_barrier(others + tuple(end))[: self.ways - 1]
            self.others = others
        return self.x

    def end(self, *late):
        while self.ks:
            self.step()
        if self.at_once:
            others = lax.optimization_barrier(self.others + late)[: self.ways - 1] if late else self.others
            mine = self.index % self.ways
            self.x = jnp.concatenate([lax.select_n(mine ^ j, self.x, *others) for j in range(self.ways)])
        return self.x.astype(F32)


class Blocks:
    def __init__(self, x, size, late=False):
        self.own, self.size = x, size
        self.far = swap(x, "chan", size, 2)
        self.near = None if late else swap(x, "chan", size, 1)

    def end(self, *others):
        if self.near is None:
            self.near = swap(after(self.own, *others), "chan", self.size, 1)
        far = after(self.far, *others) if others else self.far
        return [self.own, self.near, far, swap(far, "chan", self.size, 1)]


def sum_chan(x, size):
    k = 1
    while k < size:
        x = x + swap(x, "chan", size, k)
        k *= 2
    return x


def moment_step(weight, grad, moment, weight_norm, grad_norm):
    trust = TRUST_COEF * weight_norm / (grad_norm + DECAY * weight_norm)
    return MOMENTUM * moment + LEARN_RATE * trust * (grad + DECAY * weight)


def shards(
    dp, ch, images, groups, cotangent, weight_one, gain_one, shift_one, weight_two, gain_two, shift_two, moment_one, moment_two
):
    batch, side, _, width = images.shape
    pixels = side * batch
    images = jnp.transpose(images, (1, 2, 0, 3)).reshape(side, pixels, width)
    cotangent = jnp.transpose(cotangent, (1, 2, 0, 3)).reshape(side, pixels, LANES)
    chan, index = lax.axis_index("chan").astype(jnp.int32), lax.axis_index("dp").astype(jnp.int32)
    ways = min(4, dp)
    place = jnp.stack([chan, index % ways])
    ext = jnp.broadcast_to((5 + 2 * groups)[:, None], (batch, LANES))
    third = side // 3
    conv_in = (third + 1, third, side - 2 * third - 1)
    flow = (third, third, side - 2 * third)
    sizes = (side, batch)

    gains = [g.reshape(1, LANES) for g in (gain_one, shift_one, gain_two, shift_two)]

    low, h_one, owns, carry, stat, weights, r0 = [], [], [], None, None, weight_one, 0
    for q, count in enumerate(conv_in):
        out = conv_images(q, r0, count, *sizes, place, ext, weights, images, carry, stat)
        h, stat, chunk, own = out[:4]
        if q == 0:
            weights = out[4]
        carry = out[-1]
        h_one.append(h)
        owns.append(own)
        low.append(Blocks(chunk, ch))
        r0 += count
    wb_two, squares, *wt = prep(weight_one, weight_two, place)
    total = Sum(stat, dp, merge)
    total.step(start=(low[0].far,))
    total.step(start=(squares,))
    total.step(start=(low[1].far,))
    params_one = affine(total.end(), *gains[:2])
    params = Blocks(params_one, ch).end()

    h_two, act, carry, stat, r0 = [], [], None, None, 0
    for q, count in enumerate(flow):
        out = conv_active(q, r0, count, *sizes, place, ext, wb_two, low[q].end(), params, carry, stat)
        h, stat, rows = out[:3]
        if q == 0:
            wt_two = [after(w, stat) for w in wt[ch:]]
            wt_two = [wt_two[0]] + [swap(wt_two[k], "chan", ch, k) for k in range(1, ch)]
        h_two.append(h)
        act.append(rows)
        carry = out[-1]
        r0 += count
    params_two = affine(Sum(stat, dp, merge).end(), *gains[2:])

    out = block_end(ext, params_two, cotangent, h_two, owns, (side,), *sizes)
    block_output, grad_pre, sums = out
    sums_two = Sum(sums, dp).end()
    *grad_two, gain_two_grad, shift_two_grad = norm_back(ext, params_two, after(sums_two, *wt_two[1:]), h_two, [grad_pre], (side,), False, *sizes)
    gathered = Blocks(grad_two[0], ch, True)
    keep, *sends = weight_grad("act", place, ext, act, grad_two, ways, *sizes)
    scatter = Scatter(keep, sends, dp, index)
    scatter.step()
    sources = gathered.end(scatter.keep)
    wt_one = [after(w, scatter.keep) for w in wt[:ch]]
    wt_one = [wt_one[0]] + [swap(wt_one[k], "chan", ch, k) for k in range(1, ch)]
    dz_one, sums = conv_back("active", 0, side, *sizes, ext, wt_two, [sources], h_one, params_one, None, None)
    scatter.step(end=(sums,))
    part_two = scatter.end()
    gather_two = Gather(part_two, dp, ways, index, True)
    total = Sum(sums, dp)
    total.step(start=tuple(wt_one[2:]))
    gather_two.step()
    sums_one = total.end()
    split = (third + 1, side - third - 1)
    *grad_one, gain_one_grad, shift_one_grad = norm_back(ext, params_one, after(sums_one, gather_two.x, *wt_one[1:]), h_one, [dz_one], split, True, *sizes)
    gathered = [Blocks(g, ch, True) for g in grad_one]
    keep, *sends = weight_grad("images", place, ext, [images], grad_one, ways, *sizes)
    gather_two.step(start=(grad_one[0],), end=(keep,))
    scatter = Scatter(keep, sends, dp, index)
    scatter.step(start=(gathered[0].far,))
    sources = [g.end(scatter.keep) for g in gathered]
    weight_two_grad = gather_two.end().reshape(weight_two.shape)
    squares = jnp.sum(squares, axis=1)
    norms = jnp.sqrt(sum_chan(jnp.stack([squares[0], squares[1], jnp.sum(weight_two_grad * weight_two_grad)]), ch))
    part_one = scatter.end()
    gather_one = Gather(part_one, dp, ways, index, True)
    moment_two_new = moment_step(weight_two, weight_two_grad, moment_two, norms[1], norms[2])
    gather_one.step(end=(moment_two_new,))
    input_grad = conv_back(
        "input", 0, side, *sizes, after(ext, gather_one.x), wt_one, sources, [grad_pre], None, None, None
    )[0]
    gather_one.step(end=(input_grad,))
    weight_one_grad = gather_one.end().reshape(weight_one.shape)
    norm_one = jnp.sqrt(sum_chan(jnp.sum(weight_one_grad * weight_one_grad).reshape(1), ch))
    weight_norms = norms[:2]
    grad_norms = jnp.concatenate([norm_one, norms[2:]])
    moment_one_new = moment_step(weight_one, weight_one_grad, moment_one, norms[0], norm_one[0])

    def as_images(x):
        return jnp.transpose(x.reshape(side, side, batch, LANES), (2, 0, 1, 3))

    return (
        as_images(block_output),
        as_images(input_grad),
        weight_one_grad,
        gain_one_grad.reshape(LANES),
        shift_one_grad.reshape(LANES),
        weight_two_grad,
        gain_two_grad.reshape(LANES),
        shift_two_grad.reshape(LANES),
        moment_one_new,
        moment_two_new,
        weight_norms,
        grad_norms,
    )


def solution(mesh):
    full, rows, both = P("dp", None, None, None), P("dp"), P("dp", None, None, "chan")
    weight, channel = P(None, None, "chan"), P("chan")
    return jax.shard_map(
        functools.partial(shards, mesh.shape["dp"], mesh.shape["chan"]),
        mesh=mesh,
        in_specs=(full, rows, both, weight, channel, channel, weight, channel, channel, weight, weight),
        out_specs=(both, both, weight, channel, channel, weight, channel, channel, weight, weight, P(), P()),
        check_vma=False,
    )
```

```python
import functools

import jax
import jax.numpy as jnp
from jax import lax
from jax.experimental import pallas as pl
from jax.experimental.pallas import tpu as pltpu
from jax.sharding import PartitionSpec as P

EPSILON = 1e-05
MOMENTUM = 0.9
LEARN_RATE = 8.0
TRUST_COEF = 0.001
DECAY = 5e-05
GELU_A = 0.7978845608028654
GELU_B = 0.7978845608028654 * 0.044715
F32 = jnp.float32
BF16 = jnp.bfloat16
LANES = 128
TAPS = 9
PAIRS = ((0, 2), (2, 4), (4, 6), (6, 8), (8, 9))
VMEM_LEAST = 12 * 1024 * 1024
VMEM_OPERANDS = 7 * 1024 * 1024
DMA = pltpu.SemaphoreType.DMA


def mask_at(ext, r, c):
    if isinstance(r, int) and max(r, c) < 5:
        return None
    return jnp.where(ext > jnp.maximum(r, c), 1.0, 0.0).astype(F32)


def times(x, m):
    return x if m is None else x * m


def gelu(v):
    t = jnp.tanh(v * (GELU_A + GELU_B * (v * v)))
    half = 0.5 * v
    return half + half * t


def gelu_both(v):
    sq = v * v
    t = jnp.tanh(v * (GELU_A + GELU_B * sq))
    half = 0.5 * v
    value = half + half * t
    slope = 0.5 + 0.5 * t + (half - half * (t * t)) * (GELU_A + (3.0 * GELU_B) * sq)
    return value, slope


def call(name, body, outs, ins, scratch=(), aliases=None):
    spec = {
        "a": pl.BlockSpec(memory_space=pl.ANY),
        "v": pl.BlockSpec(memory_space=pltpu.VMEM),
        "h": pl.BlockSpec(memory_space=pltpu.HBM),
        "s": pl.BlockSpec(memory_space=pltpu.SMEM),
    }
    return pl.pallas_call(
        body,
        name=name,
        out_shape=[jax.ShapeDtypeStruct(s, d) for s, d, _ in outs],
        in_specs=[spec[w] for _, w in ins],
        out_specs=[spec[w] for _, _, w in outs],
        scratch_shapes=list(scratch),
        input_output_aliases=aliases or {},
        compiler_params=pltpu.CompilerParams(vmem_limit_bytes=max(VMEM_LEAST, VMEM_OPERANDS + room(scratch))),
        cost_estimate=pl.CostEstimate(flops=0, bytes_accessed=0, transcendentals=0),
    )(*[pltpu.with_memory_space_constraint(x, pltpu.HBM) if w == "h" else x for x, w in ins])


def segments(*splits):
    ends = sorted({sum(s[: k + 1]) for s in splits for k in range(len(s))})
    result, start = [], 0
    for end in ends:
        result.append((start, end, [row_place(s, start) for s in splits]))
        start = end
    return result


def row_place(split, r):
    at = 0
    for index, size in enumerate(split):
        if r < at + size:
            return index, at
        at += size


def room(scratch):
    total = 0
    for x in scratch:
        if hasattr(x, "memory_space") and x.memory_space == pltpu.VMEM:
            size = jnp.dtype(x.dtype).itemsize
            for n in x.shape:
                size *= n
            total += size
    return total


class Takes:
    def __init__(self, refs):
        self.refs = list(refs)

    def __call__(self, n=None):
        if n is None:
            return self.refs.pop(0)
        return [self.refs.pop(0) for _ in range(n)]


def prep_body(blocks, chan_ref, one_ref, two_ref, wb_ref, sq_ref, *wt_refs):
    chan = chan_ref[0]
    sq_ref[...] = jnp.zeros(sq_ref.shape, F32)
    for layer, w_ref in enumerate((one_ref, two_ref)):
        total = jnp.zeros((1, LANES), F32)
        for k in range(blocks):
            rows = pl.ds(pl.multiple_of(jnp.bitwise_xor(chan, k) * LANES, LANES), LANES)
            for t in range(TAPS):
                piece = w_ref[t, rows, :]
                total = total + jnp.sum(piece * piece, axis=0, keepdims=True)
                if layer:
                    wb_ref[k * LANES : (k + 1) * LANES, t * LANES : (t + 1) * LANES] = piece.astype(BF16)
                flip = TAPS - 1 - t
                wt_refs[layer * blocks + k][:, flip * LANES : (flip + 1) * LANES] = piece.T.astype(BF16)
        sq_ref[layer : layer + 1] = total


def prep(weight_one, weight_two, chan):
    width = weight_one.shape[1]
    blocks = width // LANES
    return call(
        "prep",
        functools.partial(prep_body, blocks),
        [
            ((width, TAPS * LANES), BF16, "v"),
            ((8, LANES), F32, "v"),
        ]
        + [((LANES, TAPS * LANES), BF16, "v")] * (2 * blocks),
        [(chan, "s"), (weight_one, "v"), (weight_two, "v")],
    )


def add_row(lhs_ref, w_ref, acc, slot, batch):
    rows = lhs_ref.shape[0]
    for a, b in PAIRS:
        y = jnp.dot(lhs_ref[...], w_ref[:, a * LANES : b * LANES], preferred_element_type=F32)
        for t in range(a, b):
            i, j = divmod(t, 3)
            z = y[:, (t - a) * LANES : (t - a + 1) * LANES]
            at = slot + 2 - i
            if j == 0:
                acc[at, batch:] += z[: rows - batch]
            elif j == 1:
                acc[at] += z
            else:
                acc[at, : rows - batch] += z[batch:]


def start_acc(acc, carry_ref):
    for slot in range(acc.shape[0]):
        if carry_ref is not None and slot < 2:
            acc[slot] = carry_ref[slot]
        else:
            acc[slot] = jnp.zeros(acc.shape[1:], F32)


def emitted(r0, count, side):
    first = 0 if r0 == 0 else r0 - 1
    last = side if r0 + count == side else r0 + count - 1
    return first, last, first - (r0 - 1)


def ready_rows(t, r0, count, side):
    r = r0 + t
    rows = [r - 1] if r > 0 else []
    return rows + [r] if r == side - 1 else rows


class Stats:
    def __init__(self, ext, side, batch):
        self.ext, self.side, self.batch = ext, side, batch
        self.ref = None
        zero = jnp.zeros((batch, LANES), F32)
        self.s1, self.s2, self.n = zero, zero, zero

    def row(self, acc, slot, r, low_ref=None):
        batch = self.batch
        if self.ref is None:
            s = n = jnp.zeros((batch, LANES), F32)
            for c in range(self.side):
                m = mask_at(self.ext, r, c)
                s = s + times(acc[slot, c * batch : (c + 1) * batch], m)
                n = n + (1.0 if m is None else m)
            n = jnp.sum(n, axis=0, keepdims=True)
            self.ref = jnp.sum(s, axis=0, keepdims=True) / jnp.maximum(n, 1.0)
        for c in range(self.side):
            m = mask_at(self.ext, r, c)
            d = acc[slot, c * batch : (c + 1) * batch] - self.ref
            if low_ref is not None:
                low_ref[c * batch : (c + 1) * batch] = d.astype(BF16)
            masked = times(d, m)
            self.s1 = self.s1 + masked
            self.s2 = self.s2 + masked * d
            self.n = self.n + (1.0 if m is None else m)

    def store(self, stat_ref, prev_ref, chunk):
        s1, s2, n = (jnp.sum(x, axis=0, keepdims=True) for x in (self.s1, self.s2, self.n))
        safe = jnp.maximum(n, 1.0)
        whole = (self.ref + s1 / safe, s2 - s1 * s1 / safe, n)
        stat_ref[...] = jnp.zeros(stat_ref.shape, F32) if prev_ref is None else prev_ref[...]
        if prev_ref is not None:
            whole = merge_rows(*(prev_ref[k : k + 1] for k in range(3)), *whole)
        for k in range(3):
            stat_ref[k : k + 1] = whole[k]
        stat_ref[3 + chunk : 4 + chunk] = self.ref


def merge_rows(mean_a, m2_a, n_a, mean_b, m2_b, n_b):
    n = n_a + n_b
    safe = jnp.maximum(n, 1.0)
    delta = mean_a - mean_b
    mean = (n_a * mean_a + n_b * mean_b) / safe
    return mean, m2_a + m2_b + delta * delta * (n_a * n_b / safe), n


def conv_images_body(chunk, r0, count, side, batch, blocks, *refs):
    take = Takes(refs)
    place_ref, ext_ref, w_in, x_hbm = take(4)
    carry_ref, prev_ref = take(2) if r0 else (None, None)
    h_ref, stat_ref, low_ref, own_ref = take(4)
    w_ref = take() if r0 == 0 else w_in
    carry_out = None if r0 + count == side else take()
    acc, raw, x_sem = take(3)
    lhs = take(count)
    fetches = [pltpu.make_async_copy(x_hbm.at[r0 + t], raw.at[t], x_sem.at[t]) for t in range(count)]
    fetches[0].start()
    if r0 == 0:
        w_raw, w_sem = take(2)
        taps = [pltpu.make_async_copy(w_in.at[t], w_raw.at[t], w_sem.at[t]) for t in range(TAPS)]
        for copy in taps:
            copy.start()
    for copy in fetches[1:]:
        copy.start()
    ext = ext_ref[...]
    start_acc(acc, carry_ref)
    if r0 == 0:
        for t in range(TAPS):
            taps[t].wait()
            w_ref[:, t * LANES : (t + 1) * LANES] = w_raw[t].astype(BF16)

    mine = pl.ds(pl.multiple_of(place_ref[0] * LANES, LANES), LANES)

    def stage(t):
        fetches[t].wait()
        for c in range(side):
            part = slice(c * batch, (c + 1) * batch)
            m = mask_at(ext, r0 + t, c)
            x = raw[t, part, mine]
            own_ref[t, part] = x if m is None else x * m.astype(BF16)
            for k in range(blocks):
                lanes = slice(k * LANES, (k + 1) * LANES)
                x = raw[t, part, lanes]
                lhs[t][part, lanes] = x if m is None else x * m.astype(BF16)

    first, last, _ = emitted(r0, count, side)
    stats = Stats(ext, side, batch)
    stage(0)
    for t in range(count):
        if t + 1 < count:
            stage(t + 1)
        add_row(lhs[t], w_ref, acc, t, batch)
        for r in ready_rows(t, r0, count, side):
            h_ref[r - first] = acc[r - (r0 - 1)]
            stats.row(acc, r - (r0 - 1), r, low_ref.at[r - first])
    stats.store(stat_ref, prev_ref, chunk)
    if carry_out is not None:
        carry_out[0] = acc[count]
        carry_out[1] = acc[count + 1]


def conv_images(chunk, r0, count, side, batch, place, ext, weights, images, carry, prev):
    pixels, width = side * batch, images.shape[2]
    first, last, _ = emitted(r0, count, side)
    rows = last - first
    ins = [(place, "s"), (ext, "v"), (weights, "v" if r0 else "h"), (images, "h")]
    if r0:
        ins += [(carry, "v"), (prev, "v")]
    outs = [((rows, pixels, LANES), F32, "v"), ((8, LANES), F32, "v"), ((rows, pixels, LANES), BF16, "v")]
    outs.append(((count, pixels, LANES), BF16, "v"))
    if r0 == 0:
        outs.append(((width, TAPS * LANES), BF16, "v"))
    if r0 + count != side:
        outs.append(((2, pixels, LANES), F32, "v"))
    scratch = [pltpu.VMEM((count + 2, pixels, LANES), F32), pltpu.VMEM((count, pixels, width), BF16), DMA((count,))]
    scratch += [pltpu.VMEM((pixels, width), BF16) for _ in range(count)]
    if r0 == 0:
        scratch += [pltpu.VMEM((TAPS, width, LANES), F32), DMA((TAPS,))]
    return call(
        f"conv_one_{r0}",
        functools.partial(conv_images_body, chunk, r0, count, side, batch, width // LANES),
        outs,
        ins,
        scratch,
    )


def conv_active_body(chunk, r0, count, side, batch, blocks, *refs):
    take = Takes(refs)
    place_ref, ext_ref, w_ref = take(3)
    sources, params = take(blocks), take(blocks)
    carry_ref, prev_ref = take(2) if r0 else (None, None)
    h_ref, stat_ref, act_ref = take(3)
    carry_out = None if r0 + count == side else take()
    acc = take()
    lhs = take(count)
    ext = ext_ref[...]
    start_acc(acc, carry_ref)

    def stage(t):
        for k in range(blocks):
            scale, shift = params[k][0:1], params[k][5 + chunk : 6 + chunk]
            for c in range(side):
                part = slice(c * batch, (c + 1) * batch)
                z = sources[k][t, part].astype(F32) * scale + shift
                low = times(gelu(z), mask_at(ext, r0 + t, c)).astype(BF16)
                lhs[t][part, k * LANES : (k + 1) * LANES] = low
                act_ref[t, part, k * LANES : (k + 1) * LANES] = low

    first, last, _ = emitted(r0, count, side)
    stats = Stats(ext, side, batch)
    stage(0)
    for t in range(count):
        if t + 1 < count:
            stage(t + 1)
        add_row(lhs[t], w_ref, acc, t, batch)
        for r in ready_rows(t, r0, count, side):
            h_ref[r - first] = acc[r - (r0 - 1)]
            stats.row(acc, r - (r0 - 1), r)
    stats.store(stat_ref, prev_ref, chunk)
    if carry_out is not None:
        carry_out[0] = acc[count]
        carry_out[1] = acc[count + 1]


def conv_active(chunk, r0, count, side, batch, place, ext, weights, sources, params, carry, prev):
    blocks, pixels = len(sources), side * batch
    width = LANES * blocks
    first, last, _ = emitted(r0, count, side)
    ins = [(place, "s"), (ext, "v"), (weights, "v")] + [(x, "v") for x in sources] + [(p, "v") for p in params]
    if r0:
        ins += [(carry, "v"), (prev, "v")]
    outs = [((last - first, pixels, LANES), F32, "v"), ((8, LANES), F32, "v"), ((count, pixels, width), BF16, "v")]
    if r0 + count != side:
        outs.append(((2, pixels, LANES), F32, "v"))
    scratch = [pltpu.VMEM((count + 2, pixels, LANES), F32)]
    scratch += [pltpu.VMEM((pixels, width), BF16) for _ in range(count)]
    return call(
        f"conv_two_{r0}",
        functools.partial(conv_active_body, chunk, r0, count, side, batch, blocks),
        outs,
        ins,
        scratch,
    )


def conv_back_body(kind, r0, count, side, batch, blocks, h_split, splits, *refs):
    take = Takes(refs)
    ext_ref = take()
    wt_refs = take(blocks)
    sources = [take(blocks) for _ in splits]
    first, last, _ = emitted(r0, count, side)
    active = kind == "active"
    carry_ref = prev_ref = params_ref = None
    if active:
        params_ref = take()
        h_used = sorted({row_place(h_split, r)[0] for r in range(first, last)})
        h_refs = dict(zip(h_used, take(len(h_used))))
    else:
        extras = take(len(h_split))
    if r0:
        carry_ref = take()
        prev_ref = take()
    out_ref = take()
    sum_ref = take() if active else None
    carry_out = None if r0 + count == side else take()
    acc, w_ref = take(2)
    in_sem, w_sem = take(2)
    lhs = take(3)
    rows, out_sem = (out_ref, None) if active else take(2)
    h_rows, h_sem = take(2) if active else (None, None)
    stores = []
    chunks = [row_place(splits, t) for t in range(count)]
    fetches = [
        [
            pltpu.make_async_copy(
                sources[chunks[t][0]][k].at[t - chunks[t][1]], lhs[t % 3].at[:, k * LANES : (k + 1) * LANES], in_sem.at[t * blocks + k]
            )
            for k in range(blocks)
        ]
        for t in range(count)
    ]
    weights = [
        pltpu.make_async_copy(wt_refs[k], w_ref.at[k * LANES : (k + 1) * LANES], w_sem.at[k]) for k in range(blocks)
    ]
    for copy in weights + fetches[0] + fetches[1]:
        copy.start()
    ext = ext_ref[...]
    start_acc(acc, carry_ref)
    zero = jnp.zeros((batch, LANES), F32)
    total = [zero, zero]
    if active:
        scale, shift, rscale, offset = (params_ref[k : k + 1] for k in range(4))

    def h_fetch(r):
        index, base = row_place(h_split, r)
        return pltpu.make_async_copy(h_refs[index].at[r - base], h_rows.at[r % 3], h_sem.at[r % 3])

    if active:
        for r in range(first, min(first + 2, last)):
            h_fetch(r).start()

    def finish(r):
        slot, k = r - (r0 - 1), r - first
        for c in range(side):
            part = slice(c * batch, (c + 1) * batch)
            m = mask_at(ext, r, c)
            if active:
                h = h_rows[r % 3, part]
                _, slope = gelu_both(h * scale + shift)
                dz = times(acc[slot, part], m) * slope
                rows[k, part] = dz
                total[0] = total[0] + dz
                total[1] = total[1] + dz * (h * rscale + offset)
            else:
                index, base = row_place(h_split, r)
                rows[k, part] = times(extras[index][r - base, part] + acc[slot, part], m)
        if not active:
            stores.append(pltpu.make_async_copy(rows.at[k], out_ref.at[r], out_sem.at[k]))
            stores[-1].start()

    for copy in weights:
        copy.wait()
    ready = []
    for t in range(count + 1):
        if t < count:
            for copy in fetches[t]:
                copy.wait()
            if t + 2 < count:
                for copy in fetches[t + 2]:
                    copy.start()
        for r in ready:
            if active:
                h_fetch(r).wait()
                if r + 2 < last:
                    h_fetch(r + 2).start()
        if t < count:
            add_row(lhs[t % 3], w_ref, acc, t, batch)
        for r in ready:
            finish(r)
        ready = ready_rows(t, r0, count, side) if t < count else []
    if carry_out is not None:
        carry_out[0] = acc[count]
        carry_out[1] = acc[count + 1]
    if active:
        sum_ref[...] = jnp.zeros(sum_ref.shape, F32)
        for k in range(2):
            s = jnp.sum(total[k], axis=0, keepdims=True)
            sum_ref[k : k + 1] = s if prev_ref is None else s + prev_ref[k : k + 1]
    for copy in stores:
        copy.wait()


def conv_back(kind, r0, count, side, batch, ext, weights, sources, extra, params, carry, prev):
    blocks, pixels = len(weights), side * batch
    splits = [x[0].shape[0] for x in sources]
    first, last, _ = emitted(r0, count, side)
    rows = last - first
    active = kind == "active"
    ins = [(ext, "v")] + [(x, "h") for x in weights]
    ins += [(x, "h" if kind == "active" else "a") for chunk in sources for x in chunk]
    h_split = [h.shape[0] for h in extra]
    if active:
        ins.append((params, "v"))
        ins += [(extra[k], "h") for k in sorted({row_place(h_split, r)[0] for r in range(first, last)})]
    else:
        ins += [(x, "v") for x in extra]
    aliases = {}
    if r0:
        ins.append((carry, "v"))
        if not active:
            aliases[len(ins)] = 0
        ins.append((prev, "v" if active else "h"))
    outs = [((rows if active else side, pixels, LANES), F32, "v" if active else "h")]
    if active:
        outs.append(((8, LANES), F32, "v"))
    if r0 + count != side:
        outs.append(((2, pixels, LANES), F32, "v"))
    scratch = [pltpu.VMEM((count + 2, pixels, LANES), F32), pltpu.VMEM((blocks * LANES, TAPS * LANES), BF16)]
    scratch += [DMA((count * blocks,)), DMA((blocks,))]
    scratch += [pltpu.VMEM((pixels, blocks * LANES), BF16) for _ in range(3)]
    if active:
        scratch += [pltpu.VMEM((3, pixels, LANES), F32), DMA((3,))]
    else:
        scratch += [pltpu.VMEM((rows, pixels, LANES), F32), DMA((rows,))]
    return call(
        f"back_{kind}_{r0}",
        functools.partial(conv_back_body, kind, r0, count, side, batch, blocks, h_split, splits),
        outs,
        ins,
        scratch,
        aliases,
    )


def weight_grad_body(kind, side, batch, blocks, splits, ways, *refs):
    take = Takes(refs)
    place_ref, ext_ref = take(2)
    x_refs, g_refs = take(len(splits[0])), take(len(splits[1]))
    keep_ref, *send_refs = take(ways)
    acc, gs, masked = take(3)
    raw, x_sem = take(2) if kind == "images" else (None, None)
    mine = place_ref[1]
    rows = side * batch
    def fetch(r):
        slot = lax.rem(r, 3)
        return pltpu.make_async_copy(x_refs[0].at[r], raw.at[slot], x_sem.at[slot])

    if kind == "images":
        fetch(0).start()
        fetch(1).start()
    ext = ext_ref[...]
    gs[0] = jnp.zeros((rows, LANES), BF16)
    gs[side + 1] = jnp.zeros((rows, LANES), BF16)
    for r in range(side):
        index, base = row_place(splits[1], r)
        gs[r + 1] = g_refs[index][r - base]
    acc[...] = jnp.zeros(acc.shape, F32)
    edge = jnp.zeros((batch, LANES), BF16)
    for start, stop, ((xi, xb),) in segments(splits[0]):

        @pl.loop(start, stop)
        def _(r, xi=xi, xb=xb):
            if kind == "images":

                @pl.when(r + 2 < side)
                def _():
                    fetch(r + 2).start()

                fetch(r).wait()
                for c in range(side):
                    part = slice(c * batch, (c + 1) * batch)
                    m = mask_at(ext, r, c).astype(BF16)
                    for k in range(blocks):
                        lanes = slice(k * LANES, (k + 1) * LANES)
                        masked[part, lanes] = raw[lax.rem(r, 3), part, lanes] * m
                x = masked[...]
            else:
                x = x_refs[xi][r - xb]
            parts = []
            for i in range(3):
                g = gs[r + 2 - i]
                parts.append(jnp.concatenate([g[batch:], edge], axis=0))
                parts.append(g)
                parts.append(jnp.concatenate([edge, g[: rows - batch]], axis=0))
            wide = jnp.concatenate(parts, axis=1)
            acc[...] += lax.dot_general(x, wide, (((0,), (0,)), ((), ())), preferred_element_type=F32)

    share = TAPS * blocks // ways
    for t in range(TAPS):
        for k in range(blocks):
            unit, lanes = t * blocks + k, slice(t * LANES, (t + 1) * LANES)
            if kind == "images":
                value = acc[k * LANES : (k + 1) * LANES, lanes]
            else:
                other = jnp.bitwise_xor(place_ref[0], k)
                value = acc[pl.ds(pl.multiple_of(other * LANES, LANES), LANES), lanes]
            at = slice(unit % share * LANES, (unit % share + 1) * LANES)
            distance = jnp.bitwise_xor(mine, unit // share)

            @pl.when(distance == 0)
            def _(value=value, at=at):
                keep_ref[at] = value

            for d in range(1, ways):

                @pl.when(distance == d)
                def _(value=value, at=at, d=d):
                    send_refs[d - 1][at] = value.astype(BF16)


def weight_grad(kind, place, ext, xs, gs, ways, side, batch):
    width, pixels = xs[0].shape[2], side * batch
    blocks = width // LANES
    splits = ([x.shape[0] for x in xs], [g.shape[0] for g in gs])
    share = TAPS * width // ways
    return call(
        f"wgrad_{kind}",
        functools.partial(weight_grad_body, kind, side, batch, blocks, splits, ways),
        [((share, LANES), F32, "v")] + [((share, LANES), BF16, "v")] * (ways - 1),
        [(place, "s"), (ext, "v")] + [(x, "h" if kind == "images" else "v") for x in xs] + [(g, "v") for g in gs],
        [
            pltpu.VMEM((width, TAPS * LANES), F32),
            pltpu.VMEM((side + 2, pixels, LANES), BF16),
            pltpu.VMEM((pixels, width), BF16),
        ]
        + ([pltpu.VMEM((3, pixels, width), BF16), DMA((3,))] if kind == "images" else []),
    )


def block_end_body(side, batch, split, own_split, grad_split, *refs):
    take = Takes(refs)
    ext_ref, params_ref, cot_ref = take(3)
    h_refs, own_refs = take(len(split)), take(len(own_split))
    out_hbm = take()
    grad_refs = take(len(grad_split))
    sum_ref, outs, sems = take(3)
    ext = ext_ref[...]
    scale, shift, rscale, offset = (params_ref[k : k + 1] for k in range(4))
    zero = jnp.zeros((batch, LANES), F32)
    total = (zero, zero)

    def store(r):
        return pltpu.make_async_copy(outs.at[r], out_hbm.at[r], sems.at[r])

    for start, stop, ((index, base), (wi, wb), (gi, gb)) in segments(split, own_split, grad_split):

        def one(r, carry, index=index, base=base, wi=wi, wb=wb, gi=gi, gb=gb):
            ds, dn = carry
            for c in range(side):
                part = slice(c * batch, (c + 1) * batch)
                m = mask_at(ext, r, c)
                h = h_refs[index][r - base, part]
                value, slope = gelu_both(h * scale + shift + own_refs[wi][r - wb, part].astype(F32))
                outs[r, part] = (value * m).astype(BF16)
                dz = cot_ref[r, part].astype(F32) * m * slope
                grad_refs[gi][r - gb, part] = dz
                ds = ds + dz
                dn = dn + dz * (h * rscale + offset)
            store(r).start()
            return ds, dn

        total = lax.fori_loop(start, stop, one, total)
    sum_ref[...] = jnp.zeros(sum_ref.shape, F32)
    sum_ref[0:1] = jnp.sum(total[0], axis=0, keepdims=True)
    sum_ref[1:2] = jnp.sum(total[1], axis=0, keepdims=True)
    for r in range(side):
        store(r).wait()


def block_end(ext, params, cotangent, hs, owns, grad_split, side, batch):
    pixels = side * batch
    shape = (side, pixels, LANES)
    split, own_split = [h.shape[0] for h in hs], [x.shape[0] for x in owns]
    outs = [(shape, BF16, "h")] + [((n, pixels, LANES), F32, "v") for n in grad_split] + [((8, LANES), F32, "v")]
    return call(
        "block_end",
        functools.partial(block_end_body, side, batch, split, own_split, grad_split),
        outs,
        [(ext, "v"), (params, "v"), (cotangent, "v")] + [(x, "v") for x in list(hs) + list(owns)],
        [pltpu.VMEM(shape, BF16), DMA((side,))],
    )


def norm_back_body(side, batch, far_h, splits, *refs):
    take = Takes(refs)
    ext_ref, params_ref, one_ref, other_ref = take(4)
    h_refs, dz_refs, out_refs = (take(len(s)) for s in splits)
    gain_ref, shift_ref = take(2)
    if far_h:
        h_rows, h_sem = take(2)
        for r in range(side):
            index, base = row_place(splits[0], r)
            pltpu.make_async_copy(h_refs[index].at[r - base], h_rows.at[r], h_sem.at[r]).start()
    ext = ext_ref[...]
    scale, _, rscale, offset, n = (params_ref[k : k + 1] for k in range(5))
    sums = one_ref[...] + other_ref[...]
    shift_ref[...] = sums[0:1]
    gain_ref[...] = sums[1:2]
    shift_grad, gain_grad = sums[0:1] / n, sums[1:2] / n
    b = scale * rscale * gain_grad
    c0 = scale * (shift_grad + offset * gain_grad)
    for start, stop, ((hi, hb), (zi, zb), (oi, ob)) in segments(*splits):

        @pl.loop(start, stop)
        def _(r, hi=hi, hb=hb, zi=zi, zb=zb, oi=oi, ob=ob):
            if far_h:
                pltpu.make_async_copy(h_refs[hi].at[r - hb], h_rows.at[r], h_sem.at[r]).wait()
            for c in range(side):
                part = slice(c * batch, (c + 1) * batch)
                m = mask_at(ext, r, c)
                h = h_rows[r, part] if far_h else h_refs[hi][r - hb, part]
                grad = scale * dz_refs[zi][r - zb, part] - (h * b + c0)
                out_refs[oi][r - ob, part] = (m * grad).astype(BF16)


def norm_back(ext, params, sums, hs, dzs, flow, far_h, side, batch):
    splits = ([h.shape[0] for h in hs], [z.shape[0] for z in dzs], list(flow))
    return call(
        "norm_back",
        functools.partial(norm_back_body, side, batch, far_h, splits),
        [((n, side * batch, LANES), BF16, "v") for n in flow] + [((1, LANES), F32, "v")] * 2,
        [(ext, "v"), (params, "v")] + [(x, "v") for x in sums] + [(x, "h" if far_h else "v") for x in hs] + [(x, "v") for x in dzs],
        [pltpu.VMEM((side, side * batch, LANES), F32), DMA((side,))] if far_h else [],
    )


def as_rows(values):
    row = lax.broadcasted_iota(jnp.int32, (8, LANES), 0)
    out = jnp.zeros((8, LANES), F32)
    for k, value in enumerate(values):
        out = jnp.where(row == k, value, out)
    return out


def merge(a, b):
    merged = merge_rows(*(a[k : k + 1] for k in range(3)), *(b[k : k + 1] for k in range(3)))
    return as_rows(list(merged) + [a[k : k + 1] for k in range(3, 6)])


def affine(a, gain, shift):
    center, n = a[0:1], a[2:3]
    rscale = lax.rsqrt(a[1:2] / n + EPSILON)
    scale = rscale * gain
    rows = [scale, shift - center * scale, rscale, -center * rscale, n]
    return as_rows(rows + [(a[3 + q : 4 + q] - center) * scale + shift for q in range(3)])


def swap(x, axis, size, k):
    return lax.ppermute(x, axis, [(i, i ^ k) for i in range(size)])


def after(x, *others):
    return lax.optimization_barrier((x,) + others)[0]


class Sum:
    def __init__(self, x, size, add=None):
        self.x, self.size, self.k = x, size, 1
        self.add = add or (lambda a, b: a + b)

    def step(self, start=(), end=()):
        if self.k < self.size:
            x = after(self.x, *start) if start else self.x
            other = swap(x, "dp", self.size, self.k)
            self.x = self.add(self.x, after(other, *end) if end else other)
            self.k *= 2
        return self.x

    def end(self):
        while self.k < self.size:
            self.step()
        return self.x

    def pair(self):
        while 2 * self.k < self.size:
            self.step()
        return self.x, swap(self.x, "dp", self.size, self.k)


class Scatter:
    def __init__(self, keep, sends, size, index):
        self.keep, self.sends, self.size, self.index = keep, sends, size, index
        self.k = None

    def step(self, start=(), end=()):
        if self.k is None:
            sends = self.sends
            if start:
                sends = lax.optimization_barrier(tuple(sends) + tuple(start))[: len(sends)]
            others = tuple(swap(x, "dp", self.size, d + 1) for d, x in enumerate(sends))
            if end:
                others = lax.optimization_barrier(others + tuple(end))[: len(sends)]
            for other in others:
                self.keep = self.keep + other.astype(F32)
            self.k = len(sends) + 1
        elif self.k < self.size:
            half = self.keep.shape[0] // 2
            low, high = self.keep[:half], self.keep[half:]
            upper = (self.index // self.k) % 2 == 1
            send = jnp.where(upper, low, high).astype(BF16)
            other = swap(after(send, *start) if start else send, "dp", self.size, self.k)
            self.keep = jnp.where(upper, high, low) + (after(other, *end) if end else other).astype(F32)
            self.k *= 2
        return self.keep

    def end(self):
        while self.k is None or self.k < self.size:
            self.step()
        return self.keep


class Gather:
    def __init__(self, part, size, ways, index, at_once):
        self.x, self.size, self.ways, self.index, self.at_once = part.astype(BF16), size, ways, index, at_once
        self.ks, k = [], size
        while k > ways:
            k //= 2
            self.ks.append(k)
        if at_once:
            self.ks.append(0)
        else:
            while k > 1:
                k //= 2
                self.ks.append(ways // (2 * k))

    def step(self, start=(), end=()):
        if not self.ks:
            return self.x
        x = after(self.x, *start) if start else self.x
        k = self.ks.pop(0)
        if k:
            other = swap(x, "dp", self.size, k)
            other = after(other, *end) if end else other
            upper = (self.index // k) % 2 == 1
            self.x = jnp.where(upper, jnp.concatenate([other, self.x]), jnp.concatenate([self.x, other]))
        else:
            others = tuple(swap(x, "dp", self.size, d) for d in range(1, self.ways))
            if end:
                others = lax.optimization_barrier(others + tuple(end))[: self.ways - 1]
            self.others = others
        return self.x

    def end(self, *late):
        while self.ks:
            self.step()
        if self.at_once:
            others = lax.optimization_barrier(self.others + late)[: self.ways - 1] if late else self.others
            mine = self.index % self.ways
            self.x = jnp.concatenate([lax.select_n(mine ^ j, self.x, *others) for j in range(self.ways)])
        return self.x.astype(F32)


class Blocks:
    def __init__(self, x, size, late=False):
        self.own, self.size = x, size
        self.far = swap(x, "chan", size, 2)
        self.near = None if late else swap(x, "chan", size, 1)

    def end(self, *others):
        if self.near is None:
            self.near = swap(after(self.own, *others), "chan", self.size, 1)
        far = after(self.far, *others) if others else self.far
        return [self.own, self.near, far, swap(far, "chan", self.size, 1)]


def sum_chan(x, size):
    k = 1
    while k < size:
        x = x + swap(x, "chan", size, k)
        k *= 2
    return x


def moment_step(weight, grad, moment, weight_norm, grad_norm):
    trust = TRUST_COEF * weight_norm / (grad_norm + DECAY * weight_norm)
    return MOMENTUM * moment + LEARN_RATE * trust * (grad + DECAY * weight)


def shards(
    dp, ch, images, groups, cotangent, weight_one, gain_one, shift_one, weight_two, gain_two, shift_two, moment_one, moment_two
):
    batch, side, _, width = images.shape
    pixels = side * batch
    images = jnp.transpose(images, (1, 2, 0, 3)).reshape(side, pixels, width)
    cotangent = jnp.transpose(cotangent, (1, 2, 0, 3)).reshape(side, pixels, LANES)
    chan, index = lax.axis_index("chan").astype(jnp.int32), lax.axis_index("dp").astype(jnp.int32)
    ways = min(4, dp)
    place = jnp.stack([chan, index % ways])
    ext = jnp.broadcast_to((5 + 2 * groups)[:, None], (batch, LANES))
    third = side // 3
    conv_in = (third + 1, third, side - 2 * third - 1)
    flow = (third, third, side - 2 * third)
    sizes = (side, batch)

    gains = [g.reshape(1, LANES) for g in (gain_one, shift_one, gain_two, shift_two)]

    low, h_one, owns, carry, stat, weights, r0 = [], [], [], None, None, weight_one, 0
    for q, count in enumerate(conv_in):
        out = conv_images(q, r0, count, *sizes, place, ext, weights, images, carry, stat)
        h, stat, chunk, own = out[:4]
        if q == 0:
            weights = out[4]
        carry = out[-1]
        h_one.append(h)
        owns.append(own)
        low.append(Blocks(chunk, ch))
        r0 += count
    wb_two, squares, *wt = prep(weight_one, weight_two, place)
    total = Sum(stat, dp, merge)
    total.step(start=(low[0].far,))
    total.step(start=(squares,))
    total.step(start=(low[1].far,))
    params_one = affine(total.end(), *gains[:2])
    params = Blocks(params_one, ch).end()

    h_two, act, carry, stat, r0 = [], [], None, None, 0
    for q, count in enumerate(flow):
        out = conv_active(q, r0, count, *sizes, place, ext, wb_two, low[q].end(), params, carry, stat)
        h, stat, rows = out[:3]
        if q == 0:
            wt_two = [after(w, stat) for w in wt[ch:]]
            wt_two = [wt_two[0]] + [swap(wt_two[k], "chan", ch, k) for k in range(1, ch)]
        h_two.append(h)
        act.append(rows)
        carry = out[-1]
        r0 += count
    params_two = affine(Sum(stat, dp, merge).end(), *gains[2:])

    out = block_end(ext, params_two, cotangent, h_two, owns, (side,), *sizes)
    block_output, grad_pre, sums = out
    sums_two = Sum(sums, dp).pair()
    *grad_two, gain_two_grad, shift_two_grad = norm_back(ext, params_two, (after(sums_two[0], *wt_two[1:]), sums_two[1]), h_two, [grad_pre], (side,), False, *sizes)
    gathered = Blocks(grad_two[0], ch, True)
    keep, *sends = weight_grad("act", place, ext, act, grad_two, ways, *sizes)
    scatter = Scatter(keep, sends, dp, index)
    scatter.step()
    sources = gathered.end(scatter.keep)
    wt_one = [after(w, scatter.keep) for w in wt[:ch]]
    wt_one = [wt_one[0]] + [swap(wt_one[k], "chan", ch, k) for k in range(1, ch)]
    dz_one, sums = conv_back("active", 0, side, *sizes, ext, wt_two, [sources], h_one, params_one, None, None)
    scatter.step(end=(sums,))
    part_two = scatter.end()
    gather_two = Gather(part_two, dp, ways, index, True)
    total = Sum(sums, dp)
    total.step(start=tuple(wt_one[2:]))
    gather_two.step()
    sums_one = total.pair()
    split = (third + 1, side - third - 1)
    *grad_one, gain_one_grad, shift_one_grad = norm_back(ext, params_one, (after(sums_one[0], gather_two.x, *wt_one[1:]), sums_one[1]), h_one, [dz_one], split, True, *sizes)
    gathered = [Blocks(g, ch, True) for g in grad_one]
    keep, *sends = weight_grad("images", place, ext, [images], grad_one, ways, *sizes)
    gather_two.step(start=(grad_one[0],), end=(keep,))
    scatter = Scatter(keep, sends, dp, index)
    scatter.step(start=(gathered[0].far,))
    sources = [g.end(scatter.keep) for g in gathered]
    weight_two_grad = gather_two.end().reshape(weight_two.shape)
    squares = jnp.sum(squares, axis=1)
    norms = jnp.sqrt(sum_chan(jnp.stack([squares[0], squares[1], jnp.sum(weight_two_grad * weight_two_grad)]), ch))
    part_one = scatter.end()
    gather_one = Gather(part_one, dp, ways, index, True)
    moment_two_new = moment_step(weight_two, weight_two_grad, moment_two, norms[1], norms[2])
    input_grad, carry = conv_back(
        "input", 0, split[0], *sizes, after(ext, part_one), wt_one, sources[:1], [grad_pre], None, None, None
    )
    gather_one.step(end=(moment_two_new, carry))
    input_grad = conv_back(
        "input", split[0], split[1], *sizes, after(ext, gather_one.x), wt_one, sources[1:], [grad_pre], None, carry, input_grad
    )[0]
    gather_one.step(end=(input_grad,))
    weight_one_grad = gather_one.end().reshape(weight_one.shape)
    norm_one = jnp.sqrt(sum_chan(jnp.sum(weight_one_grad * weight_one_grad).reshape(1), ch))
    weight_norms = norms[:2]
    grad_norms = jnp.concatenate([norm_one, norms[2:]])
    moment_one_new = moment_step(weight_one, weight_one_grad, moment_one, norms[0], norm_one[0])

    def as_images(x):
        return jnp.transpose(x.reshape(side, side, batch, LANES), (2, 0, 1, 3))

    return (
        as_images(block_output),
        as_images(input_grad),
        weight_one_grad,
        gain_one_grad.reshape(LANES),
        shift_one_grad.reshape(LANES),
        weight_two_grad,
        gain_two_grad.reshape(LANES),
        shift_two_grad.reshape(LANES),
        moment_one_new,
        moment_two_new,
        weight_norms,
        grad_norms,
    )


def solution(mesh):
    full, rows, both = P("dp", None, None, None), P("dp"), P("dp", None, None, "chan")
    weight, channel = P(None, None, "chan"), P("chan")
    return jax.shard_map(
        functools.partial(shards, mesh.shape["dp"], mesh.shape["chan"]),
        mesh=mesh,
        in_specs=(full, rows, both, weight, channel, channel, weight, channel, channel, weight, weight),
        out_specs=(both, both, weight, channel, channel, weight, channel, channel, weight, weight, P(), P()),
        check_vma=False,
    )
```

```python
import functools

import jax
import jax.numpy as jnp
from jax import lax
from jax.experimental import pallas as pl
from jax.experimental.pallas import tpu as pltpu
from jax.sharding import PartitionSpec as P

EPSILON = 1e-05
MOMENTUM = 0.9
LEARN_RATE = 8.0
TRUST_COEF = 0.001
DECAY = 5e-05
GELU_A = 0.7978845608028654
GELU_B = 0.7978845608028654 * 0.044715
F32 = jnp.float32
BF16 = jnp.bfloat16
LANES = 128
TAPS = 9
PAIRS = ((0, 2), (2, 4), (4, 6), (6, 8), (8, 9))
VMEM_LEAST = 12 * 1024 * 1024
VMEM_OPERANDS = 7 * 1024 * 1024
DMA = pltpu.SemaphoreType.DMA


def mask_at(ext, r, c):
    if isinstance(r, int) and max(r, c) < 5:
        return None
    return jnp.where(ext > jnp.maximum(r, c), 1.0, 0.0).astype(F32)


def times(x, m):
    return x if m is None else x * m


def gelu(v):
    t = jnp.tanh(v * (GELU_A + GELU_B * (v * v)))
    half = 0.5 * v
    return half + half * t


def gelu_both(v):
    sq = v * v
    t = jnp.tanh(v * (GELU_A + GELU_B * sq))
    half = 0.5 * v
    value = half + half * t
    slope = 0.5 + 0.5 * t + (half - half * (t * t)) * (GELU_A + (3.0 * GELU_B) * sq)
    return value, slope


def call(name, body, outs, ins, scratch=(), aliases=None):
    spec = {
        "a": pl.BlockSpec(memory_space=pl.ANY),
        "v": pl.BlockSpec(memory_space=pltpu.VMEM),
        "h": pl.BlockSpec(memory_space=pltpu.HBM),
        "s": pl.BlockSpec(memory_space=pltpu.SMEM),
    }
    return pl.pallas_call(
        body,
        name=name,
        out_shape=[jax.ShapeDtypeStruct(s, d) for s, d, _ in outs],
        in_specs=[spec[w] for _, w in ins],
        out_specs=[spec[w] for _, _, w in outs],
        scratch_shapes=list(scratch),
        input_output_aliases=aliases or {},
        compiler_params=pltpu.CompilerParams(vmem_limit_bytes=max(VMEM_LEAST, VMEM_OPERANDS + room(scratch))),
        cost_estimate=pl.CostEstimate(flops=0, bytes_accessed=0, transcendentals=0),
    )(*[pltpu.with_memory_space_constraint(x, pltpu.HBM) if w == "h" else x for x, w in ins])


def segments(*splits):
    ends = sorted({sum(s[: k + 1]) for s in splits for k in range(len(s))})
    result, start = [], 0
    for end in ends:
        result.append((start, end, [row_place(s, start) for s in splits]))
        start = end
    return result


def row_place(split, r):
    at = 0
    for index, size in enumerate(split):
        if r < at + size:
            return index, at
        at += size


def room(scratch):
    total = 0
    for x in scratch:
        if hasattr(x, "memory_space") and x.memory_space == pltpu.VMEM:
            size = jnp.dtype(x.dtype).itemsize
            for n in x.shape:
                size *= n
            total += size
    return total


class Takes:
    def __init__(self, refs):
        self.refs = list(refs)

    def __call__(self, n=None):
        if n is None:
            return self.refs.pop(0)
        return [self.refs.pop(0) for _ in range(n)]


def prep_body(blocks, chan_ref, one_ref, two_ref, wb_ref, sq_ref, *wt_refs):
    chan = chan_ref[0]
    sq_ref[...] = jnp.zeros(sq_ref.shape, F32)
    for layer, w_ref in enumerate((one_ref, two_ref)):
        total = jnp.zeros((1, LANES), F32)
        for k in range(blocks):
            rows = pl.ds(pl.multiple_of(jnp.bitwise_xor(chan, k) * LANES, LANES), LANES)
            for t in range(TAPS):
                piece = w_ref[t, rows, :]
                total = total + jnp.sum(piece * piece, axis=0, keepdims=True)
                if layer:
                    wb_ref[k * LANES : (k + 1) * LANES, t * LANES : (t + 1) * LANES] = piece.astype(BF16)
                flip = TAPS - 1 - t
                wt_refs[layer * blocks + k][:, flip * LANES : (flip + 1) * LANES] = piece.T.astype(BF16)
        sq_ref[layer : layer + 1] = total


def prep(weight_one, weight_two, chan):
    width = weight_one.shape[1]
    blocks = width // LANES
    return call(
        "prep",
        functools.partial(prep_body, blocks),
        [
            ((width, TAPS * LANES), BF16, "v"),
            ((8, LANES), F32, "v"),
        ]
        + [((LANES, TAPS * LANES), BF16, "v")] * (2 * blocks),
        [(chan, "s"), (weight_one, "v"), (weight_two, "v")],
    )


def add_row(lhs_ref, w_ref, acc, slot, batch):
    rows = lhs_ref.shape[0]
    for a, b in PAIRS:
        y = jnp.dot(lhs_ref[...], w_ref[:, a * LANES : b * LANES], preferred_element_type=F32)
        for t in range(a, b):
            i, j = divmod(t, 3)
            z = y[:, (t - a) * LANES : (t - a + 1) * LANES]
            at = slot + 2 - i
            if j == 0:
                acc[at, batch:] += z[: rows - batch]
            elif j == 1:
                acc[at] += z
            else:
                acc[at, : rows - batch] += z[batch:]


def start_acc(acc, carry_ref):
    for slot in range(acc.shape[0]):
        if carry_ref is not None and slot < 2:
            acc[slot] = carry_ref[slot]
        else:
            acc[slot] = jnp.zeros(acc.shape[1:], F32)


def emitted(r0, count, side):
    first = 0 if r0 == 0 else r0 - 1
    last = side if r0 + count == side else r0 + count - 1
    return first, last, first - (r0 - 1)


def ready_rows(t, r0, count, side):
    r = r0 + t
    rows = [r - 1] if r > 0 else []
    return rows + [r] if r == side - 1 else rows


class Stats:
    def __init__(self, ext, side, batch):
        self.ext, self.side, self.batch = ext, side, batch
        self.ref = None
        zero = jnp.zeros((batch, LANES), F32)
        self.s1, self.s2, self.n = zero, zero, zero

    def row(self, acc, slot, r, low_ref=None):
        batch = self.batch
        if self.ref is None:
            s = n = jnp.zeros((batch, LANES), F32)
            for c in range(self.side):
                m = mask_at(self.ext, r, c)
                s = s + times(acc[slot, c * batch : (c + 1) * batch], m)
                n = n + (1.0 if m is None else m)
            n = jnp.sum(n, axis=0, keepdims=True)
            self.ref = jnp.sum(s, axis=0, keepdims=True) / jnp.maximum(n, 1.0)
        for c in range(self.side):
            m = mask_at(self.ext, r, c)
            d = acc[slot, c * batch : (c + 1) * batch] - self.ref
            if low_ref is not None:
                low_ref[c * batch : (c + 1) * batch] = d.astype(BF16)
            masked = times(d, m)
            self.s1 = self.s1 + masked
            self.s2 = self.s2 + masked * d
            self.n = self.n + (1.0 if m is None else m)

    def store(self, stat_ref, prev_ref, chunk):
        s1, s2, n = (jnp.sum(x, axis=0, keepdims=True) for x in (self.s1, self.s2, self.n))
        safe = jnp.maximum(n, 1.0)
        whole = (self.ref + s1 / safe, s2 - s1 * s1 / safe, n)
        stat_ref[...] = jnp.zeros(stat_ref.shape, F32) if prev_ref is None else prev_ref[...]
        if prev_ref is not None:
            whole = merge_rows(*(prev_ref[k : k + 1] for k in range(3)), *whole)
        for k in range(3):
            stat_ref[k : k + 1] = whole[k]
        stat_ref[3 + chunk : 4 + chunk] = self.ref


def merge_rows(mean_a, m2_a, n_a, mean_b, m2_b, n_b):
    n = n_a + n_b
    safe = jnp.maximum(n, 1.0)
    delta = mean_a - mean_b
    mean = (n_a * mean_a + n_b * mean_b) / safe
    return mean, m2_a + m2_b + delta * delta * (n_a * n_b / safe), n


def conv_images_body(chunk, r0, count, side, batch, blocks, *refs):
    take = Takes(refs)
    place_ref, ext_ref, w_in, x_hbm = take(4)
    carry_ref, prev_ref = take(2) if r0 else (None, None)
    h_ref, stat_ref, low_ref, own_ref = take(4)
    w_ref = take() if r0 == 0 else w_in
    carry_out = None if r0 + count == side else take()
    acc, raw, x_sem = take(3)
    lhs = take(count)
    fetches = [pltpu.make_async_copy(x_hbm.at[r0 + t], raw.at[t], x_sem.at[t]) for t in range(count)]
    fetches[0].start()
    if r0 == 0:
        w_raw, w_sem = take(2)
        taps = [pltpu.make_async_copy(w_in.at[t], w_raw.at[t], w_sem.at[t]) for t in range(TAPS)]
        for copy in taps:
            copy.start()
    for copy in fetches[1:]:
        copy.start()
    ext = ext_ref[...]
    start_acc(acc, carry_ref)
    if r0 == 0:
        for t in range(TAPS):
            taps[t].wait()
            w_ref[:, t * LANES : (t + 1) * LANES] = w_raw[t].astype(BF16)

    mine = pl.ds(pl.multiple_of(place_ref[0] * LANES, LANES), LANES)

    def stage(t):
        fetches[t].wait()
        for c in range(side):
            part = slice(c * batch, (c + 1) * batch)
            m = mask_at(ext, r0 + t, c)
            x = raw[t, part, mine]
            own_ref[t, part] = x if m is None else x * m.astype(BF16)
            for k in range(blocks):
                lanes = slice(k * LANES, (k + 1) * LANES)
                x = raw[t, part, lanes]
                lhs[t][part, lanes] = x if m is None else x * m.astype(BF16)

    first, last, _ = emitted(r0, count, side)
    stats = Stats(ext, side, batch)
    stage(0)
    for t in range(count):
        if t + 1 < count:
            stage(t + 1)
        add_row(lhs[t], w_ref, acc, t, batch)
        for r in ready_rows(t, r0, count, side):
            h_ref[r - first] = acc[r - (r0 - 1)]
            stats.row(acc, r - (r0 - 1), r, low_ref.at[r - first])
    stats.store(stat_ref, prev_ref, chunk)
    if carry_out is not None:
        carry_out[0] = acc[count]
        carry_out[1] = acc[count + 1]


def conv_images(chunk, r0, count, side, batch, place, ext, weights, images, carry, prev):
    pixels, width = side * batch, images.shape[2]
    first, last, _ = emitted(r0, count, side)
    rows = last - first
    ins = [(place, "s"), (ext, "v"), (weights, "v" if r0 else "h"), (images, "h")]
    if r0:
        ins += [(carry, "v"), (prev, "v")]
    outs = [((rows, pixels, LANES), F32, "v"), ((8, LANES), F32, "v"), ((rows, pixels, LANES), BF16, "v")]
    outs.append(((count, pixels, LANES), BF16, "v"))
    if r0 == 0:
        outs.append(((width, TAPS * LANES), BF16, "v"))
    if r0 + count != side:
        outs.append(((2, pixels, LANES), F32, "v"))
    scratch = [pltpu.VMEM((count + 2, pixels, LANES), F32), pltpu.VMEM((count, pixels, width), BF16), DMA((count,))]
    scratch += [pltpu.VMEM((pixels, width), BF16) for _ in range(count)]
    if r0 == 0:
        scratch += [pltpu.VMEM((TAPS, width, LANES), F32), DMA((TAPS,))]
    return call(
        f"conv_one_{r0}",
        functools.partial(conv_images_body, chunk, r0, count, side, batch, width // LANES),
        outs,
        ins,
        scratch,
    )


def conv_active_body(chunk, r0, count, side, batch, blocks, *refs):
    take = Takes(refs)
    place_ref, ext_ref, w_ref = take(3)
    sources, params = take(blocks), take(blocks)
    carry_ref, prev_ref = take(2) if r0 else (None, None)
    h_ref, stat_ref, act_ref = take(3)
    carry_out = None if r0 + count == side else take()
    acc = take()
    lhs = take(count)
    ext = ext_ref[...]
    start_acc(acc, carry_ref)

    def stage(t):
        for k in range(blocks):
            scale, shift = params[k][0:1], params[k][5 + chunk : 6 + chunk]
            for c in range(side):
                part = slice(c * batch, (c + 1) * batch)
                z = sources[k][t, part].astype(F32) * scale + shift
                low = times(gelu(z), mask_at(ext, r0 + t, c)).astype(BF16)
                lhs[t][part, k * LANES : (k + 1) * LANES] = low
                act_ref[t, part, k * LANES : (k + 1) * LANES] = low

    first, last, _ = emitted(r0, count, side)
    stats = Stats(ext, side, batch)
    stage(0)
    for t in range(count):
        if t + 1 < count:
            stage(t + 1)
        add_row(lhs[t], w_ref, acc, t, batch)
        for r in ready_rows(t, r0, count, side):
            h_ref[r - first] = acc[r - (r0 - 1)]
            stats.row(acc, r - (r0 - 1), r)
    stats.store(stat_ref, prev_ref, chunk)
    if carry_out is not None:
        carry_out[0] = acc[count]
        carry_out[1] = acc[count + 1]


def conv_active(chunk, r0, count, side, batch, place, ext, weights, sources, params, carry, prev):
    blocks, pixels = len(sources), side * batch
    width = LANES * blocks
    first, last, _ = emitted(r0, count, side)
    ins = [(place, "s"), (ext, "v"), (weights, "v")] + [(x, "v") for x in sources] + [(p, "v") for p in params]
    if r0:
        ins += [(carry, "v"), (prev, "v")]
    outs = [((last - first, pixels, LANES), F32, "v"), ((8, LANES), F32, "v"), ((count, pixels, width), BF16, "v")]
    if r0 + count != side:
        outs.append(((2, pixels, LANES), F32, "v"))
    scratch = [pltpu.VMEM((count + 2, pixels, LANES), F32)]
    scratch += [pltpu.VMEM((pixels, width), BF16) for _ in range(count)]
    return call(
        f"conv_two_{r0}",
        functools.partial(conv_active_body, chunk, r0, count, side, batch, blocks),
        outs,
        ins,
        scratch,
    )


def conv_back_body(kind, r0, count, side, batch, blocks, h_split, splits, *refs):
    take = Takes(refs)
    ext_ref = take()
    wt_refs = take(blocks)
    sources = [take(blocks) for _ in splits]
    first, last, _ = emitted(r0, count, side)
    active = kind == "active"
    carry_ref = prev_ref = params_ref = None
    if active:
        params_ref = take()
        h_used = sorted({row_place(h_split, r)[0] for r in range(first, last)})
        h_refs = dict(zip(h_used, take(len(h_used))))
    else:
        extras = take(len(h_split))
    if r0:
        carry_ref = take()
        prev_ref = take()
    out_ref = take()
    sum_ref = take() if active else None
    carry_out = None if r0 + count == side else take()
    acc, w_ref = take(2)
    in_sem, w_sem = take(2)
    lhs = take(3)
    rows, out_sem = (out_ref, None) if active else take(2)
    h_rows, h_sem = take(2) if active else (None, None)
    stores = []
    chunks = [row_place(splits, t) for t in range(count)]
    fetches = [
        [
            pltpu.make_async_copy(
                sources[chunks[t][0]][k].at[t - chunks[t][1]], lhs[t % 3].at[:, k * LANES : (k + 1) * LANES], in_sem.at[t * blocks + k]
            )
            for k in range(blocks)
        ]
        for t in range(count)
    ]
    weights = [
        pltpu.make_async_copy(wt_refs[k], w_ref.at[k * LANES : (k + 1) * LANES], w_sem.at[k]) for k in range(blocks)
    ]
    for copy in weights + fetches[0] + fetches[1]:
        copy.start()
    ext = ext_ref[...]
    start_acc(acc, carry_ref)
    zero = jnp.zeros((batch, LANES), F32)
    total = [zero, zero]
    if active:
        scale, shift, rscale, offset = (params_ref[k : k + 1] for k in range(4))

    def h_fetch(r):
        index, base = row_place(h_split, r)
        return pltpu.make_async_copy(h_refs[index].at[r - base], h_rows.at[r % 3], h_sem.at[r % 3])

    if active:
        for r in range(first, min(first + 2, last)):
            h_fetch(r).start()

    def finish(r):
        slot, k = r - (r0 - 1), r - first
        for c in range(side):
            part = slice(c * batch, (c + 1) * batch)
            m = mask_at(ext, r, c)
            if active:
                h = h_rows[r % 3, part]
                _, slope = gelu_both(h * scale + shift)
                dz = times(acc[slot, part], m) * slope
                rows[k, part] = dz
                total[0] = total[0] + dz
                total[1] = total[1] + dz * (h * rscale + offset)
            else:
                index, base = row_place(h_split, r)
                rows[k, part] = times(extras[index][r - base, part] + acc[slot, part], m)
        if not active:
            stores.append(pltpu.make_async_copy(rows.at[k], out_ref.at[r], out_sem.at[k]))
            stores[-1].start()

    for copy in weights:
        copy.wait()
    ready = []
    for t in range(count + 1):
        if t < count:
            for copy in fetches[t]:
                copy.wait()
            if t + 2 < count:
                for copy in fetches[t + 2]:
                    copy.start()
        for r in ready:
            if active:
                h_fetch(r).wait()
                if r + 2 < last:
                    h_fetch(r + 2).start()
        if t < count:
            add_row(lhs[t % 3], w_ref, acc, t, batch)
        for r in ready:
            finish(r)
        ready = ready_rows(t, r0, count, side) if t < count else []
    if carry_out is not None:
        carry_out[0] = acc[count]
        carry_out[1] = acc[count + 1]
    if active:
        sum_ref[...] = jnp.zeros(sum_ref.shape, F32)
        for k in range(2):
            s = jnp.sum(total[k], axis=0, keepdims=True)
            sum_ref[k : k + 1] = s if prev_ref is None else s + prev_ref[k : k + 1]
    for copy in stores:
        copy.wait()


def conv_back(kind, r0, count, side, batch, ext, weights, sources, extra, params, carry, prev):
    blocks, pixels = len(weights), side * batch
    splits = [x[0].shape[0] for x in sources]
    first, last, _ = emitted(r0, count, side)
    rows = last - first
    active = kind == "active"
    ins = [(ext, "v")] + [(x, "h") for x in weights]
    ins += [(x, "h" if kind == "active" else "a") for chunk in sources for x in chunk]
    h_split = [h.shape[0] for h in extra]
    if active:
        ins.append((params, "v"))
        ins += [(extra[k], "h") for k in sorted({row_place(h_split, r)[0] for r in range(first, last)})]
    else:
        ins += [(x, "v") for x in extra]
    aliases = {}
    if r0:
        ins.append((carry, "v"))
        if not active:
            aliases[len(ins)] = 0
        ins.append((prev, "v" if active else "h"))
    outs = [((rows if active else side, pixels, LANES), F32, "v" if active else "h")]
    if active:
        outs.append(((8, LANES), F32, "v"))
    if r0 + count != side:
        outs.append(((2, pixels, LANES), F32, "v"))
    scratch = [pltpu.VMEM((count + 2, pixels, LANES), F32), pltpu.VMEM((blocks * LANES, TAPS * LANES), BF16)]
    scratch += [DMA((count * blocks,)), DMA((blocks,))]
    scratch += [pltpu.VMEM((pixels, blocks * LANES), BF16) for _ in range(3)]
    if active:
        scratch += [pltpu.VMEM((3, pixels, LANES), F32), DMA((3,))]
    else:
        scratch += [pltpu.VMEM((rows, pixels, LANES), F32), DMA((rows,))]
    return call(
        f"back_{kind}_{r0}",
        functools.partial(conv_back_body, kind, r0, count, side, batch, blocks, h_split, splits),
        outs,
        ins,
        scratch,
        aliases,
    )


def weight_grad_body(kind, side, batch, blocks, splits, ways, *refs):
    take = Takes(refs)
    place_ref, ext_ref = take(2)
    x_refs, g_refs = take(len(splits[0])), take(len(splits[1]))
    keep_ref, *send_refs = take(ways)
    acc, gs, masked = take(3)
    raw, x_sem = take(2) if kind == "images" else (None, None)
    mine = place_ref[1]
    rows = side * batch
    def fetch(r):
        slot = lax.rem(r, 3)
        return pltpu.make_async_copy(x_refs[0].at[r], raw.at[slot], x_sem.at[slot])

    if kind == "images":
        fetch(0).start()
        fetch(1).start()
    ext = ext_ref[...]
    gs[0] = jnp.zeros((rows, LANES), BF16)
    gs[side + 1] = jnp.zeros((rows, LANES), BF16)
    for r in range(side):
        index, base = row_place(splits[1], r)
        gs[r + 1] = g_refs[index][r - base]
    acc[...] = jnp.zeros(acc.shape, F32)
    edge = jnp.zeros((batch, LANES), BF16)
    for start, stop, ((xi, xb),) in segments(splits[0]):

        @pl.loop(start, stop)
        def _(r, xi=xi, xb=xb):
            if kind == "images":

                @pl.when(r + 2 < side)
                def _():
                    fetch(r + 2).start()

                fetch(r).wait()
                for c in range(side):
                    part = slice(c * batch, (c + 1) * batch)
                    m = mask_at(ext, r, c).astype(BF16)
                    for k in range(blocks):
                        lanes = slice(k * LANES, (k + 1) * LANES)
                        masked[part, lanes] = raw[lax.rem(r, 3), part, lanes] * m
                x = masked[...]
            else:
                x = x_refs[xi][r - xb]
            parts = []
            for i in range(3):
                g = gs[r + 2 - i]
                parts.append(jnp.concatenate([g[batch:], edge], axis=0))
                parts.append(g)
                parts.append(jnp.concatenate([edge, g[: rows - batch]], axis=0))
            wide = jnp.concatenate(parts, axis=1)
            acc[...] += lax.dot_general(x, wide, (((0,), (0,)), ((), ())), preferred_element_type=F32)

    share = TAPS * blocks // ways
    for t in range(TAPS):
        for k in range(blocks):
            unit, lanes = t * blocks + k, slice(t * LANES, (t + 1) * LANES)
            if kind == "images":
                value = acc[k * LANES : (k + 1) * LANES, lanes]
            else:
                other = jnp.bitwise_xor(place_ref[0], k)
                value = acc[pl.ds(pl.multiple_of(other * LANES, LANES), LANES), lanes]
            at = slice(unit % share * LANES, (unit % share + 1) * LANES)
            distance = jnp.bitwise_xor(mine, unit // share)

            @pl.when(distance == 0)
            def _(value=value, at=at):
                keep_ref[at] = value

            for d in range(1, ways):

                @pl.when(distance == d)
                def _(value=value, at=at, d=d):
                    send_refs[d - 1][at] = value.astype(BF16)


def weight_grad(kind, place, ext, xs, gs, ways, side, batch):
    width, pixels = xs[0].shape[2], side * batch
    blocks = width // LANES
    splits = ([x.shape[0] for x in xs], [g.shape[0] for g in gs])
    share = TAPS * width // ways
    return call(
        f"wgrad_{kind}",
        functools.partial(weight_grad_body, kind, side, batch, blocks, splits, ways),
        [((share, LANES), F32, "v")] + [((share, LANES), BF16, "v")] * (ways - 1),
        [(place, "s"), (ext, "v")] + [(x, "h" if kind == "images" else "v") for x in xs] + [(g, "v") for g in gs],
        [
            pltpu.VMEM((width, TAPS * LANES), F32),
            pltpu.VMEM((side + 2, pixels, LANES), BF16),
            pltpu.VMEM((pixels, width), BF16),
        ]
        + ([pltpu.VMEM((3, pixels, width), BF16), DMA((3,))] if kind == "images" else []),
    )


def block_end_body(side, batch, split, own_split, grad_split, *refs):
    take = Takes(refs)
    ext_ref, params_ref, cot_ref = take(3)
    h_refs, own_refs = take(len(split)), take(len(own_split))
    out_hbm = take()
    grad_refs = take(len(grad_split))
    sum_ref, outs, sems = take(3)
    ext = ext_ref[...]
    scale, shift, rscale, offset = (params_ref[k : k + 1] for k in range(4))
    zero = jnp.zeros((batch, LANES), F32)
    total = (zero, zero)

    def store(r):
        return pltpu.make_async_copy(outs.at[r], out_hbm.at[r], sems.at[r])

    for start, stop, ((index, base), (wi, wb), (gi, gb)) in segments(split, own_split, grad_split):

        def one(r, carry, index=index, base=base, wi=wi, wb=wb, gi=gi, gb=gb):
            ds, dn = carry
            for c in range(side):
                part = slice(c * batch, (c + 1) * batch)
                m = mask_at(ext, r, c)
                h = h_refs[index][r - base, part]
                value, slope = gelu_both(h * scale + shift + own_refs[wi][r - wb, part].astype(F32))
                outs[r, part] = (value * m).astype(BF16)
                dz = cot_ref[r, part].astype(F32) * m * slope
                grad_refs[gi][r - gb, part] = dz
                ds = ds + dz
                dn = dn + dz * (h * rscale + offset)
            store(r).start()
            return ds, dn

        total = lax.fori_loop(start, stop, one, total)
    sum_ref[...] = jnp.zeros(sum_ref.shape, F32)
    sum_ref[0:1] = jnp.sum(total[0], axis=0, keepdims=True)
    sum_ref[1:2] = jnp.sum(total[1], axis=0, keepdims=True)
    for r in range(side):
        store(r).wait()


def block_end(ext, params, cotangent, hs, owns, grad_split, side, batch):
    pixels = side * batch
    shape = (side, pixels, LANES)
    split, own_split = [h.shape[0] for h in hs], [x.shape[0] for x in owns]
    outs = [(shape, BF16, "h")] + [((n, pixels, LANES), F32, "v") for n in grad_split] + [((8, LANES), F32, "v")]
    return call(
        "block_end",
        functools.partial(block_end_body, side, batch, split, own_split, grad_split),
        outs,
        [(ext, "v"), (params, "v"), (cotangent, "v")] + [(x, "v") for x in list(hs) + list(owns)],
        [pltpu.VMEM(shape, BF16), DMA((side,))],
    )


def norm_back_body(side, batch, far_h, splits, *refs):
    take = Takes(refs)
    ext_ref, params_ref, one_ref, other_ref = take(4)
    h_refs, dz_refs, out_refs = (take(len(s)) for s in splits)
    gain_ref, shift_ref = take(2)
    if far_h:
        h_rows, h_sem = take(2)
        for r in range(side):
            index, base = row_place(splits[0], r)
            pltpu.make_async_copy(h_refs[index].at[r - base], h_rows.at[r], h_sem.at[r]).start()
    ext = ext_ref[...]
    scale, _, rscale, offset, n = (params_ref[k : k + 1] for k in range(5))
    sums = one_ref[...] + other_ref[...]
    shift_ref[...] = sums[0:1]
    gain_ref[...] = sums[1:2]
    shift_grad, gain_grad = sums[0:1] / n, sums[1:2] / n
    b = scale * rscale * gain_grad
    c0 = scale * (shift_grad + offset * gain_grad)
    for start, stop, ((hi, hb), (zi, zb), (oi, ob)) in segments(*splits):

        @pl.loop(start, stop)
        def _(r, hi=hi, hb=hb, zi=zi, zb=zb, oi=oi, ob=ob):
            if far_h:
                pltpu.make_async_copy(h_refs[hi].at[r - hb], h_rows.at[r], h_sem.at[r]).wait()
            for c in range(side):
                part = slice(c * batch, (c + 1) * batch)
                m = mask_at(ext, r, c)
                h = h_rows[r, part] if far_h else h_refs[hi][r - hb, part]
                grad = scale * dz_refs[zi][r - zb, part] - (h * b + c0)
                out_refs[oi][r - ob, part] = (m * grad).astype(BF16)


def norm_back(ext, params, sums, hs, dzs, flow, far_h, side, batch):
    splits = ([h.shape[0] for h in hs], [z.shape[0] for z in dzs], list(flow))
    return call(
        "norm_back",
        functools.partial(norm_back_body, side, batch, far_h, splits),
        [((n, side * batch, LANES), BF16, "v") for n in flow] + [((1, LANES), F32, "v")] * 2,
        [(ext, "v"), (params, "v")] + [(x, "v") for x in sums] + [(x, "h" if far_h else "v") for x in hs] + [(x, "v") for x in dzs],
        [pltpu.VMEM((side, side * batch, LANES), F32), DMA((side,))] if far_h else [],
    )


def as_rows(values):
    row = lax.broadcasted_iota(jnp.int32, (8, LANES), 0)
    out = jnp.zeros((8, LANES), F32)
    for k, value in enumerate(values):
        out = jnp.where(row == k, value, out)
    return out


def merge(a, b):
    merged = merge_rows(*(a[k : k + 1] for k in range(3)), *(b[k : k + 1] for k in range(3)))
    return as_rows(list(merged) + [a[k : k + 1] for k in range(3, 6)])


def affine(a, gain, shift):
    center, n = a[0:1], a[2:3]
    rscale = lax.rsqrt(a[1:2] / n + EPSILON)
    scale = rscale * gain
    rows = [scale, shift - center * scale, rscale, -center * rscale, n]
    return as_rows(rows + [(a[3 + q : 4 + q] - center) * scale + shift for q in range(3)])


def swap(x, axis, size, k):
    return lax.ppermute(x, axis, [(i, i ^ k) for i in range(size)])


def after(x, *others):
    return lax.optimization_barrier((x,) + others)[0]


class Sum:
    def __init__(self, x, size, add=None):
        self.x, self.size, self.k = x, size, 1
        self.add = add or (lambda a, b: a + b)

    def step(self, start=(), end=()):
        if self.k < self.size:
            x = after(self.x, *start) if start else self.x
            other = swap(x, "dp", self.size, self.k)
            self.x = self.add(self.x, after(other, *end) if end else other)
            self.k *= 2
        return self.x

    def end(self):
        while self.k < self.size:
            self.step()
        return self.x

    def pair(self):
        while 2 * self.k < self.size:
            self.step()
        return self.x, swap(self.x, "dp", self.size, self.k)


class Scatter:
    def __init__(self, keep, sends, size, index):
        self.keep, self.sends, self.size, self.index = keep, sends, size, index
        self.k = None

    def step(self, start=(), end=()):
        if self.k is None:
            sends = self.sends
            if start:
                sends = lax.optimization_barrier(tuple(sends) + tuple(start))[: len(sends)]
            others = tuple(swap(x, "dp", self.size, d + 1) for d, x in enumerate(sends))
            if end:
                others = lax.optimization_barrier(others + tuple(end))[: len(sends)]
            for other in others:
                self.keep = self.keep + other.astype(F32)
            self.k = len(sends) + 1
        elif self.k < self.size:
            half = self.keep.shape[0] // 2
            low, high = self.keep[:half], self.keep[half:]
            upper = (self.index // self.k) % 2 == 1
            send = jnp.where(upper, low, high).astype(BF16)
            other = swap(after(send, *start) if start else send, "dp", self.size, self.k)
            self.keep = jnp.where(upper, high, low) + (after(other, *end) if end else other).astype(F32)
            self.k *= 2
        return self.keep

    def end(self):
        while self.k is None or self.k < self.size:
            self.step()
        return self.keep


class Gather:
    def __init__(self, part, size, ways, index, at_once):
        self.x, self.size, self.ways, self.index, self.at_once = part.astype(BF16), size, ways, index, at_once
        self.ks, k = [], size
        while k > ways:
            k //= 2
            self.ks.append(k)
        if at_once:
            self.ks.append(0)
        else:
            while k > 1:
                k //= 2
                self.ks.append(ways // (2 * k))

    def step(self, start=(), end=()):
        if not self.ks:
            return self.x
        x = after(self.x, *start) if start else self.x
        k = self.ks.pop(0)
        if k:
            other = swap(x, "dp", self.size, k)
            other = after(other, *end) if end else other
            upper = (self.index // k) % 2 == 1
            self.x = jnp.where(upper, jnp.concatenate([other, self.x]), jnp.concatenate([self.x, other]))
        else:
            others = tuple(swap(x, "dp", self.size, d) for d in range(1, self.ways))
            if end:
                others = lax.optimization_barrier(others + tuple(end))[: self.ways - 1]
            self.others = others
        return self.x

    def end(self, *late):
        while self.ks:
            self.step()
        if self.at_once:
            others = lax.optimization_barrier(self.others + late)[: self.ways - 1] if late else self.others
            mine = self.index % self.ways
            self.x = jnp.concatenate([lax.select_n(mine ^ j, self.x, *others) for j in range(self.ways)])
        return self.x.astype(F32)


class Blocks:
    def __init__(self, x, size, late=False):
        self.own, self.size = x, size
        self.far = swap(x, "chan", size, 2)
        self.near = None if late else swap(x, "chan", size, 1)

    def end(self, *others):
        if self.near is None:
            self.near = swap(after(self.own, *others), "chan", self.size, 1)
        far = after(self.far, *others) if others else self.far
        return [self.own, self.near, far, swap(far, "chan", self.size, 1)]


def sum_chan(x, size):
    k = 1
    while k < size:
        x = x + swap(x, "chan", size, k)
        k *= 2
    return x


def moment_step(weight, grad, moment, weight_norm, grad_norm):
    trust = TRUST_COEF * weight_norm / (grad_norm + DECAY * weight_norm)
    return MOMENTUM * moment + LEARN_RATE * trust * (grad + DECAY * weight)


def shards(
    dp, ch, images, groups, cotangent, weight_one, gain_one, shift_one, weight_two, gain_two, shift_two, moment_one, moment_two
):
    batch, side, _, width = images.shape
    pixels = side * batch
    images = jnp.transpose(images, (1, 2, 0, 3)).reshape(side, pixels, width)
    cotangent = jnp.transpose(cotangent, (1, 2, 0, 3)).reshape(side, pixels, LANES)
    chan, index = lax.axis_index("chan").astype(jnp.int32), lax.axis_index("dp").astype(jnp.int32)
    ways = min(4, dp)
    place = jnp.stack([chan, index % ways])
    ext = jnp.broadcast_to((5 + 2 * groups)[:, None], (batch, LANES))
    third = side // 3
    conv_in = (third + 1, third, side - 2 * third - 1)
    flow = (third, third, side - 2 * third)
    sizes = (side, batch)

    gains = [g.reshape(1, LANES) for g in (gain_one, shift_one, gain_two, shift_two)]

    low, h_one, owns, carry, stat, weights, r0 = [], [], [], None, None, weight_one, 0
    for q, count in enumerate(conv_in):
        out = conv_images(q, r0, count, *sizes, place, ext, weights, images, carry, stat)
        h, stat, chunk, own = out[:4]
        if q == 0:
            weights = out[4]
        carry = out[-1]
        h_one.append(h)
        owns.append(own)
        low.append(Blocks(chunk, ch))
        r0 += count
    wb_two, squares, *wt = prep(weight_one, weight_two, place)
    total = Sum(stat, dp, merge)
    total.step(start=(low[0].far,))
    total.step(start=(squares,))
    total.step(start=(low[1].far,))
    params_one = affine(total.end(), *gains[:2])
    params = Blocks(params_one, ch).end()

    h_two, act, carry, stat, r0 = [], [], None, None, 0
    for q, count in enumerate(flow):
        out = conv_active(q, r0, count, *sizes, place, ext, wb_two, low[q].end(), params, carry, stat)
        h, stat, rows = out[:3]
        if q == 0:
            wt_two = [after(w, stat) for w in wt[ch:]]
            wt_two = [wt_two[0]] + [swap(wt_two[k], "chan", ch, k) for k in range(1, ch)]
        h_two.append(h)
        act.append(rows)
        carry = out[-1]
        r0 += count
    params_two = affine(Sum(stat, dp, merge).end(), *gains[2:])

    out = block_end(ext, params_two, cotangent, h_two, owns, (side,), *sizes)
    block_output, grad_pre, sums = out
    sums_two = Sum(sums, dp).pair()
    *grad_two, gain_two_grad, shift_two_grad = norm_back(ext, params_two, (after(sums_two[0], *wt_two[1:]), sums_two[1]), h_two, [grad_pre], (side,), False, *sizes)
    gathered = Blocks(grad_two[0], ch, True)
    keep, *sends = weight_grad("act", place, ext, act, grad_two, ways, *sizes)
    scatter = Scatter(keep, sends, dp, index)
    scatter.step()
    sources = gathered.end(scatter.keep)
    wt_one = [after(w, scatter.keep) for w in wt[:ch]]
    wt_one = [wt_one[0]] + [swap(wt_one[k], "chan", ch, k) for k in range(1, ch)]
    dz_one, sums = conv_back("active", 0, side, *sizes, ext, wt_two, [sources], h_one, params_one, None, None)
    scatter.step(end=(sums,))
    part_two = scatter.end()
    gather_two = Gather(part_two, dp, ways, index, True)
    total = Sum(sums, dp)
    total.step(start=tuple(wt_one[2:]))
    gather_two.step()
    sums_one = total.pair()
    split = (third, side - third)
    *grad_one, gain_one_grad, shift_one_grad = norm_back(ext, params_one, (after(sums_one[0], gather_two.x, *wt_one[1:]), sums_one[1]), h_one, [dz_one], split, True, *sizes)
    gathered = [Blocks(g, ch, True) for g in grad_one]
    keep, *sends = weight_grad("images", place, ext, [images], grad_one, ways, *sizes)
    gather_two.step(start=(grad_one[0],), end=(keep,))
    scatter = Scatter(keep, sends, dp, index)
    scatter.step(start=(gathered[0].far,))
    sources = [g.end(scatter.keep) for g in gathered]
    weight_two_grad = gather_two.end().reshape(weight_two.shape)
    squares = jnp.sum(squares, axis=1)
    norms = jnp.sqrt(sum_chan(jnp.stack([squares[0], squares[1], jnp.sum(weight_two_grad * weight_two_grad)]), ch))
    part_one = scatter.end()
    gather_one = Gather(part_one, dp, ways, index, True)
    moment_two_new = moment_step(weight_two, weight_two_grad, moment_two, norms[1], norms[2])
    input_grad, carry = conv_back(
        "input", 0, split[0], *sizes, after(ext, part_one), wt_one, sources[:1], [grad_pre], None, None, None
    )
    gather_one.step(end=(moment_two_new, carry))
    input_grad = conv_back(
        "input", split[0], split[1], *sizes, after(ext, gather_one.x), wt_one, sources[1:], [grad_pre], None, carry, input_grad
    )[0]
    gather_one.step(end=(input_grad,))
    weight_one_grad = gather_one.end().reshape(weight_one.shape)
    norm_one = jnp.sqrt(sum_chan(jnp.sum(weight_one_grad * weight_one_grad).reshape(1), ch))
    weight_norms = norms[:2]
    grad_norms = jnp.concatenate([norm_one, norms[2:]])
    moment_one_new = moment_step(weight_one, weight_one_grad, moment_one, norms[0], norm_one[0])

    def as_images(x):
        return jnp.transpose(x.reshape(side, side, batch, LANES), (2, 0, 1, 3))

    return (
        as_images(block_output),
        as_images(input_grad),
        weight_one_grad,
        gain_one_grad.reshape(LANES),
        shift_one_grad.reshape(LANES),
        weight_two_grad,
        gain_two_grad.reshape(LANES),
        shift_two_grad.reshape(LANES),
        moment_one_new,
        moment_two_new,
        weight_norms,
        grad_norms,
    )


def solution(mesh):
    full, rows, both = P("dp", None, None, None), P("dp"), P("dp", None, None, "chan")
    weight, channel = P(None, None, "chan"), P("chan")
    return jax.shard_map(
        functools.partial(shards, mesh.shape["dp"], mesh.shape["chan"]),
        mesh=mesh,
        in_specs=(full, rows, both, weight, channel, channel, weight, channel, channel, weight, weight),
        out_specs=(both, both, weight, channel, channel, weight, channel, channel, weight, weight, P(), P()),
        check_vma=False,
    )
```
